32 devices in a mesh: seq: 16 (over z, y, x), head: 2 (over core), dp: 1.
Axes of the slice: x: 2, y: 2, z: 4, core: 2. Of those that a mesh axis runs over, the one named last changes fastest.
Arguments:
- queries: bfloat16 [4096, 2048], P(('dp', 'seq'), 'head'), may hold values from -32 to 32
- keys: bfloat16 [4096, 2048], P(('dp', 'seq'), 'head'), may hold values from -32 to 32
- values: bfloat16 [4096, 2048], P(('dp', 'seq'), 'head'), may hold values from -6 to 6
- out_grad: bfloat16 [4096, 4096], P(('dp', 'seq')), may hold values from -6 to 6
- proj_weight: bfloat16 [4096, 2048], P(None, 'head'), may hold values from -0.09375 to 0.09375
- layout: int32 [32, 10], replicated, may hold values from -1 to 31, as said below
Outputs:
- query_grad: bfloat16 [4096, 2048], P(('dp', 'seq'), 'head')
- key_grad: bfloat16 [4096, 2048], P(('dp', 'seq'), 'head')
- value_grad: bfloat16 [4096, 2048], P(('dp', 'seq'), 'head')
- proj_grad: float32 [4096, 2048], P(('dp', 'seq'), 'head')
The draws below stay inside these ranges and needn't reach their ends.
Inputs may be any that keep to these rules, and one draw needn't show every extreme that they name: `layout`: row i lists, in increasing order, some of the blocks j < i - 7 whose remainder modulo 16 equals one offset, below 8 and shared by all rows (the last row lists all of them), then the blocks max(0, i - w + 1) to i for a window w of its own between 1 and 8, and ends with -1 in the unused entries; a row whose block follows a block of that remainder has w = 8.
All inputs are finite; a program needn't handle non-finite values.
Results may differ from the reference program's by a relative error of at most 0.03.
Values may be sent and summed in bfloat16 or wider, within the bound.
No kernel may reach another device: no remote copies, remote signals or barrier semaphores. Data moves between devices by JAX's collectives and lax.ppermute only.
A program may use at most 192 MiB of HBM per device.

```python
import jax
import jax.numpy as jnp
from jax import lax

D = 4096
HEADS = 16
HD = 128
BLK = 128
LOCAL = 8
STRIDE = 16
NB = 32
TOKENS = 4096
HF = 2048
NSUM = 2
KMAX = 10


def draw_layout(key, part):
    offset_block = jax.random.randint(jax.random.fold_in(key, 21), (), 0, STRIDE - LOCAL, dtype=jnp.int32)
    row_ids = jnp.arange(NB, dtype=jnp.int32)[:, None]
    sum_ids = jnp.arange(NSUM, dtype=jnp.int32)[None, :]
    win_ids = jnp.arange(LOCAL, dtype=jnp.int32)[None, :]
    reach_row = row_ids - LOCAL - offset_block
    strided_count = jnp.where(reach_row >= 0, jnp.maximum(reach_row, 0) // STRIDE + 1, 0)
    keep_far = jax.random.randint(jax.random.fold_in(key, 22), (NB, NSUM), 0, 4, dtype=jnp.int32) > 0
    keep_far = keep_far | (row_ids == NB - 1)
    far_entry = offset_block + STRIDE * sum_ids
    far_valid = (sum_ids < strided_count) & keep_far
    window_len = jnp.minimum(jax.random.randint(jax.random.fold_in(key, 23), (NB, 1), LOCAL // 2, LOCAL + LOCAL // 2, dtype=jnp.int32), LOCAL)
    window_len = jnp.where(row_ids % STRIDE == offset_block + 1, LOCAL, window_len)
    near_entry = row_ids - LOCAL + 1 + win_ids
    near_valid = (win_ids >= LOCAL - window_len) & (near_entry >= 0)
    entries = jnp.concatenate([jnp.broadcast_to(far_entry, (NB, NSUM)), near_entry], axis=1)
    valid = jnp.concatenate([far_valid, near_valid], axis=1)
    col_ids = jnp.arange(KMAX, dtype=jnp.int32)[None, :]
    sort_key = jnp.where(valid, 0, KMAX) + col_ids
    order = jnp.argsort(sort_key, axis=1, stable=True).astype(jnp.int32)
    sorted_entries = jnp.take_along_axis(entries, order, axis=1)
    sorted_valid = jnp.take_along_axis(valid, order, axis=1)
    table = jnp.where(sorted_valid, sorted_entries, -1)
    return table.astype(jnp.int32)


def draw_queries(key, part):
    drawn_rows = jax.random.normal(jax.random.fold_in(key, 1), (TOKENS, HF), jnp.float32)
    return jnp.clip(drawn_rows, -32.0, 32.0).astype(jnp.bfloat16)


def draw_keys(key, part):
    drawn_rows = jax.random.normal(jax.random.fold_in(key, 3), (TOKENS, HF), jnp.float32)
    return jnp.clip(drawn_rows, -32.0, 32.0).astype(jnp.bfloat16)


def strengthened(drawn, rng, source, target, shards_of, factor):
    owner, partner = [(jnp.arange(drawn.shape[position]) // (drawn.shape[position] // shards_of)).reshape([-1 if axis == position else 1 for axis in range(drawn.ndim)]) for position in (source, target)]
    chosen = jax.random.permutation(rng, shards_of)[partner]
    strong = (owner == chosen) | (owner == (partner + shards_of // 2) % shards_of)
    return jnp.where(strong, factor * drawn, drawn)


def shard_levels(own_key, shape, split, least, high):
    loudness = 1.0
    for axis_at, parts in split:
        draws = jax.random.uniform(jax.random.fold_in(jax.random.fold_in(own_key, 6), axis_at), (parts,), jnp.float32, least / len(split), high / len(split))
        loudness = loudness * jnp.repeat(jnp.exp(draws), shape[axis_at] // parts).reshape((-1,) + (1,) * (len(shape) - 1 - axis_at))
    return loudness


def normal_values(stream_key, extent, deviation, limit, shards=(), kind=jnp.bfloat16):
    values = jax.random.normal(stream_key, extent, jnp.float32) * deviation
    if len(shards) > 0:
        values = shard_levels(stream_key, extent, shards, -0.22, 0.18) * values
    return jnp.clip(values, min=-limit, max=limit).astype(kind)


def bell_draw_with(rng, shape, spread, bound, cuts, heavy, kind=jnp.bfloat16):
    values = spread * jax.random.normal(rng, shape, jnp.float32)
    if cuts:
        values = values * shard_levels(rng, shape, cuts, -0.22, 0.18)
    return jnp.clip(strengthened(values, jax.random.fold_in(rng, 3), *heavy), -bound, bound).astype(kind)


def setup_inputs(seed: int = 0, part: int = 0) -> dict:
    splits = jax.random.split(jax.random.key(seed), 7)
    own_keys = jax.random.split(jax.random.fold_in(splits[6], part), 7)
    return {
        "queries": draw_queries(jax.random.fold_in(jax.random.fold_in(splits[6], part), 71), part),
        "keys": draw_keys(jax.random.fold_in(jax.random.fold_in(splits[6], part), 71), part),
        "values": normal_values(own_keys[2], (TOKENS, HF), 1.0, 6.0, ((0, 16), (1, 2))),
        "out_grad": bell_draw_with(own_keys[3], (TOKENS, D), 1.0, 6.0, ((0, 16),), (0, 1, 16, 2.0)),
        "proj_weight": normal_values(splits[4], (D, HF), D ** -0.5, 0.09375, ((1, 2),)),
        "layout": draw_layout(jax.random.fold_in(splits[6], 71), part),
    }


def reference(queries, keys, values, out_grad, proj_weight, layout):
    score_scale = HD ** -0.5
    block_count = TOKENS // BLK
    table_width = layout.shape[1]
    attn_grad = jnp.dot(out_grad, proj_weight, preferred_element_type=jnp.float32).astype(jnp.bfloat16)
    query_blocks = queries.reshape(block_count, BLK, HEADS, HD)
    key_blocks = keys.reshape(block_count, BLK, HEADS, HD)
    value_blocks = values.reshape(block_count, BLK, HEADS, HD)
    grad_blocks = attn_grad.reshape(block_count, BLK, HEADS, HD)
    offsets = jnp.arange(BLK, dtype=jnp.int32)

    def block_step(totals, block_index):
        key_total, value_total = totals
        table_row = layout[block_index]
        safe_row = jnp.maximum(table_row, 0).astype(jnp.int32)
        query_rows = query_blocks[block_index].astype(jnp.float32)
        grad_rows = grad_blocks[block_index].astype(jnp.float32)
        key_rows = key_blocks[safe_row].astype(jnp.float32).reshape(table_width * BLK, HEADS, HD)
        value_rows = value_blocks[safe_row].astype(jnp.float32).reshape(table_width * BLK, HEADS, HD)
        query_pos = block_index * BLK + offsets
        key_pos = (safe_row[:, None] * BLK + offsets[None, :]).reshape(-1)
        listed_cols = jnp.repeat(table_row >= 0, BLK)
        allowed = listed_cols[None, :] & (key_pos[None, :] <= query_pos[:, None])
        scores = jnp.einsum("ahd,chd->hac", query_rows, key_rows) * score_scale
        scores = jnp.where(allowed[None], scores, -jnp.inf)
        row_top = jnp.max(scores, axis=-1, keepdims=True)
        log_total = row_top + jnp.log(jnp.sum(jnp.exp(scores - row_top), axis=-1, keepdims=True))
        weights = jnp.exp(scores - log_total)
        weights_low = lax.optimization_barrier(weights.astype(jnp.bfloat16)).astype(jnp.float32)
        out_rows = jnp.einsum("hac,chd->ahd", weights_low, value_rows).astype(jnp.bfloat16)
        out_back = lax.optimization_barrier(out_rows).astype(jnp.float32)
        delta_rows = jnp.transpose(jnp.sum(out_back * grad_rows, axis=-1))[:, :, None]
        grad_weights = jnp.einsum("ahd,chd->hac", grad_rows, value_rows)
        dscore = lax.optimization_barrier((score_scale * weights * (grad_weights - delta_rows)).astype(jnp.bfloat16)).astype(jnp.float32)
        query_part = jnp.einsum("hac,chd->ahd", dscore, key_rows).astype(jnp.bfloat16)
        key_part = jnp.einsum("hac,ahd->chd", dscore, query_rows).reshape(table_width, BLK, HEADS, HD)
        value_part = jnp.einsum("hac,ahd->chd", weights_low, grad_rows).reshape(table_width, BLK, HEADS, HD)
        key_total = key_total.at[safe_row].add(key_part)
        value_total = value_total.at[safe_row].add(value_part)
        return (key_total, value_total), (out_rows, query_part)

    zeros_grad = jnp.zeros((block_count, BLK, HEADS, HD), jnp.float32)
    totals, outputs = lax.scan(block_step, (zeros_grad, zeros_grad), jnp.arange(block_count, dtype=jnp.int32))
    out_blocks, query_parts = outputs
    attn_out = out_blocks.reshape(TOKENS, HEADS * HD)
    proj_grad = jnp.dot(out_grad.T, attn_out, preferred_element_type=jnp.float32)
    query_grad = query_parts.reshape(TOKENS, HEADS * HD)
    key_grad = totals[0].reshape(TOKENS, HEADS * HD).astype(jnp.bfloat16)
    value_grad = totals[1].reshape(TOKENS, HEADS * HD).astype(jnp.bfloat16)
    return (query_grad, key_grad, value_grad, proj_grad)
```

```python
import functools

import jax
import jax.numpy as jnp
from jax import lax
from jax.experimental import pallas as pl
from jax.experimental.pallas import tpu as pltpu
from jax.sharding import PartitionSpec as P

HD = 128
BLK = 128
LOCAL = 8
STRIDE = 16
PAIR = 2 * BLK
SPAN = LOCAL + 1
SCALE = HD ** (-0.5)
VMEM_LIMIT = 48 * 1024 * 1024

NT = (((1,), (1,)), ((), ()))
NN = (((1,), (0,)), ((), ()))
TN = (((0,), (0,)), ((), ()))
SMEM = pl.BlockSpec(memory_space=pltpu.SMEM)
VMEM = pl.BlockSpec(memory_space=pltpu.VMEM)


def shape(dims, dtype=jnp.bfloat16):
    return jax.ShapeDtypeStruct(dims, dtype)


def dot(a, b, dims):
    return lax.dot_general(a, b, dims, preferred_element_type=jnp.float32)


def params():
    return pltpu.CompilerParams(vmem_limit_bytes=VMEM_LIMIT)


def cost(flops, size, exps=0):
    return pl.CostEstimate(flops=flops, bytes_accessed=size, transcendentals=exps)


def call(body, scalars, arrays, outs, scratch, estimate, name):
    return pl.pallas_call(
        body,
        out_shape=outs,
        in_specs=[SMEM] * len(scalars) + [VMEM] * len(arrays),
        out_specs=[VMEM] * len(outs),
        scratch_shapes=scratch,
        compiler_params=params(),
        cost_estimate=estimate,
        name=name,
    )(*scalars, *arrays)


def pack_kv(keys, values, meta, group, width):
    rows = keys.shape[0]

    def body(meta_ref, k_ref, v_ref, *outs):
        me = meta_ref[0]
        for k in range(group):
            at = pl.multiple_of((me ^ k) * width, width)
            outs[k][0] = k_ref[:, pl.ds(at, width)]
            outs[k][1] = v_ref[:, pl.ds(at, width)]

    return call(
        body, (meta,), (keys, values), [shape((2, rows, width))] * group, [],
        cost(0, 4 * keys.size * 2), "pack_kv",
    )


def grads_packed(queries, out_grad, proj_weight, meta, group, width):
    rows, depth = out_grad.shape

    def body(meta_ref, q_ref, og_ref, w_ref, *outs):
        step = pl.program_id(0)
        got = dot(og_ref[...], w_ref[...], NN).astype(jnp.bfloat16)
        for k in range(group):

            @pl.when(step == k)
            def _():
                outs[k][0] = q_ref[...]
                outs[k][1] = got

    return pl.pallas_call(
        body,
        out_shape=[shape((2, rows, width))] * group,
        grid_spec=pltpu.PrefetchScalarGridSpec(
            num_scalar_prefetch=1,
            grid=(group,),
            in_specs=[
                pl.BlockSpec((rows, width), lambda i, m: (0, m[0] ^ i)),
                pl.BlockSpec((rows, depth), lambda i, m: (0, 0)),
                pl.BlockSpec((depth, width), lambda i, m: (0, m[0] ^ i)),
            ],
            out_specs=[pl.BlockSpec((2, rows, width), lambda i, m: (0, 0, 0))] * group,
        ),
        compiler_params=params(),
        cost_estimate=cost(2 * rows * depth * width * group, 12 * 1024 * 1024),
        name="attn_grad",
    )(meta, queries, out_grad, proj_weight)


def pack_out_grad(out_grad, meta, group, parts):
    rows, depth = out_grad.shape
    each = depth // (group * parts)

    def body(meta_ref, og_ref, *outs):
        me = meta_ref[0]
        for k in range(group):
            for part in range(parts):
                at = pl.multiple_of((part * group + (me ^ k)) * each, each)
                outs[k][part * each : (part + 1) * each, :] = og_ref[:, pl.ds(at, each)].T

    return call(
        body, (meta,), (out_grad,), [shape((parts * each, rows))] * group, [],
        cost(0, 4 * out_grad.size), "pack_out_grad",
    )


def pick_summary(pieces, meta, group):
    rows, width = pieces[0].shape[1:]

    def body(meta_ref, *refs):
        me, at = meta_ref[0], meta_ref[2] * BLK
        out = refs[group]
        for k in range(group):

            @pl.when(at // rows == (me ^ k))
            def _():
                start = pl.multiple_of(at % rows, BLK)
                out[...] = refs[k][:, pl.ds(start, BLK), :]

    return call(
        body, (meta,), tuple(pieces), [shape((2, BLK, width))], [],
        cost(0, 2 * 1024 * 1024), "pick_summary",
    )[0]


def fill_pools(meta_ref, own, prev, far, k_pool, v_pool, group, rows, slots):
    me, at_group, offset = meta_ref[0], meta_ref[1], meta_ref[2]
    whole = group * rows
    for k in range(group):
        at = pl.multiple_of((me ^ k) * rows, rows)
        k_pool[pl.ds(at, rows), :] = prev[k][0]
        v_pool[pl.ds(at, rows), :] = prev[k][1]
        k_pool[pl.ds(whole + at, rows), :] = own[k][0]
        v_pool[pl.ds(whole + at, rows), :] = own[k][1]
    tail = jnp.zeros((slots * BLK, k_pool.shape[1]), k_pool.dtype)
    k_pool[2 * whole :, :] = tail
    v_pool[2 * whole :, :] = tail

    @pl.when(at_group % 2 == 1)
    def _():
        to = pl.multiple_of(2 * whole + (at_group // 2) * BLK, BLK)
        start = pl.multiple_of(offset * BLK, BLK)
        k_pool[pl.ds(to, BLK), :] = k_pool[pl.ds(start, BLK), :]
        v_pool[pl.ds(to, BLK), :] = v_pool[pl.ds(start, BLK), :]

    for index, ref in enumerate(far):
        distance = index + 2

        @pl.when((at_group >= distance) & ((at_group - distance) % 2 == 0))
        def _():
            to = pl.multiple_of(2 * whole + ((at_group - distance) // 2) * BLK, BLK)
            k_pool[pl.ds(to, BLK), :] = ref[0]
            v_pool[pl.ds(to, BLK), :] = ref[1]


def causal_masks():
    key_at = lax.broadcasted_iota(jnp.int32, (BLK, PAIR), 0)
    query_at = lax.broadcasted_iota(jnp.int32, (BLK, PAIR), 1)
    first = (key_at <= query_at) | (query_at >= BLK)
    second = key_at <= query_at - BLK
    return first, second


def masked_scores(keys, query, bias, masks):
    raw = dot(keys, query, NT) * SCALE
    tiles = []
    for j in range(keys.shape[0] // BLK):
        tile = raw[j * BLK : (j + 1) * BLK] + bias[j : j + 1]
        if j in (LOCAL - 1, LOCAL):
            tile = jnp.where(masks[j - LOCAL + 1], tile, -jnp.inf)
        tiles.append(tile)
    return jnp.concatenate(tiles, axis=0)


def forward(qd, own, prev, far, bias, meta, group, slots):
    rows, width = qd[0].shape[1:]
    heads = width // HD
    whole = group * rows
    pairs = whole // PAIR
    counts = (group, group, group, len(far))

    def body(meta_ref, bias_ref, *refs):
        refs = list(refs)
        taken = []
        for count in counts:
            taken.append(refs[:count])
            refs = refs[count:]
        qd_refs, own_refs, prev_refs, far_refs = taken
        out_ref, lse_ref, k_pool, v_pool, q_pool = refs
        me = meta_ref[0]
        fill_pools(meta_ref, own_refs, prev_refs, far_refs, k_pool, v_pool, group, rows, slots)
        for k in range(group):
            at = pl.multiple_of((me ^ k) * rows, rows)
            q_pool[pl.ds(at, rows), :] = qd_refs[k][0]
        masks = causal_masks()

        def step(t, carry):
            at = pl.multiple_of(t * PAIR, PAIR)
            window = pl.ds(pl.multiple_of(t * PAIR + BLK, BLK), SPAN * BLK)
            bias_here = bias_ref[t]
            for h in range(heads):
                lanes = slice(h * HD, (h + 1) * HD)
                keys = jnp.concatenate([k_pool[window, lanes], k_pool[2 * whole :, lanes]], axis=0)
                vals = jnp.concatenate([v_pool[window, lanes], v_pool[2 * whole :, lanes]], axis=0)
                s = masked_scores(keys, q_pool[pl.ds(at, PAIR), lanes], bias_here, masks)
                top = jnp.max(s, axis=0, keepdims=True)
                e = jnp.exp(s - top)
                total = jnp.sum(e, axis=0, keepdims=True)
                low = (e * (1.0 / total)).astype(jnp.bfloat16)
                out_ref[pl.ds(at, PAIR), lanes] = dot(low, vals, TN).astype(jnp.bfloat16)
                lse_ref[t, h : h + 1, :] = top + jnp.log(total)
            return carry

        lax.fori_loop(0, pairs, step, 0)

    span = (SPAN + slots) * BLK
    return call(
        body, (meta,), (bias, *qd, *own, *prev, *far),
        [shape((whole, width)), shape((pairs, heads, PAIR), jnp.float32)],
        [
            pltpu.VMEM((2 * whole + slots * BLK, width), jnp.bfloat16),
            pltpu.VMEM((2 * whole + slots * BLK, width), jnp.bfloat16),
            pltpu.VMEM((whole, width), jnp.bfloat16),
        ],
        cost(4 * whole * span * width * 2, 5 * 1024 * 1024, whole * span * heads),
        "attention",
    )


def backward(qd, own, prev, far, attn, lse, bias, meta, group, slots):
    rows, width = qd[0].shape[1:]
    heads = width // HD
    whole = group * rows
    pairs = whole // PAIR
    counts = (group, group, group, len(far))
    out_counts = (group, 1, 1, len(far))
    everything = 2 * whole + slots * BLK

    def body(meta_ref, bias_ref, attn_ref, lse_ref, *refs):
        refs = list(refs)
        taken = []
        for count in counts + out_counts:
            taken.append(refs[:count])
            refs = refs[count:]
        qd_refs, own_refs, prev_refs, far_refs, dq_refs, own_out, prev_out, far_outs = taken
        own_out, prev_out = own_out[0], prev_out[0]
        k_pool, v_pool, q_pool, g_pool, dk, dv, dq = refs
        me, at_group, offset = meta_ref[0], meta_ref[1], meta_ref[2]
        fill_pools(meta_ref, own_refs, prev_refs, far_refs, k_pool, v_pool, group, rows, slots)
        for k in range(group):
            at = pl.multiple_of((me ^ k) * rows, rows)
            q_pool[pl.ds(at, rows), :] = qd_refs[k][0]
            g_pool[pl.ds(at, rows), :] = qd_refs[k][1]
        dk[...] = jnp.zeros_like(dk)
        dv[...] = jnp.zeros_like(dv)
        masks = causal_masks()

        def step(t, carry):
            at = pl.multiple_of(t * PAIR, PAIR)
            here = pl.ds(at, PAIR)
            window = pl.ds(pl.multiple_of(t * PAIR + BLK, BLK), SPAN * BLK)
            bias_here = bias_ref[t]
            for h in range(heads):
                lanes = slice(h * HD, (h + 1) * HD)
                keys = jnp.concatenate([k_pool[window, lanes], k_pool[2 * whole :, lanes]], axis=0)
                vals = jnp.concatenate([v_pool[window, lanes], v_pool[2 * whole :, lanes]], axis=0)
                query, grad = q_pool[here, lanes], g_pool[here, lanes]
                s = masked_scores(keys, query, bias_here, masks)
                probs = jnp.exp(s - lse_ref[t, h : h + 1, :])
                product = attn_ref[here, lanes].astype(jnp.float32) * grad.astype(jnp.float32)
                delta = jnp.sum(product.T, axis=0, keepdims=True)
                dprobs = dot(vals, grad, NT)
                ds = (SCALE * probs * (dprobs - delta)).astype(jnp.bfloat16)
                low = probs.astype(jnp.bfloat16)
                dq[here, lanes] = dot(ds, keys, TN).astype(jnp.bfloat16)
                dk_here = dot(ds, query, NN)
                dv_here = dot(low, grad, NN)
                dk[window, lanes] += dk_here[: SPAN * BLK]
                dv[window, lanes] += dv_here[: SPAN * BLK]
                dk[2 * whole :, lanes] += dk_here[SPAN * BLK :]
                dv[2 * whole :, lanes] += dv_here[SPAN * BLK :]
            return carry

        lax.fori_loop(0, pairs, step, 0)

        @pl.when(at_group % 2 == 1)
        def _():
            start = pl.multiple_of(2 * whole + (at_group // 2) * BLK, BLK)
            to = pl.multiple_of(offset * BLK, BLK)
            dk[pl.ds(to, BLK), :] += dk[pl.ds(start, BLK), :]
            dv[pl.ds(to, BLK), :] += dv[pl.ds(start, BLK), :]

        prev_out[0] = dk[:whole, :].astype(jnp.bfloat16)
        prev_out[1] = dv[:whole, :].astype(jnp.bfloat16)
        own_out[0] = dk[whole : 2 * whole, :]
        own_out[1] = dv[whole : 2 * whole, :]
        for k in range(group):
            at = pl.multiple_of((me ^ k) * rows, rows)
            dq_refs[k][...] = dq[pl.ds(at, rows), :]
        for index, ref in enumerate(far_outs):
            slot = jnp.maximum(at_group - index - 2, 0) // 2
            start = pl.multiple_of(2 * whole + slot * BLK, BLK)
            ref[0] = dk[pl.ds(start, BLK), :].astype(jnp.bfloat16)
            ref[1] = dv[pl.ds(start, BLK), :].astype(jnp.bfloat16)

    span = (SPAN + slots) * BLK
    outs = call(
        body, (meta,), (bias, attn, lse, *qd, *own, *prev, *far),
        [shape((rows, width))] * group
        + [shape((2, whole, width), jnp.float32), shape((2, whole, width))]
        + [shape((2, BLK, width))] * len(far),
        [
            pltpu.VMEM((everything, width), jnp.bfloat16),
            pltpu.VMEM((everything, width), jnp.bfloat16),
            pltpu.VMEM((whole, width), jnp.bfloat16),
            pltpu.VMEM((whole, width), jnp.bfloat16),
            pltpu.VMEM((everything, width), jnp.float32),
            pltpu.VMEM((everything, width), jnp.float32),
            pltpu.VMEM((whole, width), jnp.bfloat16),
        ],
        cost(10 * whole * span * width * 2, 9 * 1024 * 1024, whole * span * heads),
        "attention_back",
    )
    return outs[:group], outs[group], outs[group + 1], outs[group + 2 :]


def combine(own, returned, far, meta, group, rows):
    whole, width = own.shape[1:]

    def body(meta_ref, own_ref, ret_ref, *refs):
        far_refs, outs, acc = refs[: len(far)], refs[len(far) : -1], refs[-1]
        me, offset = meta_ref[0], meta_ref[2]
        acc[...] = own_ref[...] + ret_ref[...].astype(jnp.float32)
        at = pl.multiple_of(offset * BLK, BLK)
        for ref in far_refs:
            acc[:, pl.ds(at, BLK), :] += ref[...].astype(jnp.float32)
        for k in range(group):
            at = pl.multiple_of((me ^ k) * rows, rows)
            outs[k][...] = acc[:, pl.ds(at, rows), :].astype(jnp.bfloat16)

    return call(
        body, (meta,), (own, returned, *far), [shape((2, rows, width))] * group,
        [pltpu.VMEM((2, whole, width), jnp.float32)],
        cost(0, 4 * 1024 * 1024), "combine",
    )


def project(og, attn, meta, group, parts):
    each, rows = og[0].shape[0] // parts, og[0].shape[1]
    whole, width = attn[0].shape

    def body(meta_ref, *refs):
        og_refs, attn_refs = refs[:group], refs[group : 2 * group]
        outs, cotangent, total = refs[2 * group : -2], refs[-2], refs[-1]
        me, at_group = meta_ref[0], meta_ref[1]
        for k in range(group):
            at = pl.multiple_of((me ^ k) * rows, rows)
            cotangent[:, pl.ds(at, rows)] = og_refs[k][...]
        for k in range(group):
            at = pl.multiple_of((me ^ k) * width, width)
            total[:, pl.ds(at, width)] = dot(cotangent[...], attn_refs[k][...], NN)
        for part in range(parts):
            at = pl.multiple_of(lax.rem(at_group + part, parts) * each, each)
            outs[part][...] = total[pl.ds(at, each), :].astype(outs[part].dtype)

    full = group * width
    return call(
        body, (meta,), (*og, *attn),
        [shape((each, full), jnp.float32)] + [shape((each, full))] * (parts - 1),
        [
            pltpu.VMEM((parts * each, whole), jnp.bfloat16),
            pltpu.VMEM((parts * each, full), jnp.float32),
        ],
        cost(2 * parts * each * whole * full, 8 * 1024 * 1024), "project",
    )


def unpack(dq, dkv, meta, group):
    rows, width = dq[0].shape

    def body(meta_ref, *refs):
        q_out, k_out, v_out = refs[2 * group :]
        me = meta_ref[0]
        for k in range(group):
            at = pl.ds(pl.multiple_of((me ^ k) * width, width), width)
            q_out[:, at] = refs[k][...]
            k_out[:, at] = refs[group + k][0]
            v_out[:, at] = refs[group + k][1]

    return call(
        body, (meta,), (*dq, *dkv), [shape((rows, group * width))] * 3, [],
        cost(0, 3 * 1024 * 1024), "unpack",
    )


def listed(table, ids):
    return jnp.any(table[:, None, :] == ids[:, :, None], axis=2) & (ids >= 0)


def local(devices, queries, keys, values, out_grad, proj_weight, layout):
    rows, columns = queries.shape
    group = LOCAL * BLK // rows
    parts = devices // group
    width = columns // group
    blocks = layout.shape[0]
    slots = blocks // STRIDE
    position = lax.axis_index("seq")
    me, at_group = position % group, position // group
    offset = layout[blocks - 1, 0] % STRIDE
    meta = jnp.stack([me, at_group, offset]).astype(jnp.int32)

    def swap(piece, k):
        route = [(i, (i // group) * group + ((i % group) ^ k)) for i in range(devices)]
        return lax.ppermute(piece, "seq", route)

    def shifted(piece, distance):
        route = [
            (i, i + distance * group)
            for i in range(devices)
            if 0 <= i + distance * group < devices
        ]
        return lax.ppermute(piece, "seq", route)

    def around(piece, distance):
        return lax.ppermute(
            piece, "seq", [(i, (i + distance * group) % devices) for i in range(devices)]
        )

    def summary_route(distance, back):
        route = [
            (i, i + distance * group)
            for i in range(devices - distance * group)
            if (i // group) % 2 == 0
        ]
        return [(b, a) for a, b in route] if back else route

    def exchange(pieces):
        return [pieces[0]] + [swap(pieces[k], k) for k in range(1, group)]

    ids = at_group * LOCAL + jnp.arange(LOCAL, dtype=jnp.int32)
    table = lax.dynamic_slice_in_dim(layout, at_group * LOCAL, LOCAL, 0)
    base = ids - jnp.arange(LOCAL, dtype=jnp.int32) % 2 - (LOCAL - 1)
    near_ids = base[:, None] + jnp.arange(SPAN, dtype=jnp.int32)[None, :]
    near = listed(table, near_ids) & (near_ids >= ids[:, None] - (LOCAL - 1))
    far_ids = jnp.broadcast_to(
        jnp.arange(slots, dtype=jnp.int32)[None, :] * STRIDE + offset, (LOCAL, slots)
    )
    distant = listed(table, far_ids) & (far_ids < ids[:, None] - (LOCAL - 1))
    reads = jnp.concatenate([near, distant], axis=1)
    bias = jnp.where(reads, 0.0, -jnp.inf).astype(jnp.float32)
    bias = bias.reshape(LOCAL // 2, 2, SPAN + slots).transpose(0, 2, 1)
    bias = jnp.repeat(bias, BLK, axis=2)

    kv = pack_kv(keys, values, meta, group, width)
    own_kv = exchange(kv)
    prev_kv = [shifted(kv[0], 1)]
    qd = exchange(grads_packed(queries, out_grad, proj_weight, meta, group, width))
    prev_kv += [shifted(own_kv[k], 1) for k in range(1, group)]
    strided = pick_summary(own_kv, meta, group)
    far = [
        lax.ppermute(strided, "seq", summary_route(distance, False))
        for distance in range(2, parts)
    ]
    og = exchange(pack_out_grad(out_grad, meta, group, parts))

    attn, lse = forward(qd, own_kv, prev_kv, far, bias, meta, group, slots)
    attn_pieces = [attn] + [swap(attn, k) for k in range(1, group)]
    dq, own_grad, prev_grad, far_grad = backward(
        qd, own_kv, prev_kv, far, attn, lse, bias, meta, group, slots
    )
    returned = shifted(prev_grad, -1)
    far_back = [
        lax.ppermute(piece, "seq", summary_route(index + 2, True))
        for index, piece in enumerate(far_grad)
    ]
    dq = exchange(dq)
    partial = project(og, attn_pieces, meta, group, parts)
    arrived = [around(partial[d], d) for d in range(1, parts)]
    dkv = exchange(combine(own_grad, returned, far_back, meta, group, rows))
    query_grad, key_grad, value_grad = unpack(dq, dkv, meta, group)
    proj_grad = partial[0]
    for piece in arrived:
        proj_grad = proj_grad + piece.astype(jnp.float32)
    return (query_grad, key_grad, value_grad, proj_grad)


def solution(mesh):
    split = P(("dp", "seq"), "head")
    return jax.shard_map(
        functools.partial(local, mesh.shape["seq"]),
        mesh=mesh,
        in_specs=(split, split, split, P(("dp", "seq"), None), P(None, "head"), P()),
        out_specs=(split, split, split, split),
        check_vma=False,
    )
```

```python
import functools
import math

import jax
import jax.numpy as jnp
from jax import lax
from jax.experimental import pallas as pl
from jax.experimental.pallas import tpu as pltpu
from jax.sharding import PartitionSpec as P

HD = 128
BLK = 128
LOCAL = 8
STRIDE = 16
PAIR = 2 * BLK
SPAN = LOCAL + 1
SCALE = HD ** (-0.5)
SCALE2 = SCALE * math.log2(math.e)
VMEM_LIMIT = 48 * 1024 * 1024

NT = (((1,), (1,)), ((), ()))
NN = (((1,), (0,)), ((), ()))
TN = (((0,), (0,)), ((), ()))
SMEM = pl.BlockSpec(memory_space=pltpu.SMEM)
VMEM = pl.BlockSpec(memory_space=pltpu.VMEM)


def shape(dims, dtype=jnp.bfloat16):
    return jax.ShapeDtypeStruct(dims, dtype)


def dot(a, b, dims):
    return lax.dot_general(a, b, dims, preferred_element_type=jnp.float32)


def params():
    return pltpu.CompilerParams(vmem_limit_bytes=VMEM_LIMIT)


def cost(flops, size, exps=0):
    return pl.CostEstimate(flops=flops, bytes_accessed=size, transcendentals=exps)


def call(body, scalars, arrays, outs, scratch, estimate, name, lanes=None):
    specs = [SMEM] * len(scalars)
    for index, array in enumerate(arrays):
        block = None if lanes is None else lanes[index]
        if block is None:
            specs.append(pl.BlockSpec(array.shape, functools.partial(corner, array.ndim, 0)))
        else:
            specs.append(
                pl.BlockSpec(array.shape[:-1] + (HD,), functools.partial(corner, array.ndim, block))
            )
    return pl.pallas_call(
        body,
        grid=(1,),
        out_shape=outs,
        in_specs=specs,
        out_specs=[pl.BlockSpec(o.shape, functools.partial(corner, len(o.shape), 0)) for o in outs],
        scratch_shapes=scratch,
        compiler_params=params(),
        cost_estimate=estimate,
        name=name,
    )(*scalars, *arrays)


def corner(ndim, last, step):
    return (0,) * (ndim - 1) + (last,)


def split_refs(refs, counts):
    refs, taken = list(refs), []
    for count in counts:
        taken.append(refs[:count])
        refs = refs[count:]
    return taken, refs


def pack_kv(keys, values, meta, group, width):
    rows = keys.shape[0]

    def body(meta_ref, k_ref, v_ref, *outs):
        me = meta_ref[0]
        for k in range(group):
            at = pl.multiple_of((me ^ k) * width, width)
            outs[k][0] = k_ref[:, pl.ds(at, width)]
            outs[k][1] = v_ref[:, pl.ds(at, width)]

    return call(
        body, (meta,), (keys, values), [shape((2, rows, width))] * group, [],
        cost(0, 4 * keys.size * 2), "pack_kv",
    )


def grads_packed(queries, out_grad, proj_weight, meta, group, width):
    rows, depth = out_grad.shape

    def body(meta_ref, q_ref, og_ref, w_ref, *outs):
        step = pl.program_id(0)
        got = dot(og_ref[...], w_ref[...], NN).astype(jnp.bfloat16)
        for k in range(group):

            @pl.when(step == k)
            def _():
                outs[k][0] = q_ref[...]
                outs[k][1] = got

    return pl.pallas_call(
        body,
        out_shape=[shape((2, rows, width))] * group,
        grid_spec=pltpu.PrefetchScalarGridSpec(
            num_scalar_prefetch=1,
            grid=(group,),
            in_specs=[
                pl.BlockSpec((rows, width), lambda i, m: (0, m[0] ^ i)),
                pl.BlockSpec((rows, depth), lambda i, m: (0, 0)),
                pl.BlockSpec((depth, width), lambda i, m: (0, m[0] ^ i)),
            ],
            out_specs=[pl.BlockSpec((2, rows, width), lambda i, m: (0, 0, 0))] * group,
        ),
        compiler_params=params(),
        cost_estimate=cost(2 * rows * depth * width * group, 12 * 1024 * 1024),
        name="attn_grad",
    )(meta, queries, out_grad, proj_weight)


def pack_out_grad(out_grad, meta, group, parts):
    rows, depth = out_grad.shape
    each = depth // (group * parts)
    half = parts // 2

    def body(meta_ref, og_ref, *outs):
        me, core = meta_ref[0], meta_ref[3]
        for k in range(group):
            for part in range(half):
                at = ((core * half + part) * group + (me ^ k)) * each
                at = pl.multiple_of(at, each)
                outs[k][part * each : (part + 1) * each, :] = og_ref[:, pl.ds(at, each)].T

    return call(
        body, (meta,), (out_grad,), [shape((half * each, rows))] * group, [],
        cost(0, 3 * out_grad.size), "pack_out_grad",
    )


def join_columns(pieces, meta, group):
    height, rows = pieces[0].shape

    def body(meta_ref, *refs):
        me = meta_ref[0]
        for k in range(group):
            at = pl.multiple_of((me ^ k) * rows, rows)
            refs[group][:, pl.ds(at, rows)] = refs[k][...]

    return call(
        body, (meta,), tuple(pieces), [shape((height, group * rows))], [],
        cost(0, 2 * 1024 * 1024), "join_columns",
    )[0]


def pick_summary(pieces, meta, group):
    rows, width = pieces[0].shape[1:]

    def body(meta_ref, *refs):
        me, at = meta_ref[0], meta_ref[2] * BLK
        out = refs[group]
        for k in range(group):

            @pl.when(at // rows == (me ^ k))
            def _():
                start = pl.multiple_of(at % rows, BLK)
                out[...] = refs[k][:, pl.ds(start, BLK), :]

    return call(
        body, (meta,), tuple(pieces), [shape((2, BLK, width))], [],
        cost(0, 2 * 1024 * 1024), "pick_summary",
    )[0]


def fill_pools(meta_ref, own, prev, far, k_pool, v_pool, group, rows, slots):
    me, at_group, offset = meta_ref[0], meta_ref[1], meta_ref[2]
    whole = group * rows
    for k in range(group):
        at = pl.multiple_of((me ^ k) * rows, rows)
        k_pool[pl.ds(at, rows), :] = prev[k][0]
        v_pool[pl.ds(at, rows), :] = prev[k][1]
        k_pool[pl.ds(whole + at, rows), :] = own[k][0]
        v_pool[pl.ds(whole + at, rows), :] = own[k][1]
    tail = jnp.zeros((slots * BLK, k_pool.shape[1]), k_pool.dtype)
    k_pool[2 * whole :, :] = tail
    v_pool[2 * whole :, :] = tail

    @pl.when(at_group % 2 == 1)
    def _():
        to = pl.multiple_of(2 * whole + (at_group // 2) * BLK, BLK)
        start = pl.multiple_of(offset * BLK, BLK)
        k_pool[pl.ds(to, BLK), :] = k_pool[pl.ds(start, BLK), :]
        v_pool[pl.ds(to, BLK), :] = v_pool[pl.ds(start, BLK), :]

    for index, ref in enumerate(far):
        distance = index + 2

        @pl.when((at_group >= distance) & ((at_group - distance) % 2 == 0))
        def _():
            to = pl.multiple_of(2 * whole + ((at_group - distance) // 2) * BLK, BLK)
            k_pool[pl.ds(to, BLK), :] = ref[0]
            v_pool[pl.ds(to, BLK), :] = ref[1]


def fill_queries(meta_ref, qd, q_pool, g_pool, group, rows):
    me = meta_ref[0]
    for k in range(group):
        at = pl.multiple_of((me ^ k) * rows, rows)
        q_pool[pl.ds(at, rows), :] = qd[k][0]
        g_pool[pl.ds(at, rows), :] = qd[k][1]


def causal_masks():
    key_at = lax.broadcasted_iota(jnp.int32, (BLK, PAIR), 0)
    query_at = lax.broadcasted_iota(jnp.int32, (BLK, PAIR), 1)
    first = (key_at <= query_at) | (query_at >= BLK)
    second = key_at <= query_at - BLK
    return first, second


def masked_scores(keys, query, bias, masks):
    raw = dot(keys, query, NT) * SCALE2
    tiles = []
    for j in range(keys.shape[0] // BLK):
        tile = raw[j * BLK : (j + 1) * BLK] + bias[j]
        if masks is not None and j in (LOCAL - 1, LOCAL):
            tile = jnp.where(masks[j - LOCAL + 1], tile, -jnp.inf)
        tiles.append(tile)
    return jnp.concatenate(tiles, axis=0)


def bias_rows(bias_ref, t, picked):
    return [bias_ref[t, j : j + 1, :] for j in picked]


def forward(head, qd, own, prev, far, bias, stats, meta, group, slots):
    rows = qd[0].shape[1]
    whole = group * rows
    pairs = whole // PAIR
    counts = (group, group, group, len(far))

    def body(meta_ref, bias_ref, before_ref, *refs):
        (qd_refs, own_refs, prev_refs, far_refs), refs = split_refs(refs, counts)
        out_ref, stats_ref, k_pool, v_pool, q_pool, g_pool = refs
        fill_pools(meta_ref, own_refs, prev_refs, far_refs, k_pool, v_pool, group, rows, slots)
        fill_queries(meta_ref, qd_refs, q_pool, g_pool, group, rows)
        stats_ref[...] = before_ref[...]
        masks = causal_masks()
        for t in range(pairs):
            here = slice(t * PAIR, (t + 1) * PAIR)
            window = slice(t * PAIR + BLK, t * PAIR + BLK + SPAN * BLK)
            keys = jnp.concatenate([k_pool[window, :], k_pool[2 * whole :, :]], axis=0)
            vals = jnp.concatenate([v_pool[window, :], v_pool[2 * whole :, :]], axis=0)
            s = masked_scores(keys, q_pool[here, :], bias_rows(bias_ref, t, range(SPAN + slots)), masks)
            top = jnp.max(s, axis=0, keepdims=True)
            e = jnp.exp2(s - top)
            total = jnp.sum(e, axis=0, keepdims=True)
            low = (e * (1.0 / total)).astype(jnp.bfloat16)
            out = dot(low, vals, TN).astype(jnp.bfloat16)
            out_ref[here, :] = out
            product = out.astype(jnp.float32) * g_pool[here, :].astype(jnp.float32)
            stats_ref[t, 2 * head : 2 * head + 1, :] = top + jnp.log2(total)
            stats_ref[t, 2 * head + 1 : 2 * head + 2, :] = jnp.sum(product.T, axis=0, keepdims=True)

    span = (SPAN + slots) * BLK
    lanes = [None, None] + [head] * sum(counts)
    return call(
        body, (meta,), (bias, stats, *qd, *own, *prev, *far),
        [shape((whole, HD)), shape(stats.shape, jnp.float32)],
        [
            pltpu.VMEM((2 * whole + slots * BLK, HD), jnp.bfloat16),
            pltpu.VMEM((2 * whole + slots * BLK, HD), jnp.bfloat16),
            pltpu.VMEM((whole, HD), jnp.bfloat16),
            pltpu.VMEM((whole, HD), jnp.bfloat16),
        ],
        cost(4 * whole * span * HD * 2, 3 * 1024 * 1024, whole * span),
        f"attention_{head}", lanes,
    )


def backward(head, qd, own, prev, far, bias, stats, meta, group, slots):
    rows = qd[0].shape[1]
    whole = group * rows
    pairs = whole // PAIR
    counts = (group, group, group, len(far))
    everything = 2 * whole + slots * BLK

    def body(meta_ref, bias_ref, stats_ref, *refs):
        (qd_refs, own_refs, prev_refs, far_refs), refs = split_refs(refs, counts)
        ((dq_ref, grad_ref), far_outs), refs = split_refs(refs, (2, len(far)))
        k_pool, v_pool, q_pool, g_pool, far_sum = refs
        at_group = meta_ref[1]
        fill_pools(meta_ref, own_refs, prev_refs, far_refs, k_pool, v_pool, group, rows, slots)
        fill_queries(meta_ref, qd_refs, q_pool, g_pool, group, rows)
        masks = causal_masks()
        grad_ref[...] = jnp.zeros_like(grad_ref)
        far_sum[...] = jnp.zeros_like(far_sum)
        for t in range(pairs):
            here = slice(t * PAIR, (t + 1) * PAIR)
            window = slice(t * PAIR + BLK, t * PAIR + BLK + SPAN * BLK)
            before = max(whole - (t * PAIR + BLK), 0)
            end = SPAN * BLK
            mine = slice(t * PAIR + BLK + before - whole, t * PAIR + BLK + end - whole)
            keys = jnp.concatenate([k_pool[window, :], k_pool[2 * whole :, :]], axis=0)
            vals = jnp.concatenate([v_pool[window, :], v_pool[2 * whole :, :]], axis=0)
            query, grad = q_pool[here, :], g_pool[here, :]
            s = masked_scores(keys, query, bias_rows(bias_ref, t, range(SPAN + slots)), masks)
            probs = jnp.exp2(s - stats_ref[t, 2 * head : 2 * head + 1, :])
            delta = stats_ref[t, 2 * head + 1 : 2 * head + 2, :]
            ds = (probs * (dot(vals, grad, NT) - delta)).astype(jnp.bfloat16)
            low = probs.astype(jnp.bfloat16)
            dq_ref[here, :] = (dot(ds, keys, TN) * SCALE).astype(jnp.bfloat16)
            grad_ref[0, mine, :] += dot(ds[before:end], query, NN)
            grad_ref[1, mine, :] += dot(low[before:end], grad, NN)
            far_sum[0] += dot(ds[end:], query, NN)
            far_sum[1] += dot(low[end:], grad, NN)
        for index, ref in enumerate(far_outs):
            slot = jnp.maximum(at_group - index - 2, 0) // 2
            start = pl.multiple_of(slot * BLK, BLK)
            ref[0] = (far_sum[0, pl.ds(start, BLK), :] * SCALE).astype(jnp.bfloat16)
            ref[1] = far_sum[1, pl.ds(start, BLK), :].astype(jnp.bfloat16)

    span = (SPAN + slots) * BLK
    lanes = [None, None] + [head] * sum(counts)
    outs = call(
        body, (meta,), (bias, stats, *qd, *own, *prev, *far),
        [shape((whole, HD)), shape((2, whole, HD), jnp.float32)]
        + [shape((2, BLK, HD))] * len(far),
        [
            pltpu.VMEM((everything, HD), jnp.bfloat16),
            pltpu.VMEM((everything, HD), jnp.bfloat16),
            pltpu.VMEM((whole, HD), jnp.bfloat16),
            pltpu.VMEM((whole, HD), jnp.bfloat16),
            pltpu.VMEM((2, slots * BLK, HD), jnp.float32),
        ],
        cost(8 * whole * span * HD * 2, 4 * 1024 * 1024, whole * span),
        f"attention_back_{head}", lanes,
    )
    return outs[0], outs[1], outs[2:]


def backward_next(grads, qd, own, bias, stats, meta, group):
    rows, width = qd[0].shape[1:]
    heads = width // HD
    whole = group * rows
    pairs = whole // PAIR

    def body(meta_ref, bias_ref, stats_ref, *refs):
        (grad_refs, qd_refs, own_refs, (out,)), refs = split_refs(refs, (heads, group, group, 1))
        k_pool, v_pool, q_pool, g_pool = refs
        me = meta_ref[0]
        strided = pl.ds(pl.multiple_of(meta_ref[2] * BLK, BLK), BLK)
        for k in range(group):
            at = pl.multiple_of((me ^ k) * rows, rows)
            k_pool[pl.ds(at, rows), :] = own_refs[k][0]
            v_pool[pl.ds(at, rows), :] = own_refs[k][1]
        fill_queries(meta_ref, qd_refs, q_pool, g_pool, group, rows)
        for h in range(heads):
            lanes = slice(h * HD, (h + 1) * HD)
            out[0, :, lanes] = grad_refs[h][0]
            out[1, :, lanes] = grad_refs[h][1]
            for t in range(pairs):
                here = slice(t * PAIR, (t + 1) * PAIR)
                window = slice(t * PAIR + BLK, whole)
                near = (whole - BLK) // BLK - t * (PAIR // BLK)
                keys = jnp.concatenate([k_pool[window, lanes], k_pool[strided, lanes]], axis=0)
                vals = jnp.concatenate([v_pool[window, lanes], v_pool[strided, lanes]], axis=0)
                query, grad = q_pool[here, lanes], g_pool[here, lanes]
                rows_here = bias_rows(bias_ref, t, list(range(near)) + [SPAN])
                s = masked_scores(keys, query, rows_here, None)
                probs = jnp.exp2(s - stats_ref[t, 2 * h : 2 * h + 1, :])
                delta = stats_ref[t, 2 * h + 1 : 2 * h + 2, :]
                ds = (probs * (dot(vals, grad, NT) - delta)).astype(jnp.bfloat16)
                dk = dot(ds, query, NN)
                dv = dot(probs.astype(jnp.bfloat16), grad, NN)
                out[0, window, lanes] += dk[: near * BLK]
                out[1, window, lanes] += dv[: near * BLK]
                out[0, strided, lanes] += dk[near * BLK :]
                out[1, strided, lanes] += dv[near * BLK :]
        out[0] = out[0] * SCALE

    return call(
        body, (meta,), (bias, stats, *grads, *qd, *own),
        [shape((2, whole, width), jnp.float32)],
        [pltpu.VMEM((whole, width), jnp.bfloat16)] * 4,
        cost(8 * whole * 5 * BLK * width, 7 * 1024 * 1024, whole * 5 * BLK * heads),
        "attention_back_next",
    )[0]


def combine(dq, own, far, meta, group, rows):
    whole, width = own.shape[1:]

    def body(meta_ref, own_ref, *refs):
        (dq_refs, far_refs, outs, (acc,)), refs = split_refs(refs, (len(dq), len(far), group, 1))
        me, offset = meta_ref[0], meta_ref[2]
        acc[...] = own_ref[...]
        at = pl.multiple_of(offset * BLK, BLK)
        for ref in far_refs:
            acc[:, pl.ds(at, BLK), :] += ref[...].astype(jnp.float32)
        for k in range(group):
            here = pl.ds(pl.multiple_of((me ^ k) * rows, rows), rows)
            for h in range(len(dq)):
                outs[k][0, :, h * HD : (h + 1) * HD] = dq_refs[h][here, :]
            outs[k][1] = acc[0, here, :].astype(jnp.bfloat16)
            outs[k][2] = acc[1, here, :].astype(jnp.bfloat16)

    return call(
        body, (meta,), (own, *dq, *far), [shape((3, rows, width))] * group,
        [pltpu.VMEM((2, whole, width), jnp.float32)],
        cost(0, 4 * 1024 * 1024), "combine",
    )


def project(head, mine, theirs, attn, meta, group, parts):
    height, whole = mine.shape
    each = 2 * height // parts
    full = group * HD

    def body(meta_ref, mine_ref, theirs_ref, *refs):
        (attn_refs, (keep, send, pool, total)), refs = split_refs(refs, (group, 4))
        me, at_group, core = meta_ref[0], meta_ref[1], meta_ref[3]
        for k in range(group):
            at = pl.multiple_of((me ^ k) * HD, HD)
            pool[:, pl.ds(at, HD)] = attn_refs[k][...]
        first = pl.ds(pl.multiple_of(core * height, height), height)
        second = pl.ds(pl.multiple_of((1 - core) * height, height), height)
        total[first, :] = dot(mine_ref[...], pool[...], NN)
        total[second, :] = dot(theirs_ref[...], pool[...], NN)
        for m in range(parts):
            at = pl.multiple_of((at_group ^ m) * each, each)
            if m % 2 == 0:
                keep[m // 2] = total[pl.ds(at, each), :]
            else:
                send[m // 2] = total[pl.ds(at, each), :].astype(jnp.bfloat16)

    return call(
        body, (meta,), (mine, theirs, *attn),
        [shape((parts // 2, each, full), jnp.float32), shape((parts // 2, each, full))],
        [pltpu.VMEM((whole, full), jnp.bfloat16), pltpu.VMEM((2 * height, full), jnp.float32)],
        cost(4 * height * whole * full, 6 * 1024 * 1024), f"project_{head}",
    )


def halve(head, keep, arrived):
    parts, each, full = keep.shape

    def body(keep_ref, arrived_ref, stay, send):
        for m in range(parts):
            summed = keep_ref[m] + arrived_ref[m].astype(jnp.float32)
            if m % 2 == 0:
                stay[m // 2] = summed
            else:
                send[m // 2] = summed.astype(jnp.bfloat16)

    return call(
        body, (), (keep, arrived),
        [shape((parts // 2, each, full), jnp.float32), shape((parts // 2, each, full))], [],
        cost(0, 3 * 1024 * 1024), f"halve_{head}",
    )


def finish(keep, arrived, group):
    heads = len(keep)
    each = keep[0].shape[1]

    def body(*refs):
        out = refs[2 * heads]
        for h in range(heads):
            total = refs[h][0] + refs[heads + h][0].astype(jnp.float32)
            for j in range(group):
                at = (j * heads + h) * HD
                out[:, at : at + HD] = total[:, j * HD : (j + 1) * HD]

    return call(
        body, (), (*keep, *arrived), [shape((each, group * heads * HD), jnp.float32)], [],
        cost(0, 3 * 1024 * 1024), "finish",
    )[0]


def unpack(pieces, meta, group):
    rows, width = pieces[0].shape[1:]

    def body(meta_ref, *refs):
        me = meta_ref[0]
        for k in range(group):
            at = pl.ds(pl.multiple_of((me ^ k) * width, width), width)
            for which in range(3):
                refs[group + which][:, at] = refs[k][which]

    return call(
        body, (meta,), tuple(pieces), [shape((rows, group * width))] * 3, [],
        cost(0, 3 * 1024 * 1024), "unpack",
    )


def listed(table, ids):
    return jnp.any(table[:, None, :] == ids[:, :, None], axis=2) & (ids >= 0)


def after(value, *others):
    return lax.optimization_barrier((value, *others))[0]


def reading(layout, at_group, offset, slots):
    ids = at_group * LOCAL + jnp.arange(LOCAL, dtype=jnp.int32)
    table = lax.dynamic_slice_in_dim(layout, at_group * LOCAL, LOCAL, 0)
    base = ids - jnp.arange(LOCAL, dtype=jnp.int32) % 2 - (LOCAL - 1)
    near_ids = base[:, None] + jnp.arange(SPAN, dtype=jnp.int32)[None, :]
    near = listed(table, near_ids) & (near_ids >= ids[:, None] - (LOCAL - 1))
    far_ids = jnp.broadcast_to(
        jnp.arange(slots, dtype=jnp.int32)[None, :] * STRIDE + offset, (LOCAL, slots)
    )
    distant = listed(table, far_ids) & (far_ids < ids[:, None] - (LOCAL - 1))
    return near, distant


def as_bias(reads):
    bias = jnp.where(reads, 0.0, -jnp.inf).astype(jnp.float32)
    bias = bias.reshape(LOCAL // 2, 2, reads.shape[1]).transpose(0, 2, 1)
    return jnp.repeat(bias, BLK, axis=2)


def local(devices, queries, keys, values, out_grad, proj_weight, layout):
    rows, columns = queries.shape
    group = LOCAL * BLK // rows
    parts = devices // group
    width = columns // group
    heads = width // HD
    blocks = layout.shape[0]
    slots = blocks // STRIDE
    position = lax.axis_index("seq")
    me, at_group = position % group, position // group
    core = lax.axis_index("head")
    offset = layout[blocks - 1, 0] % STRIDE
    place = jnp.stack([me, at_group]).astype(jnp.int32)
    meta = jnp.stack([me, at_group, offset, core]).astype(jnp.int32)

    def swap(piece, k):
        route = [(i, (i // group) * group + ((i % group) ^ k)) for i in range(devices)]
        return lax.ppermute(piece, "seq", route)

    def shifted(piece, distance):
        route = [
            (i, i + distance * group)
            for i in range(devices)
            if 0 <= i + distance * group < devices
        ]
        return lax.ppermute(piece, "seq", route)

    def swap_groups(piece, bit):
        route = [(i, ((i // group) ^ bit) * group + i % group) for i in range(devices)]
        return lax.ppermute(piece, "seq", route)

    def summary_route(distance, back):
        route = [
            (i, i + distance * group)
            for i in range(devices - distance * group)
            if (i // group) % 2 == 0
        ]
        return [(b, a) for a, b in route] if back else route

    def exchange(pieces):
        return [pieces[0]] + [swap(pieces[k], k) for k in range(1, group)]

    kv = pack_kv(keys, values, place, group, width)
    own_kv = exchange(kv)
    prev_kv = [shifted(kv[0], 1)]
    prev_kv += [shifted(own_kv[k], 1) for k in range(1, group)]
    qd_cut = grads_packed(queries, out_grad, proj_weight, after(place, kv[0]), group, width)
    qd = exchange(qd_cut)
    next_qd = [shifted(piece, -1) for piece in qd]
    strided = pick_summary(own_kv, meta, group)
    far = [
        lax.ppermute(strided, "seq", summary_route(distance, False))
        for distance in range(2, parts)
    ]
    og = exchange(pack_out_grad(out_grad, after(meta, qd[1], qd[2]), group, parts))
    mine = join_columns(og, meta, group)
    theirs = lax.ppermute(mine, "head", [(0, 1), (1, 0)])

    near, distant = reading(layout, at_group, offset, slots)
    bias = as_bias(jnp.concatenate([near, distant], axis=1))
    follows = at_group + 1 < parts
    near, distant = reading(layout, at_group + 1, offset, slots)
    hers = jnp.any(distant & (jnp.arange(slots)[None, :] * 2 == at_group), axis=1, keepdims=True)
    bias_next = as_bias(jnp.concatenate([near, hers], axis=1) & follows)

    stats = jnp.zeros((LOCAL // 2, 2 * heads, PAIR), jnp.float32)
    attn = []
    for h in range(heads):
        got, stats = forward(h, qd, own_kv, prev_kv, far, bias, stats, meta, group, slots)
        attn.append([got] + [swap(got, k) for k in range(1, group)])
    next_stats = shifted(stats, -1)

    dq, grads, far_grads, keep, arrived = [], [], [], [], []
    for h in range(heads):
        got = backward(h, qd, own_kv, prev_kv, far, bias, stats, meta, group, slots)
        dq.append(got[0])
        grads.append(got[1])
        far_grads.append(got[2])
        kept, sent = project(h, mine, theirs, attn[h], meta, group, parts)
        bit = 1
        arrival = swap_groups(sent, bit)
        while kept.shape[0] > 1:
            bit *= 2
            kept, sent = halve(h, kept, arrival)
            arrival = swap_groups(sent, bit)
        keep.append(kept)
        arrived.append(arrival)
    far_back = [
        lax.ppermute(jnp.concatenate(pieces, axis=2), "seq", summary_route(index + 2, True))
        for index, pieces in enumerate(zip(*far_grads))
    ]
    own_grad = backward_next(grads, next_qd, own_kv, bias_next, next_stats, meta, group)
    final = exchange(combine(dq, own_grad, far_back, meta, group, rows))
    query_grad, key_grad, value_grad = unpack(final, meta, group)
    proj_grad = finish(keep, arrived, group)
    return (query_grad, key_grad, value_grad, proj_grad)


def solution(mesh):
    split = P(("dp", "seq"), "head")
    return jax.shard_map(
        functools.partial(local, mesh.shape["seq"]),
        mesh=mesh,
        in_specs=(split, split, split, P(("dp", "seq"), None), P(None, "head"), P()),
        out_specs=(split, split, split, split),
        check_vma=False,
    )
```

```python
import functools
import math

import jax
import jax.numpy as jnp
from jax import lax
from jax.experimental import pallas as pl
from jax.experimental.pallas import tpu as pltpu
from jax.sharding import PartitionSpec as P

HD = 128
BLK = 128
LOCAL = 8
STRIDE = 16
PAIR = 2 * BLK
SPAN = LOCAL + 1
SCALE = HD ** (-0.5)
SCALE2 = SCALE * math.log2(math.e)
MIB = 1024 * 1024

NT = (((1,), (1,)), ((), ()))
NN = (((1,), (0,)), ((), ()))
TN = (((0,), (0,)), ((), ()))
SMEM = pl.BlockSpec(memory_space=pltpu.SMEM)
VMEM = pl.BlockSpec(memory_space=pltpu.VMEM)


def shape(dims, dtype=jnp.bfloat16):
    return jax.ShapeDtypeStruct(dims, dtype)


def dot(a, b, dims):
    return lax.dot_general(a, b, dims, preferred_element_type=jnp.float32)


def params(size):
    return pltpu.CompilerParams(vmem_limit_bytes=size * MIB)


def cost(flops, size, exps=0):
    return pl.CostEstimate(flops=1, bytes_accessed=1, transcendentals=0)


def call(body, scalars, arrays, outs, scratch, estimate, name, size=16):
    return pl.pallas_call(
        body,
        out_shape=outs,
        in_specs=[SMEM] * len(scalars) + [VMEM] * len(arrays),
        out_specs=[VMEM] * len(outs),
        scratch_shapes=scratch,
        compiler_params=params(size),
        cost_estimate=estimate,
        name=name,
    )(*scalars, *arrays)


def one_head(refs, head):
    return [ref.at[(slice(None),) * (ref.ndim - 1) + (pl.ds(head * HD, HD),)] for ref in refs]


def split_refs(refs, counts):
    refs, taken = list(refs), []
    for count in counts:
        taken.append(refs[:count])
        refs = refs[count:]
    return taken, refs


def pack_kv(keys, values, meta, group, width):
    rows = keys.shape[0]

    def body(meta_ref, k_ref, v_ref, *outs):
        me = meta_ref[0]
        for k in range(group):
            at = pl.multiple_of((me ^ k) * width, width)
            outs[k][0] = k_ref[:, pl.ds(at, width)]
            outs[k][1] = v_ref[:, pl.ds(at, width)]

    return call(
        body, (meta,), (keys, values), [shape((2, rows, width))] * group, [],
        cost(0, 4 * keys.size * 2), "pack_kv",
    )


def grads_packed(queries, out_grad, proj_weight, meta, group, width):
    rows, depth = out_grad.shape

    def body(meta_ref, q_ref, og_ref, w_ref, *outs):
        step = pl.program_id(0)
        got = dot(og_ref[...], w_ref[...], NN).astype(jnp.bfloat16)
        for k in range(group):

            @pl.when(step == k)
            def _():
                outs[k][0] = q_ref[...]
                outs[k][1] = got

    return pl.pallas_call(
        body,
        out_shape=[shape((2, rows, width))] * group,
        grid_spec=pltpu.PrefetchScalarGridSpec(
            num_scalar_prefetch=1,
            grid=(group,),
            in_specs=[
                pl.BlockSpec((rows, width), lambda i, m: (0, m[0] ^ i)),
                pl.BlockSpec((rows, depth), lambda i, m: (0, 0)),
                pl.BlockSpec((depth, width), lambda i, m: (0, m[0] ^ i)),
            ],
            out_specs=[pl.BlockSpec((2, rows, width), lambda i, m: (0, 0, 0))] * group,
        ),
        compiler_params=params(16),
        cost_estimate=cost(2 * rows * depth * width * group, 12 * 1024 * 1024),
        name="attn_grad",
    )(meta, queries, out_grad, proj_weight)


def pack_out_grad(out_grad, meta, group, parts):
    rows, depth = out_grad.shape
    each = depth // (group * parts)
    half = parts // 2

    def body(meta_ref, og_ref, *outs):
        me, core = meta_ref[0], meta_ref[3]
        for k in range(group):
            for part in range(half):
                at = ((core * half + part) * group + (me ^ k)) * each
                at = pl.multiple_of(at, each)
                outs[k][part * each : (part + 1) * each, :] = og_ref[:, pl.ds(at, each)].T

    return call(
        body, (meta,), (out_grad,), [shape((half * each, rows))] * group, [],
        cost(0, 3 * out_grad.size), "pack_out_grad",
    )


def join_columns(pieces, meta, group):
    height, rows = pieces[0].shape

    def body(meta_ref, *refs):
        me = meta_ref[0]
        for k in range(group):
            at = pl.multiple_of((me ^ k) * rows, rows)
            refs[group][:, pl.ds(at, rows)] = refs[k][...]

    return call(
        body, (meta,), tuple(pieces), [shape((height, group * rows))], [],
        cost(0, 2 * 1024 * 1024), "join_columns",
    )[0]


def assemble_kv(pieces, meta, group):
    rows, width = pieces[0].shape[1:]

    def body(meta_ref, *refs):
        me = meta_ref[0]
        pool, rest, strided = refs[group:]
        for k in range(group):
            pool[:, pl.ds(pl.multiple_of((me ^ k) * rows, rows), rows), :] = refs[k][...]
            if k > 0:
                rest[k - 1] = refs[k][...]
        strided[...] = pool[:, pl.ds(pl.multiple_of(meta_ref[2] * BLK, BLK), BLK), :]

    return call(
        body, (meta,), tuple(pieces),
        [
            shape((2, group * rows, width)),
            shape((group - 1, 2, rows, width)),
            shape((2, BLK, width)),
        ],
        [], cost(0, 3 * 1024 * 1024), "assemble_kv",
    )


def assemble(pieces, meta, group):
    lead, rows, width = pieces[0].shape

    def body(meta_ref, *refs):
        me = meta_ref[0]
        for k in range(group):
            at = pl.multiple_of((me ^ k) * rows, rows)
            refs[group][:, pl.ds(at, rows), :] = refs[k][...]

    return call(
        body, (meta,), tuple(pieces), [shape((lead, group * rows, width))], [],
        cost(0, 2 * 1024 * 1024), "assemble",
    )[0]


def masks_of(layout, meta, parts, slots):
    width = layout.shape[1]
    pairs = LOCAL // 2

    def body(meta_ref, table, own_ref, next_ref):
        at_group = meta_ref[1]
        low_half = lax.broadcasted_iota(jnp.int32, (1, PAIR), 1) < BLK

        def bits_of(group_at, row):
            block = group_at * LOCAL + row
            base = block - row % 2 - (LOCAL - 1)
            at = jnp.minimum(block, table.shape[0] - 1)
            bits = jnp.int32(0)
            for c in range(width):
                entry = table[at, c]
                near = entry >= jnp.maximum(block - (LOCAL - 1), 0)
                place = jnp.where(near, entry - base, SPAN + jnp.maximum(entry, 0) // STRIDE)
                bit = jnp.left_shift(jnp.int32(1), place)
                bits = bits | jnp.where(entry >= 0, bit, 0)
            return jnp.where(group_at < parts, bits, 0)

        def row_of(first, second, place):
            one = jnp.where((jnp.right_shift(first, place) & 1) == 1, 0.0, -jnp.inf)
            two = jnp.where((jnp.right_shift(second, place) & 1) == 1, 0.0, -jnp.inf)
            return jnp.where(low_half, one, two).astype(jnp.float32)

        for t in range(pairs):
            first, second = bits_of(at_group, 2 * t), bits_of(at_group, 2 * t + 1)
            for place in range(SPAN + slots):
                own_ref[t, place : place + 1, :] = row_of(first, second, place)
            first, second = bits_of(at_group + 1, 2 * t), bits_of(at_group + 1, 2 * t + 1)
            for place in range(SPAN):
                next_ref[t, place : place + 1, :] = row_of(first, second, place)
            even = at_group % 2 == 0
            place = SPAN + at_group // 2
            first, second = jnp.where(even, first, 0), jnp.where(even, second, 0)
            next_ref[t, SPAN : SPAN + 1, :] = row_of(first, second, place)

    return call(
        body, (meta, layout), (),
        [
            shape((pairs, SPAN + slots, PAIR), jnp.float32),
            shape((pairs, SPAN + 1, PAIR), jnp.float32),
        ],
        [], cost(0, 128 * 1024), "masks",
    )


def fill_pools(meta_ref, own, prev, rest, far, k_pool, v_pool, group, rows, slots):
    me, at_group, offset = meta_ref[0], meta_ref[1], meta_ref[2]
    whole = group * rows
    k_pool[whole : 2 * whole, :] = own[0]
    v_pool[whole : 2 * whole, :] = own[1]
    for k in range(group):
        at = pl.multiple_of((me ^ k) * rows, rows)
        k_pool[pl.ds(at, rows), :] = prev[0] if k == 0 else rest[k - 1, 0]
        v_pool[pl.ds(at, rows), :] = prev[1] if k == 0 else rest[k - 1, 1]
    tail = jnp.zeros((slots * BLK, k_pool.shape[1]), k_pool.dtype)
    k_pool[2 * whole :, :] = tail
    v_pool[2 * whole :, :] = tail

    @pl.when(at_group % 2 == 1)
    def _():
        to = pl.multiple_of(2 * whole + (at_group // 2) * BLK, BLK)
        start = pl.multiple_of(offset * BLK, BLK)
        k_pool[pl.ds(to, BLK), :] = k_pool[pl.ds(start, BLK), :]
        v_pool[pl.ds(to, BLK), :] = v_pool[pl.ds(start, BLK), :]

    for index, ref in enumerate(far):
        distance = index + 2

        @pl.when((at_group >= distance) & ((at_group - distance) % 2 == 0))
        def _():
            to = pl.multiple_of(2 * whole + ((at_group - distance) // 2) * BLK, BLK)
            k_pool[pl.ds(to, BLK), :] = ref[0]
            v_pool[pl.ds(to, BLK), :] = ref[1]


def causal_masks():
    key_at = lax.broadcasted_iota(jnp.int32, (BLK, PAIR), 0)
    query_at = lax.broadcasted_iota(jnp.int32, (BLK, PAIR), 1)
    first = (key_at <= query_at) | (query_at >= BLK)
    second = key_at <= query_at - BLK
    return first, second


def masked_scores(keys, query, bias, masks):
    raw = dot(keys, query, NT) * SCALE2
    tiles = []
    for j in range(keys.shape[0] // BLK):
        tile = raw[j * BLK : (j + 1) * BLK] + bias[j]
        if masks is not None and j in (LOCAL - 1, LOCAL):
            tile = jnp.where(masks[j - LOCAL + 1], tile, -jnp.inf)
        tiles.append(tile)
    return jnp.concatenate(tiles, axis=0)


def bias_rows(bias_ref, t, picked):
    return [bias_ref[t, j : j + 1, :] for j in picked]


def forward(head, qd, own, prev, rest, far, bias, stats, meta, group, slots):
    whole = qd.shape[1]
    rows = whole // group
    pairs = whole // PAIR
    counts = (4, len(far))

    def body(meta_ref, bias_ref, before_ref, *refs):
        (around, far_refs), refs = split_refs(refs, counts)
        qd_ref, *around = one_head(around, head)
        far_refs = one_head(far_refs, head)
        out_ref, stats_ref, k_pool, v_pool = refs
        fill_pools(meta_ref, *around, far_refs, k_pool, v_pool, group, rows, slots)
        stats_ref[...] = before_ref[...]
        masks = causal_masks()
        for t in range(pairs):
            here = slice(t * PAIR, (t + 1) * PAIR)
            window = slice(t * PAIR + BLK, t * PAIR + BLK + SPAN * BLK)
            keys = jnp.concatenate([k_pool[window, :], k_pool[2 * whole :, :]], axis=0)
            vals = jnp.concatenate([v_pool[window, :], v_pool[2 * whole :, :]], axis=0)
            s = masked_scores(keys, qd_ref[0, here, :], bias_rows(bias_ref, t, range(SPAN + slots)), masks)
            top = jnp.max(s, axis=0, keepdims=True)
            e = jnp.exp2(s - top)
            total = jnp.sum(e, axis=0, keepdims=True)
            low = (e * (1.0 / total)).astype(jnp.bfloat16)
            out = dot(low, vals, TN).astype(jnp.bfloat16)
            out_ref[here, :] = out
            product = out.astype(jnp.float32) * qd_ref[1, here, :].astype(jnp.float32)
            stats_ref[t, 2 * head : 2 * head + 1, :] = top + jnp.log2(total)
            stats_ref[t, 2 * head + 1 : 2 * head + 2, :] = jnp.sum(product.T, axis=0, keepdims=True)

    span = (SPAN + slots) * BLK
    return call(
        body, (meta,), (bias, stats, qd, own, prev, rest, *far),
        [shape((whole, HD)), shape(stats.shape, jnp.float32)],
        [pltpu.VMEM((2 * whole + slots * BLK, HD), jnp.bfloat16)] * 2,
        cost(4 * whole * span * HD * 2, 3 * 1024 * 1024, whole * span),
        f"attention_{head}", 24,
    )


def backward(head, qd, own, prev, rest, far, before, bias, stats, meta, group, slots):
    whole, width = qd.shape[1:]
    rows = whole // group
    pairs = whole // PAIR
    counts = (4, len(far), len(before))
    everything = 2 * whole + slots * BLK

    def body(meta_ref, bias_ref, stats_ref, *refs):
        (around, far_refs, before_refs), refs = split_refs(refs, counts)
        qd_ref, *around = one_head(around, head)
        far_refs = one_head(far_refs, head)
        ((dq_ref, grad_ref), far_outs), refs = split_refs(refs, (2, len(far)))
        k_pool, v_pool, far_sum = refs
        at_group = meta_ref[1]
        fill_pools(meta_ref, *around, far_refs, k_pool, v_pool, group, rows, slots)
        masks = causal_masks()
        grad_ref[...] = jnp.zeros_like(grad_ref)
        far_sum[...] = jnp.zeros_like(far_sum)
        for t in range(pairs):
            here = slice(t * PAIR, (t + 1) * PAIR)
            window = slice(t * PAIR + BLK, t * PAIR + BLK + SPAN * BLK)
            others = max(whole - (t * PAIR + BLK), 0)
            end = SPAN * BLK
            mine = slice(t * PAIR + BLK + others - whole, t * PAIR + BLK + end - whole)
            keys = jnp.concatenate([k_pool[window, :], k_pool[2 * whole :, :]], axis=0)
            vals = jnp.concatenate([v_pool[window, :], v_pool[2 * whole :, :]], axis=0)
            query, grad = qd_ref[0, here, :], qd_ref[1, here, :]
            s = masked_scores(keys, query, bias_rows(bias_ref, t, range(SPAN + slots)), masks)
            probs = jnp.exp2(s - stats_ref[t, 2 * head : 2 * head + 1, :])
            delta = stats_ref[t, 2 * head + 1 : 2 * head + 2, :]
            ds = (probs * (dot(vals, grad, NT) - delta)).astype(jnp.bfloat16)
            low = probs.astype(jnp.bfloat16)
            dq_ref[here, :] = (dot(ds, keys, TN) * SCALE).astype(jnp.bfloat16)
            grad_ref[0, mine, :] += dot(ds[others:end], query, NN)
            grad_ref[1, mine, :] += dot(low[others:end], grad, NN)
            far_sum[0] += dot(ds[end:], query, NN)
            far_sum[1] += dot(low[end:], grad, NN)
        for index, ref in enumerate(far_outs):
            slot = jnp.maximum(at_group - index - 2, 0) // 2
            start = pl.multiple_of(slot * BLK, BLK)
            ref[...] = before_refs[index][...]
            lanes = slice(head * HD, (head + 1) * HD)
            ref[0, :, lanes] = (far_sum[0, pl.ds(start, BLK), :] * SCALE).astype(jnp.bfloat16)
            ref[1, :, lanes] = far_sum[1, pl.ds(start, BLK), :].astype(jnp.bfloat16)

    span = (SPAN + slots) * BLK
    outs = call(
        body, (meta,), (bias, stats, qd, own, prev, rest, *far, *before),
        [shape((whole, HD)), shape((2, whole, HD), jnp.float32)]
        + [shape((2, BLK, width))] * len(far),
        [
            pltpu.VMEM((everything, HD), jnp.bfloat16),
            pltpu.VMEM((everything, HD), jnp.bfloat16),
            pltpu.VMEM((2, slots * BLK, HD), jnp.float32),
        ],
        cost(8 * whole * span * HD * 2, 4 * 1024 * 1024, whole * span),
        f"attention_back_{head}", 24,
    )
    return outs[0], outs[1], outs[2:]


def backward_next(grads, qd, own, bias, stats, meta):
    whole, width = qd.shape[1:]
    heads = width // HD
    pairs = whole // PAIR

    def body(meta_ref, bias_ref, stats_ref, *refs):
        (grad_refs, (qd_ref, own_ref, out)), refs = split_refs(refs, (heads, 3))
        strided = pl.ds(pl.multiple_of(meta_ref[2] * BLK, BLK), BLK)
        for h in range(heads):
            lanes = slice(h * HD, (h + 1) * HD)
            out[0, :, lanes] = grad_refs[h][0]
            out[1, :, lanes] = grad_refs[h][1]
            for t in range(pairs):
                here = slice(t * PAIR, (t + 1) * PAIR)
                window = slice(t * PAIR + BLK, whole)
                near = (whole - BLK) // BLK - t * (PAIR // BLK)
                keys = jnp.concatenate([own_ref[0, window, lanes], own_ref[0, strided, lanes]], axis=0)
                vals = jnp.concatenate([own_ref[1, window, lanes], own_ref[1, strided, lanes]], axis=0)
                query, grad = qd_ref[0, here, lanes], qd_ref[1, here, lanes]
                rows_here = bias_rows(bias_ref, t, list(range(near)) + [SPAN])
                s = masked_scores(keys, query, rows_here, None)
                probs = jnp.exp2(s - stats_ref[t, 2 * h : 2 * h + 1, :])
                delta = stats_ref[t, 2 * h + 1 : 2 * h + 2, :]
                ds = (probs * (dot(vals, grad, NT) - delta)).astype(jnp.bfloat16)
                dk = dot(ds, query, NN)
                dv = dot(probs.astype(jnp.bfloat16), grad, NN)
                out[0, window, lanes] += dk[: near * BLK]
                out[1, window, lanes] += dv[: near * BLK]
                out[0, strided, lanes] += dk[near * BLK :]
                out[1, strided, lanes] += dv[near * BLK :]
        out[0] = out[0] * SCALE

    return call(
        body, (meta,), (bias, stats, *grads, qd, own),
        [shape((2, whole, width), jnp.float32)], [],
        cost(8 * whole * 5 * BLK * width, 7 * 1024 * 1024, whole * 5 * BLK * heads),
        "attention_back_next", 24,
    )[0]


def combine(dq, own, far, meta, group, rows):
    whole, width = own.shape[1:]

    def body(meta_ref, own_ref, *refs):
        (dq_refs, far_refs, outs, (acc,)), refs = split_refs(refs, (len(dq), len(far), group, 1))
        me, offset = meta_ref[0], meta_ref[2]
        acc[...] = own_ref[...]
        at = pl.multiple_of(offset * BLK, BLK)
        for ref in far_refs:
            acc[:, pl.ds(at, BLK), :] += ref[...].astype(jnp.float32)
        for k in range(group):
            here = pl.ds(pl.multiple_of((me ^ k) * rows, rows), rows)
            for h in range(len(dq)):
                outs[k][0, :, h * HD : (h + 1) * HD] = dq_refs[h][here, :]
            outs[k][1] = acc[0, here, :].astype(jnp.bfloat16)
            outs[k][2] = acc[1, here, :].astype(jnp.bfloat16)

    return call(
        body, (meta,), (own, *dq, *far), [shape((3, rows, width))] * group,
        [pltpu.VMEM((2, whole, width), jnp.float32)],
        cost(0, 4 * 1024 * 1024), "combine",
    )


def project(head, mine, theirs, attn, before, meta, group, parts):
    height, whole = mine.shape
    each = 2 * height // parts
    full = group * HD
    more = parts // 2 - 1

    def body(meta_ref, mine_ref, theirs_ref, *refs):
        (attn_refs, before_refs, outs), refs = split_refs(refs, (group, len(before), 6))
        keep, first, odds, evens, pool, total = outs
        for ref in before_refs:
            first[:head] = ref[...]
        me, at_group, core = meta_ref[0], meta_ref[1], meta_ref[3]
        for k in range(group):
            at = pl.multiple_of((me ^ k) * HD, HD)
            pool[:, pl.ds(at, HD)] = attn_refs[k][...]
        upper = pl.ds(pl.multiple_of(core * height, height), height)
        lower = pl.ds(pl.multiple_of((1 - core) * height, height), height)
        total[upper, :] = dot(mine_ref[...], pool[...], NN)
        total[lower, :] = dot(theirs_ref[...], pool[...], NN)
        for m in range(parts):
            part = total[pl.ds(pl.multiple_of((at_group ^ m) * each, each), each), :]
            if m == 0:
                keep[...] = part
            elif m == 1:
                first[head] = part.astype(jnp.bfloat16)
            elif m % 2 == 1:
                odds[m // 2 - 1] = part.astype(jnp.bfloat16)
            else:
                evens[m // 2 - 1] = part

    return call(
        body, (meta,), (mine, theirs, *attn, *before),
        [
            shape((each, full), jnp.float32),
            shape((head + 1, each, full)),
            shape((more, each, full)),
            shape((more, each, full), jnp.float32),
        ],
        [pltpu.VMEM((whole, full), jnp.bfloat16), pltpu.VMEM((2 * height, full), jnp.float32)],
        cost(4 * height * whole * full, 6 * 1024 * 1024), f"project_{head}",
    )


def halve(head, evens, arrived):
    count, each, full = evens.shape
    more = (count - 1) // 2

    def body(evens_ref, arrived_ref, first, *rest):
        for m in range(1, count + 1):
            summed = evens_ref[m - 1] + arrived_ref[m - 1].astype(jnp.float32)
            if m == 1:
                first[...] = summed.astype(jnp.bfloat16)
            elif m % 2 == 1:
                rest[0][m // 2 - 1] = summed.astype(jnp.bfloat16)
            else:
                rest[1][m // 2 - 1] = summed

    others = [shape((more, each, full)), shape((more, each, full), jnp.float32)]
    return call(
        body, (), (evens, arrived), [shape((each, full))] + (others if more else []), [],
        cost(0, 3 * 1024 * 1024), f"halve_{head}",
    )


def finish(keep, neighbour, arrived, group):
    heads = len(keep)
    count = len(arrived[0])
    each = keep[0].shape[0]

    def body(*refs):
        (keep_refs, arrived_refs, (first, out)), refs = split_refs(refs, (heads, heads * count, 2))
        for h in range(heads):
            total = keep_refs[h][...] + first[h].astype(jnp.float32)
            for ref in arrived_refs[h * count : (h + 1) * count]:
                total = total + ref[...].astype(jnp.float32)
            for j in range(group):
                at = (j * heads + h) * HD
                out[:, at : at + HD] = total[:, j * HD : (j + 1) * HD]

    flat = [piece for pieces in arrived for piece in pieces]
    return call(
        body, (), (*keep, *flat, neighbour),
        [shape((each, group * heads * HD), jnp.float32)], [],
        cost(0, 3 * 1024 * 1024), "finish",
    )[0]


def unpack(pieces, meta, group):
    rows, width = pieces[0].shape[1:]

    def body(meta_ref, *refs):
        me = meta_ref[0]
        for k in range(group):
            at = pl.ds(pl.multiple_of((me ^ k) * width, width), width)
            for which in range(3):
                refs[group + which][:, at] = refs[k][which]

    return call(
        body, (meta,), tuple(pieces), [shape((rows, group * width))] * 3, [],
        cost(0, 3 * 1024 * 1024), "unpack",
    )


def after(value, *others):
    return lax.optimization_barrier((value, *others))[0]


def local(devices, queries, keys, values, out_grad, proj_weight, layout):
    rows, columns = queries.shape
    group = LOCAL * BLK // rows
    parts = devices // group
    width = columns // group
    heads = width // HD
    blocks = layout.shape[0]
    slots = blocks // STRIDE
    position = lax.axis_index("seq")
    me, at_group = position % group, position // group
    core = lax.axis_index("head")
    offset = layout[blocks - 1, 0] % STRIDE
    place = jnp.stack([me, at_group]).astype(jnp.int32)
    meta = jnp.stack([me, at_group, offset, core]).astype(jnp.int32)

    def swap(piece, k):
        route = [(i, (i // group) * group + ((i % group) ^ k)) for i in range(devices)]
        return lax.ppermute(piece, "seq", route)

    def shifted(piece, distance):
        route = [
            (i, i + distance * group)
            for i in range(devices)
            if 0 <= i + distance * group < devices
        ]
        return lax.ppermute(piece, "seq", route)

    def swap_groups(piece, bit):
        route = [(i, ((i // group) ^ bit) * group + i % group) for i in range(devices)]
        return lax.ppermute(piece, "seq", route)

    def summary_route(distance, back):
        route = [
            (i, i + distance * group)
            for i in range(devices - distance * group)
            if (i // group) % 2 == 0
        ]
        return [(b, a) for a, b in route] if back else route

    def exchange(pieces):
        return [pieces[0]] + [swap(pieces[k], k) for k in range(1, group)]

    def add_up(head, odds, evens, before, token):
        arrivals, bit = [], 2
        odds = after(odds, *jax.tree.leaves(before))
        while True:
            first, *more = halve(head, evens, odds)
            token = after(token, first)
            arrivals.append(swap_groups(first, bit))
            if not more:
                return arrivals, token
            odds, evens = swap_groups(more[0], bit), more[1]
            bit *= 2

    kv = pack_kv(keys, values, place, group, width)
    own_kv = exchange(kv)
    prev = shifted(kv[0], 1)
    early = after(place, own_kv[1])
    qd_cut = grads_packed(queries, out_grad, proj_weight, early, group, width)
    pool, others, strided = assemble_kv(own_kv, after(meta, prev, qd_cut[0]), group)
    rest = shifted(others, 1)
    qd_pieces = exchange(qd_cut)
    bias, bias_next = masks_of(layout, after(meta, strided), parts, slots)
    qd = assemble(qd_pieces, after(meta, bias), group)
    next_qd = shifted(qd, -1)
    strided = after(strided, qd)
    far = [
        lax.ppermute(strided, "seq", summary_route(distance, False))
        for distance in range(2, parts)
    ]
    og = exchange(pack_out_grad(out_grad, after(meta, rest, *far), group, parts))

    stats = jnp.zeros((LOCAL // 2, 2 * heads, PAIR), jnp.float32)
    order = after(meta, og[0])
    attn = []
    for h in range(heads):
        got, stats = forward(h, qd, pool, prev, rest, far, bias, stats, order, group, slots)
        attn.append([got] + [swap(got, k) for k in range(1, group)])
        if h == 0:
            mine = join_columns(og, after(meta, got), group)
            theirs = lax.ppermute(mine, "head", [(0, 1), (1, 0)])
        order = after(meta, got, mine)
    next_stats = shifted(stats, -1)

    dq, grads, keep, finals, firsts = [], [], [], [], []
    far_grads = [jnp.zeros((2, BLK, width), jnp.bfloat16) for _ in far]
    order = after(meta, stats, theirs)
    for h in range(heads):
        got = backward(
            h, qd, pool, prev, rest, far, far_grads, bias, stats, order, group, slots
        )
        dq.append(got[0])
        grads.append(got[1])
        far_grads = got[2]
        order = after(order, got[0], next_stats)
        if h > 0:
            sums, order = add_up(h - 1, odds, evens, got[0], order)
            finals.append(sums)
        kept, first, odds, evens = project(
            h, mine, theirs, attn[h], firsts, order, group, parts
        )
        keep.append(kept)
        firsts = [first]
        odds = swap_groups(odds, 1)
        order = after(meta, first, next_qd)
    neighbour = swap_groups(first, 1)
    far_back = [
        lax.ppermute(piece, "seq", summary_route(index + 2, True))
        for index, piece in enumerate(far_grads)
    ]
    own_grad = backward_next(grads, next_qd, pool, bias_next, next_stats, order)
    sums, order = add_up(heads - 1, odds, evens, (own_grad, finals[0]), meta)
    finals.append(sums)
    final = exchange(combine(dq, own_grad, far_back, order, group, rows))
    query_grad, key_grad, value_grad = unpack(final, meta, group)
    proj_grad = finish(keep, neighbour, finals, group)
    return (query_grad, key_grad, value_grad, proj_grad)


def solution(mesh):
    split = P(("dp", "seq"), "head")
    return jax.shard_map(
        functools.partial(local, mesh.shape["seq"]),
        mesh=mesh,
        in_specs=(split, split, split, P(("dp", "seq"), None), P(None, "head"), P()),
        out_specs=(split, split, split, split),
        check_vma=False,
    )
```

```python
import functools
import math

import jax
import jax.numpy as jnp
from jax import lax
from jax.experimental import pallas as pl
from jax.experimental.pallas import tpu as pltpu
from jax.sharding import PartitionSpec as P

HD = 128
BLK = 128
LOCAL = 8
STRIDE = 16
PAIR = 2 * BLK
SPAN = LOCAL + 1
SCALE = HD ** (-0.5)
SCALE2 = SCALE * math.log2(math.e)
MIB = 1024 * 1024

NT = (((1,), (1,)), ((), ()))
NN = (((1,), (0,)), ((), ()))
TN = (((0,), (0,)), ((), ()))
SMEM = pl.BlockSpec(memory_space=pltpu.SMEM)
VMEM = pl.BlockSpec(memory_space=pltpu.VMEM)
HBM = pl.BlockSpec(memory_space=pltpu.HBM)


def shape(dims, dtype=jnp.bfloat16):
    return jax.ShapeDtypeStruct(dims, dtype)


def dot(a, b, dims):
    return lax.dot_general(a, b, dims, preferred_element_type=jnp.float32)


def params(size):
    return pltpu.CompilerParams(vmem_limit_bytes=size * MIB)


def cost(flops, size, exps=0):
    return pl.CostEstimate(flops=1, bytes_accessed=1, transcendentals=0)


def call(body, scalars, arrays, outs, scratch, estimate, name, size=16):
    return pl.pallas_call(
        body,
        out_shape=outs,
        in_specs=[SMEM] * len(scalars) + [VMEM] * len(arrays),
        out_specs=[VMEM] * len(outs),
        scratch_shapes=scratch,
        compiler_params=params(size),
        cost_estimate=estimate,
        name=name,
    )(*scalars, *arrays)


def one_head(refs, head):
    return [ref.at[(slice(None),) * (ref.ndim - 1) + (pl.ds(head * HD, HD),)] for ref in refs]


def split_refs(refs, counts):
    refs, taken = list(refs), []
    for count in counts:
        taken.append(refs[:count])
        refs = refs[count:]
    return taken, refs


def copied(*copies):
    for copy in copies:
        copy.start()
    for copy in copies:
        copy.wait()


def pack_kv(keys, values, meta, group, width):
    rows = keys.shape[0]

    def body(meta_ref, k_ref, v_ref, *refs):
        outs, sems = refs[:group], refs[group]
        me = meta_ref[0]
        copies = []
        for k in range(group):
            at = pl.ds(pl.multiple_of((me ^ k) * width, width), width)
            for which, source in enumerate((k_ref, v_ref)):
                copies.append(
                    pltpu.make_async_copy(source.at[:, at], outs[k].at[which], sems.at[k, which])
                )
        copied(*copies)

    return pl.pallas_call(
        body,
        out_shape=[shape((2, rows, width))] * group,
        in_specs=[SMEM, HBM, HBM],
        out_specs=[VMEM] * group,
        scratch_shapes=[pltpu.SemaphoreType.DMA((group, 2))],
        compiler_params=params(16),
        cost_estimate=cost(0, 4 * keys.size * 2),
        name="pack_kv",
    )(meta, keys, values)


def grads_packed(queries, out_grad, proj_weight, meta, group, width):
    rows, depth = out_grad.shape

    def body(meta_ref, q_ref, og_ref, w_ref, *refs):
        outs, (og, w, q_sems, w_sems, og_sem) = refs[:group], refs[group:]
        me = meta_ref[0]
        og_copy = pltpu.make_async_copy(og_ref, og, og_sem)
        og_copy.start()
        q_copies, w_copies = [], []
        for k in range(group):
            at = pl.ds(pl.multiple_of((me ^ k) * width, width), width)
            w_copies.append(pltpu.make_async_copy(w_ref.at[:, at], w.at[k], w_sems.at[k]))
            w_copies[k].start()
        for k in range(group):
            at = pl.ds(pl.multiple_of((me ^ k) * width, width), width)
            q_copies.append(pltpu.make_async_copy(q_ref.at[:, at], outs[k].at[0], q_sems.at[k]))
            q_copies[k].start()
        og_copy.wait()
        for k in range(group):
            w_copies[k].wait()
            outs[k][1] = dot(og[...], w[k], NN).astype(jnp.bfloat16)
        for k in range(group):
            q_copies[k].wait()

    return pl.pallas_call(
        body,
        out_shape=[shape((2, rows, width))] * group,
        in_specs=[SMEM, HBM, HBM, HBM],
        out_specs=[VMEM] * group,
        scratch_shapes=[
            pltpu.VMEM((rows, depth), jnp.bfloat16),
            pltpu.VMEM((group, depth, width), jnp.bfloat16),
            pltpu.SemaphoreType.DMA((group,)),
            pltpu.SemaphoreType.DMA((group,)),
            pltpu.SemaphoreType.DMA,
        ],
        compiler_params=params(24),
        cost_estimate=cost(2 * rows * depth * width * group, 12 * 1024 * 1024),
        name="attn_grad",
    )(meta, queries, out_grad, proj_weight)


def pack_out_grad(out_grad, meta, group, parts):
    rows, depth = out_grad.shape
    each = depth // (group * parts)
    half = parts // 2

    def body(meta_ref, og_ref, *refs):
        outs, (held, sems) = refs[:group], refs[group:]
        me, core = meta_ref[0], meta_ref[3]
        copies = []
        for k in range(group):
            for part in range(half):
                at = ((core * half + part) * group + (me ^ k)) * each
                at = pl.ds(pl.multiple_of(at, each), each)
                copies.append(
                    pltpu.make_async_copy(og_ref.at[:, at], held.at[k, part], sems.at[k, part])
                )
        copied(*copies)
        for k in range(group):
            for part in range(half):
                outs[k][part * each : (part + 1) * each, :] = held[k, part].T

    return pl.pallas_call(
        body,
        out_shape=[shape((half * each, rows))] * group,
        in_specs=[SMEM, HBM],
        out_specs=[VMEM] * group,
        scratch_shapes=[
            pltpu.VMEM((group, half, rows, each), jnp.bfloat16),
            pltpu.SemaphoreType.DMA((group, half)),
        ],
        compiler_params=params(16),
        cost_estimate=cost(0, 3 * out_grad.size),
        name="pack_out_grad",
    )(meta, out_grad)


def join_columns(pieces, meta, group):
    height, rows = pieces[0].shape

    def body(meta_ref, *refs):
        me = meta_ref[0]
        for k in range(group):
            at = pl.multiple_of((me ^ k) * rows, rows)
            refs[group][:, pl.ds(at, rows)] = refs[k][...]

    return call(
        body, (meta,), tuple(pieces), [shape((height, group * rows))], [],
        cost(0, 2 * 1024 * 1024), "join_columns",
    )[0]


def assemble_kv(pieces, meta, group):
    rows, width = pieces[0].shape[1:]

    def body(meta_ref, *refs):
        me = meta_ref[0]
        pool, rest, strided = refs[group:]
        for k in range(group):
            pool[:, pl.ds(pl.multiple_of((me ^ k) * rows, rows), rows), :] = refs[k][...]
            if k > 0:
                rest[k - 1] = refs[k][...]
        strided[...] = pool[:, pl.ds(pl.multiple_of(meta_ref[2] * BLK, BLK), BLK), :]

    return call(
        body, (meta,), tuple(pieces),
        [
            shape((2, group * rows, width)),
            shape((group - 1, 2, rows, width)),
            shape((2, BLK, width)),
        ],
        [], cost(0, 3 * 1024 * 1024), "assemble_kv",
    )


def assemble(pieces, meta, group):
    lead, rows, width = pieces[0].shape

    def body(meta_ref, *refs):
        me = meta_ref[0]
        for k in range(group):
            at = pl.multiple_of((me ^ k) * rows, rows)
            refs[group][:, pl.ds(at, rows), :] = refs[k][...]

    return call(
        body, (meta,), tuple(pieces), [shape((lead, group * rows, width))], [],
        cost(0, 2 * 1024 * 1024), "assemble",
    )[0]


def masks_of(layout, meta, parts, slots):
    width = layout.shape[1]
    pairs = LOCAL // 2

    def body(meta_ref, table, own_ref, next_ref):
        at_group = meta_ref[1]
        low_half = lax.broadcasted_iota(jnp.int32, (1, PAIR), 1) < BLK

        def bits_of(group_at, row):
            block = group_at * LOCAL + row
            base = block - row % 2 - (LOCAL - 1)
            at = jnp.minimum(block, table.shape[0] - 1)
            bits = jnp.int32(0)
            for c in range(width):
                entry = table[at, c]
                near = entry >= jnp.maximum(block - (LOCAL - 1), 0)
                place = jnp.where(near, entry - base, SPAN + jnp.maximum(entry, 0) // STRIDE)
                bit = jnp.left_shift(jnp.int32(1), place)
                bits = bits | jnp.where(entry >= 0, bit, 0)
            return jnp.where(group_at < parts, bits, 0)

        def row_of(first, second, place):
            one = jnp.where((jnp.right_shift(first, place) & 1) == 1, 0.0, -jnp.inf)
            two = jnp.where((jnp.right_shift(second, place) & 1) == 1, 0.0, -jnp.inf)
            return jnp.where(low_half, one, two).astype(jnp.float32)

        for t in range(pairs):
            first, second = bits_of(at_group, 2 * t), bits_of(at_group, 2 * t + 1)
            for place in range(SPAN + slots):
                own_ref[t, place : place + 1, :] = row_of(first, second, place)
            first, second = bits_of(at_group + 1, 2 * t), bits_of(at_group + 1, 2 * t + 1)
            for place in range(SPAN):
                next_ref[t, place : place + 1, :] = row_of(first, second, place)
            even = at_group % 2 == 0
            place = SPAN + at_group // 2
            first, second = jnp.where(even, first, 0), jnp.where(even, second, 0)
            next_ref[t, SPAN : SPAN + 1, :] = row_of(first, second, place)

    return call(
        body, (meta, layout), (),
        [
            shape((pairs, SPAN + slots, PAIR), jnp.float32),
            shape((pairs, SPAN + 1, PAIR), jnp.float32),
        ],
        [], cost(0, 128 * 1024), "masks",
    )


def fill_pools(meta_ref, own, prev, rest, far, k_pool, v_pool, group, rows, slots):
    me, at_group, offset = meta_ref[0], meta_ref[1], meta_ref[2]
    whole = group * rows
    k_pool[whole : 2 * whole, :] = own[0]
    v_pool[whole : 2 * whole, :] = own[1]
    for k in range(group):
        at = pl.multiple_of((me ^ k) * rows, rows)
        k_pool[pl.ds(at, rows), :] = prev[0] if k == 0 else rest[k - 1, 0]
        v_pool[pl.ds(at, rows), :] = prev[1] if k == 0 else rest[k - 1, 1]
    tail = jnp.zeros((slots * BLK, k_pool.shape[1]), k_pool.dtype)
    k_pool[2 * whole :, :] = tail
    v_pool[2 * whole :, :] = tail

    @pl.when(at_group % 2 == 1)
    def _():
        to = pl.multiple_of(2 * whole + (at_group // 2) * BLK, BLK)
        start = pl.multiple_of(offset * BLK, BLK)
        k_pool[pl.ds(to, BLK), :] = k_pool[pl.ds(start, BLK), :]
        v_pool[pl.ds(to, BLK), :] = v_pool[pl.ds(start, BLK), :]

    for index, ref in enumerate(far):
        distance = index + 2

        @pl.when((at_group >= distance) & ((at_group - distance) % 2 == 0))
        def _():
            to = pl.multiple_of(2 * whole + ((at_group - distance) // 2) * BLK, BLK)
            k_pool[pl.ds(to, BLK), :] = ref[0]
            v_pool[pl.ds(to, BLK), :] = ref[1]


def causal_masks():
    key_at = lax.broadcasted_iota(jnp.int32, (BLK, PAIR), 0)
    query_at = lax.broadcasted_iota(jnp.int32, (BLK, PAIR), 1)
    first = (key_at <= query_at) | (query_at >= BLK)
    second = key_at <= query_at - BLK
    return first, second


def masked_scores(keys, query, bias, masks):
    raw = dot(keys, query, NT) * SCALE2
    tiles = []
    for j in range(keys.shape[0] // BLK):
        tile = raw[j * BLK : (j + 1) * BLK] + bias[j]
        if masks is not None and j in (LOCAL - 1, LOCAL):
            tile = jnp.where(masks[j - LOCAL + 1], tile, -jnp.inf)
        tiles.append(tile)
    return jnp.concatenate(tiles, axis=0)


def bias_rows(bias_ref, t, picked):
    return [bias_ref[t, j : j + 1, :] for j in picked]


def forward(head, qd, own, prev, rest, far, bias, stats, meta, group, slots):
    whole = qd.shape[1]
    rows = whole // group
    pairs = whole // PAIR
    counts = (4, len(far))

    def body(meta_ref, bias_ref, before_ref, *refs):
        (around, far_refs), refs = split_refs(refs, counts)
        qd_ref, *around = one_head(around, head)
        far_refs = one_head(far_refs, head)
        out_ref, stats_ref, k_pool, v_pool = refs
        fill_pools(meta_ref, *around, far_refs, k_pool, v_pool, group, rows, slots)
        stats_ref[...] = before_ref[...]
        masks = causal_masks()
        for t in range(pairs):
            here = slice(t * PAIR, (t + 1) * PAIR)
            window = slice(t * PAIR + BLK, t * PAIR + BLK + SPAN * BLK)
            keys = jnp.concatenate([k_pool[window, :], k_pool[2 * whole :, :]], axis=0)
            vals = jnp.concatenate([v_pool[window, :], v_pool[2 * whole :, :]], axis=0)
            s = masked_scores(keys, qd_ref[0, here, :], bias_rows(bias_ref, t, range(SPAN + slots)), masks)
            top = jnp.max(s, axis=0, keepdims=True)
            e = jnp.exp2(s - top)
            total = jnp.sum(e, axis=0, keepdims=True)
            low = (e * (1.0 / total)).astype(jnp.bfloat16)
            out = dot(low, vals, TN).astype(jnp.bfloat16)
            out_ref[here, :] = out
            product = out.astype(jnp.float32) * qd_ref[1, here, :].astype(jnp.float32)
            stats_ref[t, 2 * head : 2 * head + 1, :] = top + jnp.log2(total)
            stats_ref[t, 2 * head + 1 : 2 * head + 2, :] = jnp.sum(product.T, axis=0, keepdims=True)

    span = (SPAN + slots) * BLK
    return call(
        body, (meta,), (bias, stats, qd, own, prev, rest, *far),
        [shape((whole, HD)), shape(stats.shape, jnp.float32)],
        [pltpu.VMEM((2 * whole + slots * BLK, HD), jnp.bfloat16)] * 2,
        cost(4 * whole * span * HD * 2, 3 * 1024 * 1024, whole * span),
        f"attention_{head}", 24,
    )


def backward(head, qd, own, prev, rest, far, before, bias, stats, meta, group, slots):
    whole, width = qd.shape[1:]
    rows = whole // group
    pairs = whole // PAIR
    counts = (4, len(far), len(before))
    everything = 2 * whole + slots * BLK

    def body(meta_ref, bias_ref, stats_ref, *refs):
        (around, far_refs, before_refs), refs = split_refs(refs, counts)
        qd_ref, *around = one_head(around, head)
        far_refs = one_head(far_refs, head)
        ((dq_ref, grad_ref), far_outs), refs = split_refs(refs, (2, len(far)))
        k_pool, v_pool, far_sum = refs
        at_group = meta_ref[1]
        fill_pools(meta_ref, *around, far_refs, k_pool, v_pool, group, rows, slots)
        masks = causal_masks()
        grad_ref[...] = jnp.zeros_like(grad_ref)
        far_sum[...] = jnp.zeros_like(far_sum)
        for t in range(pairs):
            here = slice(t * PAIR, (t + 1) * PAIR)
            window = slice(t * PAIR + BLK, t * PAIR + BLK + SPAN * BLK)
            others = max(whole - (t * PAIR + BLK), 0)
            end = SPAN * BLK
            mine = slice(t * PAIR + BLK + others - whole, t * PAIR + BLK + end - whole)
            keys = jnp.concatenate([k_pool[window, :], k_pool[2 * whole :, :]], axis=0)
            vals = jnp.concatenate([v_pool[window, :], v_pool[2 * whole :, :]], axis=0)
            query, grad = qd_ref[0, here, :], qd_ref[1, here, :]
            s = masked_scores(keys, query, bias_rows(bias_ref, t, range(SPAN + slots)), masks)
            probs = jnp.exp2(s - stats_ref[t, 2 * head : 2 * head + 1, :])
            delta = stats_ref[t, 2 * head + 1 : 2 * head + 2, :]
            ds = (probs * (dot(vals, grad, NT) - delta)).astype(jnp.bfloat16)
            low = probs.astype(jnp.bfloat16)
            dq_ref[here, :] = (dot(ds, keys, TN) * SCALE).astype(jnp.bfloat16)
            grad_ref[0, mine, :] += dot(ds[others:end], query, NN)
            grad_ref[1, mine, :] += dot(low[others:end], grad, NN)
            far_sum[0] += dot(ds[end:], query, NN)
            far_sum[1] += dot(low[end:], grad, NN)
        for index, ref in enumerate(far_outs):
            slot = jnp.maximum(at_group - index - 2, 0) // 2
            start = pl.multiple_of(slot * BLK, BLK)
            ref[...] = before_refs[index][...]
            lanes = slice(head * HD, (head + 1) * HD)
            ref[0, :, lanes] = (far_sum[0, pl.ds(start, BLK), :] * SCALE).astype(jnp.bfloat16)
            ref[1, :, lanes] = far_sum[1, pl.ds(start, BLK), :].astype(jnp.bfloat16)

    span = (SPAN + slots) * BLK
    outs = call(
        body, (meta,), (bias, stats, qd, own, prev, rest, *far, *before),
        [shape((whole, HD)), shape((2, whole, HD), jnp.float32)]
        + [shape((2, BLK, width))] * len(far),
        [
            pltpu.VMEM((everything, HD), jnp.bfloat16),
            pltpu.VMEM((everything, HD), jnp.bfloat16),
            pltpu.VMEM((2, slots * BLK, HD), jnp.float32),
        ],
        cost(8 * whole * span * HD * 2, 4 * 1024 * 1024, whole * span),
        f"attention_back_{head}", 24,
    )
    return outs[0], outs[1], outs[2:]


def backward_next(grads, qd, own, bias, stats, meta):
    whole, width = qd.shape[1:]
    heads = width // HD
    pairs = whole // PAIR

    def body(meta_ref, bias_ref, stats_ref, *refs):
        (grad_refs, (qd_ref, own_ref, out)), refs = split_refs(refs, (heads, 3))
        strided = pl.ds(pl.multiple_of(meta_ref[2] * BLK, BLK), BLK)
        for h in range(heads):
            lanes = slice(h * HD, (h + 1) * HD)
            out[0, :, lanes] = grad_refs[h][0]
            out[1, :, lanes] = grad_refs[h][1]
            for t in range(pairs):
                here = slice(t * PAIR, (t + 1) * PAIR)
                window = slice(t * PAIR + BLK, whole)
                near = (whole - BLK) // BLK - t * (PAIR // BLK)
                keys = jnp.concatenate([own_ref[0, window, lanes], own_ref[0, strided, lanes]], axis=0)
                vals = jnp.concatenate([own_ref[1, window, lanes], own_ref[1, strided, lanes]], axis=0)
                query, grad = qd_ref[0, here, lanes], qd_ref[1, here, lanes]
                rows_here = bias_rows(bias_ref, t, list(range(near)) + [SPAN])
                s = masked_scores(keys, query, rows_here, None)
                probs = jnp.exp2(s - stats_ref[t, 2 * h : 2 * h + 1, :])
                delta = stats_ref[t, 2 * h + 1 : 2 * h + 2, :]
                ds = (probs * (dot(vals, grad, NT) - delta)).astype(jnp.bfloat16)
                dk = dot(ds, query, NN)
                dv = dot(probs.astype(jnp.bfloat16), grad, NN)
                out[0, window, lanes] += dk[: near * BLK]
                out[1, window, lanes] += dv[: near * BLK]
                out[0, strided, lanes] += dk[near * BLK :]
                out[1, strided, lanes] += dv[near * BLK :]
        out[0] = out[0] * SCALE

    return call(
        body, (meta,), (bias, stats, *grads, qd, own),
        [shape((2, whole, width), jnp.float32)], [],
        cost(8 * whole * 5 * BLK * width, 7 * 1024 * 1024, whole * 5 * BLK * heads),
        "attention_back_next", 24,
    )[0]


def combine(dq, own, far, meta, group, rows):
    whole, width = own.shape[1:]

    def body(meta_ref, own_ref, *refs):
        (dq_refs, far_refs, outs, (acc,)), refs = split_refs(refs, (len(dq), len(far), group, 1))
        me, offset = meta_ref[0], meta_ref[2]
        acc[...] = own_ref[...]
        at = pl.multiple_of(offset * BLK, BLK)
        for ref in far_refs:
            acc[:, pl.ds(at, BLK), :] += ref[...].astype(jnp.float32)
        for k in range(group):
            here = pl.ds(pl.multiple_of((me ^ k) * rows, rows), rows)
            for h in range(len(dq)):
                outs[k][0, :, h * HD : (h + 1) * HD] = dq_refs[h][here, :]
            outs[k][1] = acc[0, here, :].astype(jnp.bfloat16)
            outs[k][2] = acc[1, here, :].astype(jnp.bfloat16)

    return call(
        body, (meta,), (own, *dq, *far), [shape((3, rows, width))] * group,
        [pltpu.VMEM((2, whole, width), jnp.float32)],
        cost(0, 4 * 1024 * 1024), "combine",
    )


def project(head, mine, theirs, attn, before, meta, group, parts):
    height, whole = mine.shape
    each = 2 * height // parts
    full = group * HD
    more = parts // 2 - 1

    def body(meta_ref, mine_ref, theirs_ref, *refs):
        (attn_refs, before_refs, outs), refs = split_refs(refs, (group, len(before), 6))
        keep, first, odds, evens, pool, total = outs
        for ref in before_refs:
            first[:head] = ref[...]
        me, at_group, core = meta_ref[0], meta_ref[1], meta_ref[3]
        for k in range(group):
            at = pl.multiple_of((me ^ k) * HD, HD)
            pool[:, pl.ds(at, HD)] = attn_refs[k][...]
        upper = pl.ds(pl.multiple_of(core * height, height), height)
        lower = pl.ds(pl.multiple_of((1 - core) * height, height), height)
        total[upper, :] = dot(mine_ref[...], pool[...], NN)
        total[lower, :] = dot(theirs_ref[...], pool[...], NN)
        for m in range(parts):
            part = total[pl.ds(pl.multiple_of((at_group ^ m) * each, each), each), :]
            if m == 0:
                keep[...] = part
            elif m == 1:
                first[head] = part.astype(jnp.bfloat16)
            elif m % 2 == 1:
                odds[m // 2 - 1] = part.astype(jnp.bfloat16)
            else:
                evens[m // 2 - 1] = part

    return call(
        body, (meta,), (mine, theirs, *attn, *before),
        [
            shape((each, full), jnp.float32),
            shape((head + 1, each, full)),
            shape((more, each, full)),
            shape((more, each, full), jnp.float32),
        ],
        [pltpu.VMEM((whole, full), jnp.bfloat16), pltpu.VMEM((2 * height, full), jnp.float32)],
        cost(4 * height * whole * full, 6 * 1024 * 1024), f"project_{head}",
    )


def halve(head, evens, arrived):
    count, each, full = evens.shape
    more = (count - 1) // 2

    def body(evens_ref, arrived_ref, first, *rest):
        for m in range(1, count + 1):
            summed = evens_ref[m - 1] + arrived_ref[m - 1].astype(jnp.float32)
            if m == 1:
                first[...] = summed.astype(jnp.bfloat16)
            elif m % 2 == 1:
                rest[0][m // 2 - 1] = summed.astype(jnp.bfloat16)
            else:
                rest[1][m // 2 - 1] = summed

    others = [shape((more, each, full)), shape((more, each, full), jnp.float32)]
    return call(
        body, (), (evens, arrived), [shape((each, full))] + (others if more else []), [],
        cost(0, 3 * 1024 * 1024), f"halve_{head}",
    )


def finish(keep, neighbour, arrived, group):
    heads = len(keep)
    count = len(arrived[0])
    each = keep[0].shape[0]

    def body(*refs):
        (keep_refs, arrived_refs, (first, out)), refs = split_refs(refs, (heads, heads * count, 2))
        for h in range(heads):
            total = keep_refs[h][...] + first[h].astype(jnp.float32)
            for ref in arrived_refs[h * count : (h + 1) * count]:
                total = total + ref[...].astype(jnp.float32)
            for j in range(group):
                at = (j * heads + h) * HD
                out[:, at : at + HD] = total[:, j * HD : (j + 1) * HD]

    flat = [piece for pieces in arrived for piece in pieces]
    return call(
        body, (), (*keep, *flat, neighbour),
        [shape((each, group * heads * HD), jnp.float32)], [],
        cost(0, 3 * 1024 * 1024), "finish",
    )[0]


def unpack(pieces, meta, group):
    rows, width = pieces[0].shape[1:]

    def body(meta_ref, *refs):
        me = meta_ref[0]
        for k in range(group):
            at = pl.ds(pl.multiple_of((me ^ k) * width, width), width)
            for which in range(3):
                refs[group + which][:, at] = refs[k][which]

    return call(
        body, (meta,), tuple(pieces), [shape((rows, group * width))] * 3, [],
        cost(0, 3 * 1024 * 1024), "unpack",
    )


def after(value, *others):
    return lax.optimization_barrier((value, *others))[0]


def local(devices, queries, keys, values, out_grad, proj_weight, layout):
    rows, columns = queries.shape
    group = LOCAL * BLK // rows
    parts = devices // group
    width = columns // group
    heads = width // HD
    blocks = layout.shape[0]
    slots = blocks // STRIDE
    position = lax.axis_index("seq")
    me, at_group = position % group, position // group
    core = lax.axis_index("head")
    offset = layout[blocks - 1, 0] % STRIDE
    place = jnp.stack([me, at_group]).astype(jnp.int32)
    meta = jnp.stack([me, at_group, offset, core]).astype(jnp.int32)

    def swap(piece, k):
        route = [(i, (i // group) * group + ((i % group) ^ k)) for i in range(devices)]
        return lax.ppermute(piece, "seq", route)

    def shifted(piece, distance):
        route = [
            (i, i + distance * group)
            for i in range(devices)
            if 0 <= i + distance * group < devices
        ]
        return lax.ppermute(piece, "seq", route)

    def swap_groups(piece, bit):
        route = [(i, ((i // group) ^ bit) * group + i % group) for i in range(devices)]
        return lax.ppermute(piece, "seq", route)

    def summary_route(distance, back):
        route = [
            (i, i + distance * group)
            for i in range(devices - distance * group)
            if (i // group) % 2 == 0
        ]
        return [(b, a) for a, b in route] if back else route

    def exchange(pieces):
        return [pieces[0]] + [swap(pieces[k], k) for k in range(1, group)]

    def add_up(head, odds, evens, before, token):
        arrivals, bit = [], 2
        odds = after(odds, *jax.tree.leaves(before))
        while True:
            first, *more = halve(head, evens, odds)
            token = after(token, first)
            arrivals.append(swap_groups(first, bit))
            if not more:
                return arrivals, token
            odds, evens = swap_groups(more[0], bit), more[1]
            bit *= 2

    kv = pack_kv(keys, values, place, group, width)
    own_kv = exchange(kv)
    prev = shifted(kv[0], 1)
    early = after(place, own_kv[1])
    qd_cut = grads_packed(queries, out_grad, proj_weight, early, group, width)
    pool, others, strided = assemble_kv(own_kv, after(meta, prev, qd_cut[0]), group)
    rest = shifted(others, 1)
    far = [
        lax.ppermute(strided, "seq", summary_route(distance, False))
        for distance in range(2, parts)
    ]
    qd_pieces = exchange(qd_cut)
    bias, bias_next = masks_of(layout, after(meta, strided), parts, slots)
    qd = assemble(qd_pieces, after(meta, bias, *far), group)
    next_qd = shifted(qd, -1)
    og = exchange(pack_out_grad(out_grad, after(meta, qd), group, parts))

    stats = jnp.zeros((LOCAL // 2, 2 * heads, PAIR), jnp.float32)
    order = after(meta, og[0])
    attn = []
    for h in range(heads):
        got, stats = forward(h, qd, pool, prev, rest, far, bias, stats, order, group, slots)
        attn.append([got] + [swap(got, k) for k in range(1, group)])
        if h == 0:
            mine = join_columns(og, after(meta, got), group)
            theirs = lax.ppermute(mine, "head", [(0, 1), (1, 0)])
        order = after(meta, got, mine)
    next_stats = shifted(after(stats, next_qd), -1)

    dq, grads, keep, finals, firsts = [], [], [], [], []
    far_grads = [jnp.zeros((2, BLK, width), jnp.bfloat16) for _ in far]
    order = after(meta, stats, theirs)
    for h in range(heads):
        got = backward(
            h, qd, pool, prev, rest, far, far_grads, bias, stats, order, group, slots
        )
        dq.append(got[0])
        grads.append(got[1])
        far_grads = got[2]
        order = after(order, got[0], next_stats)
        if h > 0:
            sums, order = add_up(h - 1, odds, evens, got[0], order)
            finals.append(sums)
        kept, first, odds, evens = project(
            h, mine, theirs, attn[h], firsts, order, group, parts
        )
        keep.append(kept)
        firsts = [first]
        odds = swap_groups(odds, 1)
        order = after(meta, first)
    neighbour = swap_groups(first, 1)
    far_back = [
        lax.ppermute(piece, "seq", summary_route(index + 2, True))
        for index, piece in enumerate(far_grads)
    ]
    own_grad = backward_next(grads, next_qd, pool, bias_next, next_stats, order)
    sums, order = add_up(heads - 1, odds, evens, (own_grad, finals[0]), meta)
    finals.append(sums)
    final = exchange(combine(dq, own_grad, far_back, order, group, rows))
    query_grad, key_grad, value_grad = unpack(final, meta, group)
    proj_grad = finish(keep, neighbour, finals, group)
    return (query_grad, key_grad, value_grad, proj_grad)


def solution(mesh):
    split = P(("dp", "seq"), "head")
    return jax.shard_map(
        functools.partial(local, mesh.shape["seq"]),
        mesh=mesh,
        in_specs=(split, split, split, P(("dp", "seq"), None), P(None, "head"), P()),
        out_specs=(split, split, split, split),
        check_vma=False,
    )
```

```python
import functools
import math

import jax
import jax.numpy as jnp
from jax import lax
from jax.experimental import pallas as pl
from jax.experimental.pallas import tpu as pltpu
from jax.sharding import PartitionSpec as P

HD = 128
BLK = 128
LOCAL = 8
STRIDE = 16
PAIR = 2 * BLK
SPAN = LOCAL + 1
SCALE = HD ** (-0.5)
SCALE2 = SCALE * math.log2(math.e)
MIB = 1024 * 1024

NT = (((1,), (1,)), ((), ()))
NN = (((1,), (0,)), ((), ()))
TN = (((0,), (0,)), ((), ()))
SMEM = pl.BlockSpec(memory_space=pltpu.SMEM)
VMEM = pl.BlockSpec(memory_space=pltpu.VMEM)
HBM = pl.BlockSpec(memory_space=pltpu.HBM)
ANY = pl.BlockSpec(memory_space=pl.ANY)


def shape(dims, dtype=jnp.bfloat16):
    return jax.ShapeDtypeStruct(dims, dtype)


def dot(a, b, dims):
    return lax.dot_general(a, b, dims, preferred_element_type=jnp.float32)


def params(size):
    return pltpu.CompilerParams(vmem_limit_bytes=size * MIB)


def cost(flops, size, exps=0):
    return pl.CostEstimate(flops=1, bytes_accessed=1, transcendentals=0)


def call(body, scalars, arrays, outs, scratch, estimate, name, size=16):
    return pl.pallas_call(
        body,
        out_shape=outs,
        in_specs=[SMEM] * len(scalars) + [VMEM] * len(arrays),
        out_specs=[VMEM] * len(outs),
        scratch_shapes=scratch,
        compiler_params=params(size),
        cost_estimate=estimate,
        name=name,
    )(*scalars, *arrays)


def one_head(refs, head):
    return [ref.at[(slice(None),) * (ref.ndim - 1) + (pl.ds(head * HD, HD),)] for ref in refs]


def split_refs(refs, counts):
    refs, taken = list(refs), []
    for count in counts:
        taken.append(refs[:count])
        refs = refs[count:]
    return taken, refs


def copied(*copies):
    for copy in copies:
        copy.start()
    for copy in copies:
        copy.wait()


def pack_kv(keys, values, meta, group, width):
    rows = keys.shape[0]

    def body(meta_ref, k_ref, v_ref, *refs):
        outs, sems = refs[:group], refs[group]
        me = meta_ref[0]
        copies = []
        for k in range(group):
            at = pl.ds(pl.multiple_of((me ^ k) * width, width), width)
            for which, source in enumerate((k_ref, v_ref)):
                copies.append(
                    pltpu.make_async_copy(source.at[:, at], outs[k].at[which], sems.at[k, which])
                )
        copied(*copies)

    return pl.pallas_call(
        body,
        out_shape=[shape((2, rows, width))] * group,
        in_specs=[SMEM, HBM, HBM],
        out_specs=[VMEM] * group,
        scratch_shapes=[pltpu.SemaphoreType.DMA((group, 2))],
        compiler_params=params(60),
        cost_estimate=cost(0, 4 * keys.size * 2),
        name="pack_kv",
    )(meta, keys, values)


def grads_packed(queries, out_grad, proj_weight, meta, group, width):
    rows, depth = out_grad.shape

    def body(meta_ref, q_ref, og_ref, w_ref, *refs):
        outs, (og, w, q_sems, w_sems, og_sem) = refs[:group], refs[group:]
        me = meta_ref[0]
        og_copy = pltpu.make_async_copy(og_ref, og, og_sem)
        og_copy.start()
        q_copies, w_copies = [], []
        for k in range(group):
            at = pl.ds(pl.multiple_of((me ^ k) * width, width), width)
            w_copies.append(pltpu.make_async_copy(w_ref.at[:, at], w.at[k], w_sems.at[k]))
            w_copies[k].start()
        for k in range(group):
            at = pl.ds(pl.multiple_of((me ^ k) * width, width), width)
            q_copies.append(pltpu.make_async_copy(q_ref.at[:, at], outs[k].at[0], q_sems.at[k]))
            q_copies[k].start()
        og_copy.wait()
        for k in range(group):
            w_copies[k].wait()
            outs[k][1] = dot(og[...], w[k], NN).astype(jnp.bfloat16)
        for k in range(group):
            q_copies[k].wait()

    return pl.pallas_call(
        body,
        out_shape=[shape((2, rows, width))] * group,
        in_specs=[SMEM, HBM, HBM, HBM],
        out_specs=[VMEM] * group,
        scratch_shapes=[
            pltpu.VMEM((rows, depth), jnp.bfloat16),
            pltpu.VMEM((group, depth, width), jnp.bfloat16),
            pltpu.SemaphoreType.DMA((group,)),
            pltpu.SemaphoreType.DMA((group,)),
            pltpu.SemaphoreType.DMA,
        ],
        compiler_params=params(60),
        cost_estimate=cost(2 * rows * depth * width * group, 12 * 1024 * 1024),
        name="attn_grad",
    )(meta, queries, out_grad, proj_weight)


def pack_out_grad(out_grad, meta, group, parts):
    rows, depth = out_grad.shape
    each = depth // (group * parts)
    half = parts // 2

    def body(meta_ref, og_ref, *refs):
        outs, (held, sems) = refs[:group], refs[group:]
        me, core = meta_ref[0], meta_ref[3]
        copies = []
        for k in range(group):
            for part in range(half):
                at = ((core * half + part) * group + (me ^ k)) * each
                at = pl.ds(pl.multiple_of(at, each), each)
                copies.append(
                    pltpu.make_async_copy(og_ref.at[:, at], held.at[k, part], sems.at[k, part])
                )
        copied(*copies)
        for k in range(group):
            for part in range(half):
                outs[k][part * each : (part + 1) * each, :] = held[k, part].T

    return pl.pallas_call(
        body,
        out_shape=[shape((half * each, rows))] * group,
        in_specs=[SMEM, HBM],
        out_specs=[VMEM] * group,
        scratch_shapes=[
            pltpu.VMEM((group, half, rows, each), jnp.bfloat16),
            pltpu.SemaphoreType.DMA((group, half)),
        ],
        compiler_params=params(16),
        cost_estimate=cost(0, 3 * out_grad.size),
        name="pack_out_grad",
    )(meta, out_grad)


def join_columns(pieces, meta, group):
    height, rows = pieces[0].shape

    def body(meta_ref, *refs):
        me = meta_ref[0]
        for k in range(group):
            at = pl.multiple_of((me ^ k) * rows, rows)
            refs[group][:, pl.ds(at, rows)] = refs[k][...]

    return call(
        body, (meta,), tuple(pieces), [shape((height, group * rows))], [],
        cost(0, 2 * 1024 * 1024), "join_columns",
    )[0]


def assemble_kv(pieces, meta, group):
    rows, width = pieces[0].shape[1:]

    def body(meta_ref, *refs):
        me = meta_ref[0]
        pool, rest, strided, sems = refs[group:]
        copies = []
        for k in range(group):
            at = pl.ds(pl.multiple_of((me ^ k) * rows, rows), rows)
            copies.append(pltpu.make_async_copy(refs[k], pool.at[:, at, :], sems.at[0, k]))
            if k > 0:
                copies.append(pltpu.make_async_copy(refs[k], rest.at[k - 1], sems.at[1, k]))
        copied(*copies)
        strided[...] = pool[:, pl.ds(pl.multiple_of(meta_ref[2] * BLK, BLK), BLK), :]

    return pl.pallas_call(
        body,
        out_shape=[
            shape((2, group * rows, width)),
            shape((group - 1, 2, rows, width)),
            shape((2, BLK, width)),
        ],
        in_specs=[SMEM] + [ANY] * group,
        out_specs=[VMEM] * 3,
        scratch_shapes=[pltpu.SemaphoreType.DMA((2, group))],
        compiler_params=params(16),
        cost_estimate=cost(0, 3 * MIB),
        name="assemble_kv",
    )(meta, *pieces)


def assemble(pieces, meta, group):
    lead, rows, width = pieces[0].shape

    def body(meta_ref, *refs):
        me = meta_ref[0]
        copies = []
        for k in range(group):
            at = pl.ds(pl.multiple_of((me ^ k) * rows, rows), rows)
            target = refs[group].at[:, at, :]
            copies.append(pltpu.make_async_copy(refs[k], target, refs[group + 1].at[k]))
        copied(*copies)

    return pl.pallas_call(
        body,
        out_shape=shape((lead, group * rows, width)),
        in_specs=[SMEM] + [ANY] * group,
        out_specs=VMEM,
        scratch_shapes=[pltpu.SemaphoreType.DMA((group,))],
        compiler_params=params(16),
        cost_estimate=cost(0, 2 * MIB),
        name="assemble",
    )(meta, *pieces)


def masks_of(layout, meta, parts, slots):
    width = layout.shape[1]
    pairs = LOCAL // 2

    def body(meta_ref, table, own_ref, next_ref):
        at_group = meta_ref[1]
        low_half = lax.broadcasted_iota(jnp.int32, (1, PAIR), 1) < BLK

        def bits_of(group_at, row):
            block = group_at * LOCAL + row
            base = block - row % 2 - (LOCAL - 1)
            at = jnp.minimum(block, table.shape[0] - 1)
            bits = jnp.int32(0)
            for c in range(width):
                entry = table[at, c]
                near = entry >= jnp.maximum(block - (LOCAL - 1), 0)
                place = jnp.where(near, entry - base, SPAN + jnp.maximum(entry, 0) // STRIDE)
                bit = jnp.left_shift(jnp.int32(1), place)
                bits = bits | jnp.where(entry >= 0, bit, 0)
            return jnp.where(group_at < parts, bits, 0)

        def row_of(first, second, place):
            one = jnp.where((jnp.right_shift(first, place) & 1) == 1, 0.0, -jnp.inf)
            two = jnp.where((jnp.right_shift(second, place) & 1) == 1, 0.0, -jnp.inf)
            return jnp.where(low_half, one, two).astype(jnp.float32)

        for t in range(pairs):
            first, second = bits_of(at_group, 2 * t), bits_of(at_group, 2 * t + 1)
            for place in range(SPAN + slots):
                own_ref[t, place : place + 1, :] = row_of(first, second, place)
            first, second = bits_of(at_group + 1, 2 * t), bits_of(at_group + 1, 2 * t + 1)
            for place in range(SPAN):
                next_ref[t, place : place + 1, :] = row_of(first, second, place)
            even = at_group % 2 == 0
            place = SPAN + at_group // 2
            first, second = jnp.where(even, first, 0), jnp.where(even, second, 0)
            next_ref[t, SPAN : SPAN + 1, :] = row_of(first, second, place)

    return call(
        body, (meta, layout), (),
        [
            shape((pairs, SPAN + slots, PAIR), jnp.float32),
            shape((pairs, SPAN + 1, PAIR), jnp.float32),
        ],
        [], cost(0, 128 * 1024), "masks",
    )


def fill_pools(meta_ref, own, prev, rest, far, k_pool, v_pool, group, rows, slots):
    me, at_group, offset = meta_ref[0], meta_ref[1], meta_ref[2]
    whole = group * rows
    k_pool[whole : 2 * whole, :] = own[0]
    v_pool[whole : 2 * whole, :] = own[1]
    for k in range(group):
        at = pl.multiple_of((me ^ k) * rows, rows)
        k_pool[pl.ds(at, rows), :] = prev[0] if k == 0 else rest[k - 1, 0]
        v_pool[pl.ds(at, rows), :] = prev[1] if k == 0 else rest[k - 1, 1]
    tail = jnp.zeros((slots * BLK, k_pool.shape[1]), k_pool.dtype)
    k_pool[2 * whole :, :] = tail
    v_pool[2 * whole :, :] = tail

    @pl.when(at_group % 2 == 1)
    def _():
        to = pl.multiple_of(2 * whole + (at_group // 2) * BLK, BLK)
        start = pl.multiple_of(offset * BLK, BLK)
        k_pool[pl.ds(to, BLK), :] = k_pool[pl.ds(start, BLK), :]
        v_pool[pl.ds(to, BLK), :] = v_pool[pl.ds(start, BLK), :]

    for index, ref in enumerate(far):
        distance = index + 2

        @pl.when((at_group >= distance) & ((at_group - distance) % 2 == 0))
        def _():
            to = pl.multiple_of(2 * whole + ((at_group - distance) // 2) * BLK, BLK)
            k_pool[pl.ds(to, BLK), :] = ref[0]
            v_pool[pl.ds(to, BLK), :] = ref[1]


def causal_masks():
    key_at = lax.broadcasted_iota(jnp.int32, (BLK, PAIR), 0)
    query_at = lax.broadcasted_iota(jnp.int32, (BLK, PAIR), 1)
    first = (key_at <= query_at) | (query_at >= BLK)
    second = key_at <= query_at - BLK
    return first, second


def masked_scores(keys, query, bias, masks):
    raw = dot(keys, query, NT) * SCALE2
    tiles = []
    for j in range(keys.shape[0] // BLK):
        tile = raw[j * BLK : (j + 1) * BLK] + bias[j]
        if masks is not None and j in (LOCAL - 1, LOCAL):
            tile = jnp.where(masks[j - LOCAL + 1], tile, -jnp.inf)
        tiles.append(tile)
    return jnp.concatenate(tiles, axis=0)


def bias_rows(bias_ref, t, picked):
    return [bias_ref[t, j : j + 1, :] for j in picked]


def forward(head, qd, own, prev, rest, far, bias, stats, meta, group, slots):
    whole = qd.shape[1]
    rows = whole // group
    pairs = whole // PAIR
    counts = (4, len(far))

    def body(meta_ref, bias_ref, before_ref, *refs):
        (around, far_refs), refs = split_refs(refs, counts)
        qd_ref, *around = one_head(around, head)
        far_refs = one_head(far_refs, head)
        out_ref, stats_ref, k_pool, v_pool = refs
        fill_pools(meta_ref, *around, far_refs, k_pool, v_pool, group, rows, slots)
        stats_ref[...] = before_ref[...]
        masks = causal_masks()
        for t in range(pairs):
            here = slice(t * PAIR, (t + 1) * PAIR)
            window = slice(t * PAIR + BLK, t * PAIR + BLK + SPAN * BLK)
            keys = jnp.concatenate([k_pool[window, :], k_pool[2 * whole :, :]], axis=0)
            vals = jnp.concatenate([v_pool[window, :], v_pool[2 * whole :, :]], axis=0)
            s = masked_scores(keys, qd_ref[0, here, :], bias_rows(bias_ref, t, range(SPAN + slots)), masks)
            top = jnp.max(s, axis=0, keepdims=True)
            e = jnp.exp2(s - top)
            total = jnp.sum(e, axis=0, keepdims=True)
            low = (e * (1.0 / total)).astype(jnp.bfloat16)
            out = dot(low, vals, TN).astype(jnp.bfloat16)
            out_ref[here, :] = out
            product = out.astype(jnp.float32) * qd_ref[1, here, :].astype(jnp.float32)
            stats_ref[t, 2 * head : 2 * head + 1, :] = top + jnp.log2(total)
            stats_ref[t, 2 * head + 1 : 2 * head + 2, :] = jnp.sum(product.T, axis=0, keepdims=True)

    span = (SPAN + slots) * BLK
    return call(
        body, (meta,), (bias, stats, qd, own, prev, rest, *far),
        [shape((whole, HD)), shape(stats.shape, jnp.float32)],
        [pltpu.VMEM((2 * whole + slots * BLK, HD), jnp.bfloat16)] * 2,
        cost(4 * whole * span * HD * 2, 3 * 1024 * 1024, whole * span),
        f"attention_{head}", 24,
    )


def backward(head, qd, own, prev, rest, far, before, bias, stats, meta, group, slots):
    whole, width = qd.shape[1:]
    rows = whole // group
    pairs = whole // PAIR
    counts = (4, len(far), len(before))
    everything = 2 * whole + slots * BLK

    def body(meta_ref, bias_ref, stats_ref, *refs):
        (around, far_refs, before_refs), refs = split_refs(refs, counts)
        qd_ref, *around = one_head(around, head)
        far_refs = one_head(far_refs, head)
        ((dq_ref, grad_ref), far_outs), refs = split_refs(refs, (2, len(far)))
        k_pool, v_pool, far_sum = refs
        at_group = meta_ref[1]
        fill_pools(meta_ref, *around, far_refs, k_pool, v_pool, group, rows, slots)
        masks = causal_masks()
        grad_ref[...] = jnp.zeros_like(grad_ref)
        far_sum[...] = jnp.zeros_like(far_sum)
        for t in range(pairs):
            here = slice(t * PAIR, (t + 1) * PAIR)
            window = slice(t * PAIR + BLK, t * PAIR + BLK + SPAN * BLK)
            others = max(whole - (t * PAIR + BLK), 0)
            end = SPAN * BLK
            mine = slice(t * PAIR + BLK + others - whole, t * PAIR + BLK + end - whole)
            keys = jnp.concatenate([k_pool[window, :], k_pool[2 * whole :, :]], axis=0)
            vals = jnp.concatenate([v_pool[window, :], v_pool[2 * whole :, :]], axis=0)
            query, grad = qd_ref[0, here, :], qd_ref[1, here, :]
            s = masked_scores(keys, query, bias_rows(bias_ref, t, range(SPAN + slots)), masks)
            probs = jnp.exp2(s - stats_ref[t, 2 * head : 2 * head + 1, :])
            delta = stats_ref[t, 2 * head + 1 : 2 * head + 2, :]
            ds = (probs * (dot(vals, grad, NT) - delta)).astype(jnp.bfloat16)
            low = probs.astype(jnp.bfloat16)
            dq_ref[here, :] = (dot(ds, keys, TN) * SCALE).astype(jnp.bfloat16)
            grad_ref[0, mine, :] += dot(ds[others:end], query, NN)
            grad_ref[1, mine, :] += dot(low[others:end], grad, NN)
            far_sum[0] += dot(ds[end:], query, NN)
            far_sum[1] += dot(low[end:], grad, NN)
        for index, ref in enumerate(far_outs):
            slot = jnp.maximum(at_group - index - 2, 0) // 2
            start = pl.multiple_of(slot * BLK, BLK)
            ref[...] = before_refs[index][...]
            lanes = slice(head * HD, (head + 1) * HD)
            ref[0, :, lanes] = (far_sum[0, pl.ds(start, BLK), :] * SCALE).astype(jnp.bfloat16)
            ref[1, :, lanes] = far_sum[1, pl.ds(start, BLK), :].astype(jnp.bfloat16)

    span = (SPAN + slots) * BLK
    outs = call(
        body, (meta,), (bias, stats, qd, own, prev, rest, *far, *before),
        [shape((whole, HD)), shape((2, whole, HD), jnp.float32)]
        + [shape((2, BLK, width))] * len(far),
        [
            pltpu.VMEM((everything, HD), jnp.bfloat16),
            pltpu.VMEM((everything, HD), jnp.bfloat16),
            pltpu.VMEM((2, slots * BLK, HD), jnp.float32),
        ],
        cost(8 * whole * span * HD * 2, 4 * 1024 * 1024, whole * span),
        f"attention_back_{head}", 24,
    )
    return outs[0], outs[1], outs[2:]


def backward_next(grads, qd, own, bias, stats, meta):
    whole, width = qd.shape[1:]
    heads = width // HD
    pairs = whole // PAIR

    def body(meta_ref, bias_ref, stats_ref, *refs):
        (grad_refs, (qd_ref, own_ref, out)), refs = split_refs(refs, (heads, 3))
        strided = pl.ds(pl.multiple_of(meta_ref[2] * BLK, BLK), BLK)
        for h in range(heads):
            lanes = slice(h * HD, (h + 1) * HD)
            out[0, :, lanes] = grad_refs[h][0]
            out[1, :, lanes] = grad_refs[h][1]
            for t in range(pairs):
                here = slice(t * PAIR, (t + 1) * PAIR)
                window = slice(t * PAIR + BLK, whole)
                near = (whole - BLK) // BLK - t * (PAIR // BLK)
                keys = jnp.concatenate([own_ref[0, window, lanes], own_ref[0, strided, lanes]], axis=0)
                vals = jnp.concatenate([own_ref[1, window, lanes], own_ref[1, strided, lanes]], axis=0)
                query, grad = qd_ref[0, here, lanes], qd_ref[1, here, lanes]
                rows_here = bias_rows(bias_ref, t, list(range(near)) + [SPAN])
                s = masked_scores(keys, query, rows_here, None)
                probs = jnp.exp2(s - stats_ref[t, 2 * h : 2 * h + 1, :])
                delta = stats_ref[t, 2 * h + 1 : 2 * h + 2, :]
                ds = (probs * (dot(vals, grad, NT) - delta)).astype(jnp.bfloat16)
                dk = dot(ds, query, NN)
                dv = dot(probs.astype(jnp.bfloat16), grad, NN)
                out[0, window, lanes] += dk[: near * BLK]
                out[1, window, lanes] += dv[: near * BLK]
                out[0, strided, lanes] += dk[near * BLK :]
                out[1, strided, lanes] += dv[near * BLK :]
        out[0] = out[0] * SCALE

    return call(
        body, (meta,), (bias, stats, *grads, qd, own),
        [shape((2, whole, width), jnp.float32)], [],
        cost(8 * whole * 5 * BLK * width, 7 * 1024 * 1024, whole * 5 * BLK * heads),
        "attention_back_next", 24,
    )[0]


def combine(dq, own, far, meta, group, rows):
    whole, width = own.shape[1:]

    def body(meta_ref, own_ref, *refs):
        (dq_refs, far_refs, outs, (acc,)), refs = split_refs(refs, (len(dq), len(far), group, 1))
        me, offset = meta_ref[0], meta_ref[2]
        acc[...] = own_ref[...]
        at = pl.multiple_of(offset * BLK, BLK)
        for ref in far_refs:
            acc[:, pl.ds(at, BLK), :] += ref[...].astype(jnp.float32)
        for k in range(group):
            here = pl.ds(pl.multiple_of((me ^ k) * rows, rows), rows)
            for h in range(len(dq)):
                outs[k][0, :, h * HD : (h + 1) * HD] = dq_refs[h][here, :]
            outs[k][1] = acc[0, here, :].astype(jnp.bfloat16)
            outs[k][2] = acc[1, here, :].astype(jnp.bfloat16)

    return call(
        body, (meta,), (own, *dq, *far), [shape((3, rows, width))] * group,
        [pltpu.VMEM((2, whole, width), jnp.float32)],
        cost(0, 4 * 1024 * 1024), "combine",
    )


def project(head, mine, theirs, attn, before, meta, group, parts):
    height, whole = mine.shape
    each = 2 * height // parts
    full = group * HD
    more = parts // 2 - 1

    def body(meta_ref, mine_ref, theirs_ref, *refs):
        (attn_refs, before_refs, outs), refs = split_refs(refs, (group, len(before), 6))
        keep, first, odds, evens, pool, total = outs
        for ref in before_refs:
            first[:head] = ref[...]
        me, at_group, core = meta_ref[0], meta_ref[1], meta_ref[3]
        for k in range(group):
            at = pl.multiple_of((me ^ k) * HD, HD)
            pool[:, pl.ds(at, HD)] = attn_refs[k][...]
        upper = pl.ds(pl.multiple_of(core * height, height), height)
        lower = pl.ds(pl.multiple_of((1 - core) * height, height), height)
        total[upper, :] = dot(mine_ref[...], pool[...], NN)
        total[lower, :] = dot(theirs_ref[...], pool[...], NN)
        for m in range(parts):
            part = total[pl.ds(pl.multiple_of((at_group ^ m) * each, each), each), :]
            if m == 0:
                keep[...] = part
            elif m == 1:
                first[head] = part.astype(jnp.bfloat16)
            elif m % 2 == 1:
                odds[m // 2 - 1] = part.astype(jnp.bfloat16)
            else:
                evens[m // 2 - 1] = part

    return call(
        body, (meta,), (mine, theirs, *attn, *before),
        [
            shape((each, full), jnp.float32),
            shape((head + 1, each, full)),
            shape((more, each, full)),
            shape((more, each, full), jnp.float32),
        ],
        [pltpu.VMEM((whole, full), jnp.bfloat16), pltpu.VMEM((2 * height, full), jnp.float32)],
        cost(4 * height * whole * full, 6 * 1024 * 1024), f"project_{head}",
    )


def halve(head, evens, arrived):
    count, each, full = evens.shape
    more = (count - 1) // 2

    def body(evens_ref, arrived_ref, first, *rest):
        for m in range(1, count + 1):
            summed = evens_ref[m - 1] + arrived_ref[m - 1].astype(jnp.float32)
            if m == 1:
                first[...] = summed.astype(jnp.bfloat16)
            elif m % 2 == 1:
                rest[0][m // 2 - 1] = summed.astype(jnp.bfloat16)
            else:
                rest[1][m // 2 - 1] = summed

    others = [shape((more, each, full)), shape((more, each, full), jnp.float32)]
    return call(
        body, (), (evens, arrived), [shape((each, full))] + (others if more else []), [],
        cost(0, 3 * 1024 * 1024), f"halve_{head}",
    )


def finish(keep, neighbour, arrived, group):
    heads = len(keep)
    count = len(arrived[0])
    each = keep[0].shape[0]

    def body(*refs):
        (keep_refs, arrived_refs, (first, out)), refs = split_refs(refs, (heads, heads * count, 2))
        for h in range(heads):
            total = keep_refs[h][...] + first[h].astype(jnp.float32)
            for ref in arrived_refs[h * count : (h + 1) * count]:
                total = total + ref[...].astype(jnp.float32)
            for j in range(group):
                at = (j * heads + h) * HD
                out[:, at : at + HD] = total[:, j * HD : (j + 1) * HD]

    flat = [piece for pieces in arrived for piece in pieces]
    return call(
        body, (), (*keep, *flat, neighbour),
        [shape((each, group * heads * HD), jnp.float32)], [],
        cost(0, 3 * 1024 * 1024), "finish",
    )[0]


def unpack(pieces, meta, group):
    rows, width = pieces[0].shape[1:]

    def body(meta_ref, *refs):
        me = meta_ref[0]
        outs, sems = refs[group:-1], refs[-1]
        copies = []
        for k in range(group):
            at = pl.ds(pl.multiple_of((me ^ k) * width, width), width)
            for which in range(3):
                target = outs[which].at[:, at]
                copies.append(
                    pltpu.make_async_copy(refs[k].at[which], target, sems.at[k, which])
                )
        copied(*copies)

    return pl.pallas_call(
        body,
        out_shape=[shape((rows, group * width))] * 3,
        in_specs=[SMEM] + [ANY] * group,
        out_specs=[ANY] * 3,
        scratch_shapes=[pltpu.SemaphoreType.DMA((group, 3))],
        compiler_params=params(16),
        cost_estimate=cost(0, 3 * MIB),
        name="unpack",
    )(meta, *pieces)


def after(value, *others):
    return lax.optimization_barrier((value, *others))[0]


def local(devices, queries, keys, values, out_grad, proj_weight, layout):
    rows, columns = queries.shape
    group = LOCAL * BLK // rows
    parts = devices // group
    width = columns // group
    heads = width // HD
    blocks = layout.shape[0]
    slots = blocks // STRIDE
    position = lax.axis_index("seq")
    me, at_group = position % group, position // group
    core = lax.axis_index("head")
    offset = layout[blocks - 1, 0] % STRIDE
    place = jnp.stack([me, at_group]).astype(jnp.int32)
    meta = jnp.stack([me, at_group, offset, core]).astype(jnp.int32)

    def swap(piece, k):
        route = [(i, (i // group) * group + ((i % group) ^ k)) for i in range(devices)]
        return lax.ppermute(piece, "seq", route)

    def shifted(piece, distance):
        route = [
            (i, i + distance * group)
            for i in range(devices)
            if 0 <= i + distance * group < devices
        ]
        return lax.ppermute(piece, "seq", route)

    def swap_groups(piece, bit):
        route = [(i, ((i // group) ^ bit) * group + i % group) for i in range(devices)]
        return lax.ppermute(piece, "seq", route)

    def summary_route(distance, back):
        route = [
            (i, i + distance * group)
            for i in range(devices - distance * group)
            if (i // group) % 2 == 0
        ]
        return [(b, a) for a, b in route] if back else route

    def exchange(pieces):
        return [pieces[0]] + [swap(pieces[k], k) for k in range(1, group)]

    def add_up(head, odds, evens, before, token):
        arrivals, bit = [], 2
        odds = after(odds, *jax.tree.leaves(before))
        while True:
            first, *more = halve(head, evens, odds)
            token = after(token, first)
            arrivals.append(swap_groups(first, bit))
            if not more:
                return arrivals, token
            odds, evens = swap_groups(more[0], bit), more[1]
            bit *= 2

    kv = pack_kv(keys, values, place, group, width)
    own_kv = exchange(kv)
    prev = shifted(kv[0], 1)
    early = after(place, own_kv[1])
    qd_cut = grads_packed(queries, out_grad, proj_weight, early, group, width)
    pool, others, strided = assemble_kv(own_kv, after(meta, prev, qd_cut[0]), group)
    rest = shifted(others, 1)
    far = [
        lax.ppermute(strided, "seq", summary_route(distance, False))
        for distance in range(2, parts)
    ]
    qd_pieces = exchange(qd_cut)
    bias, bias_next = masks_of(layout, after(meta, strided), parts, slots)
    qd = assemble(qd_pieces, after(meta, bias), group)
    next_qd = shifted(qd, -1)
    og = exchange(pack_out_grad(out_grad, after(meta, qd, *far), group, parts))

    stats = jnp.zeros((LOCAL // 2, 2 * heads, PAIR), jnp.float32)
    order = after(meta, og[0])
    attn = []
    for h in range(heads):
        got, stats = forward(h, qd, pool, prev, rest, far, bias, stats, order, group, slots)
        attn.append([got] + [swap(got, k) for k in range(1, group)])
        if h == 0:
            mine = join_columns(og, after(meta, got), group)
            theirs = lax.ppermute(mine, "head", [(0, 1), (1, 0)])
        order = after(meta, got, mine)
    next_stats = shifted(after(stats, next_qd), -1)

    dq, grads, keep, finals, firsts = [], [], [], [], []
    far_grads = [jnp.zeros((2, BLK, width), jnp.bfloat16) for _ in far]
    order = after(meta, stats, theirs)
    for h in range(heads):
        got = backward(
            h, qd, pool, prev, rest, far, far_grads, bias, stats, order, group, slots
        )
        dq.append(got[0])
        grads.append(got[1])
        far_grads = got[2]
        order = after(order, got[0], next_stats)
        if h > 0:
            sums, order = add_up(h - 1, odds, evens, got[0], order)
            finals.append(sums)
        kept, first, odds, evens = project(
            h, mine, theirs, attn[h], firsts, order, group, parts
        )
        keep.append(kept)
        firsts = [first]
        odds = swap_groups(odds, 1)
        order = after(meta, first)
    neighbour = swap_groups(first, 1)
    far_back = [
        lax.ppermute(piece, "seq", summary_route(index + 2, True))
        for index, piece in enumerate(far_grads)
    ]
    order = after(order, finals[0])
    own_grad = backward_next(grads, next_qd, pool, bias_next, next_stats, order)
    sums, order = add_up(heads - 1, odds, evens, (own_grad, finals[0]), meta)
    finals.append(sums)
    final = exchange(combine(dq, own_grad, far_back, order, group, rows))
    query_grad, key_grad, value_grad = unpack(final, meta, group)
    proj_grad = finish(keep, neighbour, finals, group)
    return (query_grad, key_grad, value_grad, proj_grad)


def solution(mesh):
    split = P(("dp", "seq"), "head")
    return jax.shard_map(
        functools.partial(local, mesh.shape["seq"]),
        mesh=mesh,
        in_specs=(split, split, split, P(("dp", "seq"), None), P(None, "head"), P()),
        out_specs=(split, split, split, split),
        check_vma=False,
    )
```

```python
import functools
import math

import jax
import jax.numpy as jnp
from jax import lax
from jax.experimental import pallas as pl
from jax.experimental.pallas import tpu as pltpu
from jax.sharding import PartitionSpec as P

HD = 128
BLK = 128
LOCAL = 8
STRIDE = 16
PAIR = 2 * BLK
SPAN = LOCAL + 1
SCALE = HD ** (-0.5)
SCALE2 = SCALE * math.log2(math.e)
MIB = 1024 * 1024

NT = (((1,), (1,)), ((), ()))
NN = (((1,), (0,)), ((), ()))
TN = (((0,), (0,)), ((), ()))
SMEM = pl.BlockSpec(memory_space=pltpu.SMEM)
VMEM = pl.BlockSpec(memory_space=pltpu.VMEM)
HBM = pl.BlockSpec(memory_space=pltpu.HBM)
ANY = pl.BlockSpec(memory_space=pl.ANY)


def shape(dims, dtype=jnp.bfloat16):
    return jax.ShapeDtypeStruct(dims, dtype)


def dot(a, b, dims):
    return lax.dot_general(a, b, dims, preferred_element_type=jnp.float32)


def params(size):
    return pltpu.CompilerParams(vmem_limit_bytes=size * MIB)


def cost(flops, size, exps=0):
    return pl.CostEstimate(flops=1, bytes_accessed=1, transcendentals=0)


def call(body, scalars, arrays, outs, scratch, estimate, name, size=16):
    return pl.pallas_call(
        body,
        out_shape=outs,
        in_specs=[SMEM] * len(scalars) + [VMEM] * len(arrays),
        out_specs=[VMEM] * len(outs),
        scratch_shapes=scratch,
        compiler_params=params(size),
        cost_estimate=estimate,
        name=name,
    )(*scalars, *arrays)


def one_head(refs, head):
    return [ref.at[(slice(None),) * (ref.ndim - 1) + (pl.ds(head * HD, HD),)] for ref in refs]


def split_refs(refs, counts):
    refs, taken = list(refs), []
    for count in counts:
        taken.append(refs[:count])
        refs = refs[count:]
    return taken, refs


def copied(*copies):
    for copy in copies:
        copy.start()
    for copy in copies:
        copy.wait()


def pack_kv(keys, values, meta, group, width):
    rows = keys.shape[0]

    def body(meta_ref, k_ref, v_ref, *refs):
        outs, (k_in, v_in, sems) = refs[:group], refs[group:]
        me = meta_ref[0]
        copied(
            pltpu.make_async_copy(k_ref, k_in, sems.at[0]),
            pltpu.make_async_copy(v_ref, v_in, sems.at[1]),
        )
        for k in range(group):
            at = pl.ds(pl.multiple_of((me ^ k) * width, width), width)
            outs[k][0] = k_in[:, at]
            outs[k][1] = v_in[:, at]

    return pl.pallas_call(
        body,
        out_shape=[shape((2, rows, width))] * group,
        in_specs=[SMEM, HBM, HBM],
        out_specs=[VMEM] * group,
        scratch_shapes=[
            pltpu.VMEM(keys.shape, jnp.bfloat16),
            pltpu.VMEM(keys.shape, jnp.bfloat16),
            pltpu.SemaphoreType.DMA((2,)),
        ],
        compiler_params=params(60),
        cost_estimate=cost(0, 4 * keys.size * 2),
        name="pack_kv",
    )(meta, keys, values)


def grads_packed(queries, out_grad, proj_weight, meta, group, parts):
    rows, depth = out_grad.shape
    columns = queries.shape[1]
    width = columns // group
    each = depth // (group * parts)
    half = parts // 2
    chunks = 8
    step = depth // chunks
    assert rows == width

    def body(meta_ref, q_ref, og_ref, w_ref, *refs):
        outs, (q, og, w, total, sems, w_sems) = refs[:group], refs[group:]
        me, core = meta_ref[0], meta_ref[2]
        og_copy = pltpu.make_async_copy(og_ref, og, sems.at[0])
        q_copy = pltpu.make_async_copy(q_ref, q, sems.at[1])
        og_copy.start()
        w_copies = []
        for c in range(chunks):
            at = slice(c * step, (c + 1) * step)
            w_copies.append(pltpu.make_async_copy(w_ref.at[at, :], w.at[at, :], w_sems.at[c]))
            w_copies[c].start()
        q_copy.start()
        og_copy.wait()
        for k in range(group):
            for part in range(half):
                at = ((core * half + part) * group + (me ^ k)) * each
                at = pl.multiple_of(at, each)
                to = 2 * rows + part * each
                outs[k][to : to + each, :] = og[:, pl.ds(at, each)].T
        for c in range(chunks):
            at = slice(c * step, (c + 1) * step)
            w_copies[c].wait()
            got = dot(og[:, at], w[at, :], NN)
            if c == 0:
                total[...] = got
            else:
                total[...] += got
        q_copy.wait()
        for k in range(group):
            at = pl.ds(pl.multiple_of((me ^ k) * width, width), width)
            outs[k][:rows, :] = q[:, at]
            outs[k][rows : 2 * rows, :] = total[:, at].astype(jnp.bfloat16)

    return pl.pallas_call(
        body,
        out_shape=[shape((2 * rows + half * each, rows))] * group,
        in_specs=[SMEM, HBM, HBM, HBM],
        out_specs=[VMEM] * group,
        scratch_shapes=[
            pltpu.VMEM((rows, columns), jnp.bfloat16),
            pltpu.VMEM((rows, depth), jnp.bfloat16),
            pltpu.VMEM((depth, columns), jnp.bfloat16),
            pltpu.VMEM((rows, columns), jnp.float32),
            pltpu.SemaphoreType.DMA((2,)),
            pltpu.SemaphoreType.DMA((chunks,)),
        ],
        compiler_params=params(60),
        cost_estimate=cost(2 * rows * depth * columns, 12 * 1024 * 1024),
        name="attn_grad",
    )(meta, queries, out_grad, proj_weight)


def assemble_kv(pieces, meta, group):
    rows, width = pieces[0].shape[1:]

    def body(meta_ref, *refs):
        me = meta_ref[0]
        pool, strided, sems = refs[group:]
        copies = []
        for k in range(group):
            at = pl.ds(pl.multiple_of((me ^ k) * rows, rows), rows)
            copies.append(pltpu.make_async_copy(refs[k], pool.at[:, at, :], sems.at[k]))
        copied(*copies)
        strided[...] = pool[:, pl.ds(pl.multiple_of(meta_ref[2] * BLK, BLK), BLK), :]

    return pl.pallas_call(
        body,
        out_shape=[
            shape((2, group * rows, width)),
            shape((2, BLK, width)),
        ],
        in_specs=[SMEM] + [ANY] * group,
        out_specs=[VMEM] * 2,
        scratch_shapes=[pltpu.SemaphoreType.DMA((group,))],
        compiler_params=params(16),
        cost_estimate=cost(0, 3 * MIB),
        name="assemble_kv",
    )(meta, *pieces)


def assemble(pieces, meta, group):
    rows = pieces[0].shape[1]
    height = pieces[0].shape[0] - 2 * rows

    def body(meta_ref, *refs):
        me = meta_ref[0]
        qd, og = refs[group:]
        for k in range(group):
            at = pl.ds(pl.multiple_of((me ^ k) * rows, rows), rows)
            qd[0, at, :] = refs[k][:rows, :]
            qd[1, at, :] = refs[k][rows : 2 * rows, :]
            og[:, at] = refs[k][2 * rows :, :]

    return call(
        body, (meta,), tuple(pieces),
        [shape((2, group * rows, rows)), shape((height, group * rows))], [],
        cost(0, 4 * MIB), "assemble",
    )


def masks_of(layout, meta, parts, slots):
    width = layout.shape[1]
    pairs = LOCAL // 2

    def body(meta_ref, table, own_ref, next_ref):
        at_group = meta_ref[1]
        low_half = lax.broadcasted_iota(jnp.int32, (1, PAIR), 1) < BLK

        def bits_of(group_at, row):
            block = group_at * LOCAL + row
            base = block - row % 2 - (LOCAL - 1)
            at = jnp.minimum(block, table.shape[0] - 1)
            bits = jnp.int32(0)
            for c in range(width):
                entry = table[at, c]
                near = entry >= jnp.maximum(block - (LOCAL - 1), 0)
                place = jnp.where(near, entry - base, SPAN + jnp.maximum(entry, 0) // STRIDE)
                bit = jnp.left_shift(jnp.int32(1), place)
                bits = bits | jnp.where(entry >= 0, bit, 0)
            return jnp.where(group_at < parts, bits, 0)

        def row_of(first, second, place):
            one = jnp.where((jnp.right_shift(first, place) & 1) == 1, 0.0, -jnp.inf)
            two = jnp.where((jnp.right_shift(second, place) & 1) == 1, 0.0, -jnp.inf)
            return jnp.where(low_half, one, two).astype(jnp.float32)

        for t in range(pairs):
            first, second = bits_of(at_group, 2 * t), bits_of(at_group, 2 * t + 1)
            for place in range(SPAN + slots):
                own_ref[t, place : place + 1, :] = row_of(first, second, place)
            first, second = bits_of(at_group + 1, 2 * t), bits_of(at_group + 1, 2 * t + 1)
            for place in range(SPAN):
                next_ref[t, place : place + 1, :] = row_of(first, second, place)
            even = at_group % 2 == 0
            place = SPAN + at_group // 2
            first, second = jnp.where(even, first, 0), jnp.where(even, second, 0)
            next_ref[t, SPAN : SPAN + 1, :] = row_of(first, second, place)

    return call(
        body, (meta, layout), (),
        [
            shape((pairs, SPAN + slots, PAIR), jnp.float32),
            shape((pairs, SPAN + 1, PAIR), jnp.float32),
        ],
        [], cost(0, 128 * 1024), "masks",
    )


def fill_pools(meta_ref, own, prev, far, k_pool, v_pool, slots):
    at_group, offset = meta_ref[1], meta_ref[2]
    whole = own.shape[1]
    k_pool[:whole, :] = prev[0]
    v_pool[:whole, :] = prev[1]
    k_pool[whole : 2 * whole, :] = own[0]
    v_pool[whole : 2 * whole, :] = own[1]
    tail = jnp.zeros((slots * BLK, k_pool.shape[1]), k_pool.dtype)
    k_pool[2 * whole :, :] = tail
    v_pool[2 * whole :, :] = tail

    @pl.when(at_group % 2 == 1)
    def _():
        to = pl.multiple_of(2 * whole + (at_group // 2) * BLK, BLK)
        start = pl.multiple_of(offset * BLK, BLK)
        k_pool[pl.ds(to, BLK), :] = k_pool[pl.ds(start, BLK), :]
        v_pool[pl.ds(to, BLK), :] = v_pool[pl.ds(start, BLK), :]

    for index, ref in enumerate(far):
        distance = index + 2

        @pl.when((at_group >= distance) & ((at_group - distance) % 2 == 0))
        def _():
            to = pl.multiple_of(2 * whole + ((at_group - distance) // 2) * BLK, BLK)
            k_pool[pl.ds(to, BLK), :] = ref[0]
            v_pool[pl.ds(to, BLK), :] = ref[1]


def causal_masks():
    key_at = lax.broadcasted_iota(jnp.int32, (BLK, PAIR), 0)
    query_at = lax.broadcasted_iota(jnp.int32, (BLK, PAIR), 1)
    first = (key_at <= query_at) | (query_at >= BLK)
    second = key_at <= query_at - BLK
    return first, second


def masked_scores(keys, query, bias, masks):
    raw = dot(keys, query, NT) * SCALE2
    tiles = []
    for j in range(keys.shape[0] // BLK):
        tile = raw[j * BLK : (j + 1) * BLK] + bias[j]
        if masks is not None and j in (LOCAL - 1, LOCAL):
            tile = jnp.where(masks[j - LOCAL + 1], tile, -jnp.inf)
        tiles.append(tile)
    return jnp.concatenate(tiles, axis=0)


def bias_rows(bias_ref, t, picked):
    return [bias_ref[t, j : j + 1, :] for j in picked]


def forward(head, qd, own, prev, far, bias, stats, meta, group, slots):
    whole = qd.shape[1]
    pairs = whole // PAIR
    counts = (3, len(far))

    def body(meta_ref, bias_ref, before_ref, *refs):
        (around, far_refs), refs = split_refs(refs, counts)
        qd_ref, *around = one_head(around, head)
        far_refs = one_head(far_refs, head)
        out_ref, stats_ref, k_pool, v_pool = refs
        fill_pools(meta_ref, *around, far_refs, k_pool, v_pool, slots)
        stats_ref[...] = before_ref[...]
        masks = causal_masks()
        for t in range(pairs):
            here = slice(t * PAIR, (t + 1) * PAIR)
            window = slice(t * PAIR + BLK, t * PAIR + BLK + SPAN * BLK)
            keys = jnp.concatenate([k_pool[window, :], k_pool[2 * whole :, :]], axis=0)
            vals = jnp.concatenate([v_pool[window, :], v_pool[2 * whole :, :]], axis=0)
            s = masked_scores(keys, qd_ref[0, here, :], bias_rows(bias_ref, t, range(SPAN + slots)), masks)
            top = jnp.max(s, axis=0, keepdims=True)
            e = jnp.exp2(s - top)
            total = jnp.sum(e, axis=0, keepdims=True)
            low = (e * (1.0 / total)).astype(jnp.bfloat16)
            out = dot(low, vals, TN).astype(jnp.bfloat16)
            out_ref[here, :] = out
            product = out.astype(jnp.float32) * qd_ref[1, here, :].astype(jnp.float32)
            stats_ref[t, 2 * head : 2 * head + 1, :] = top + jnp.log2(total)
            stats_ref[t, 2 * head + 1 : 2 * head + 2, :] = jnp.sum(product.T, axis=0, keepdims=True)

    span = (SPAN + slots) * BLK
    return call(
        body, (meta,), (bias, stats, qd, own, prev, *far),
        [shape((whole, HD)), shape(stats.shape, jnp.float32)],
        [pltpu.VMEM((2 * whole + slots * BLK, HD), jnp.bfloat16)] * 2,
        cost(4 * whole * span * HD * 2, 3 * 1024 * 1024, whole * span),
        f"attention_{head}", 24,
    )


def backward(head, qd, own, prev, far, before, bias, stats, meta, group, slots):
    whole, width = qd.shape[1:]
    pairs = whole // PAIR
    counts = (3, len(far), len(before))
    everything = 2 * whole + slots * BLK

    def body(meta_ref, bias_ref, stats_ref, *refs):
        (around, far_refs, before_refs), refs = split_refs(refs, counts)
        qd_ref, *around = one_head(around, head)
        far_refs = one_head(far_refs, head)
        ((dq_ref, grad_ref), far_outs), refs = split_refs(refs, (2, len(far)))
        k_pool, v_pool, far_sum = refs
        at_group = meta_ref[1]
        fill_pools(meta_ref, *around, far_refs, k_pool, v_pool, slots)
        masks = causal_masks()
        grad_ref[...] = jnp.zeros_like(grad_ref)
        far_sum[...] = jnp.zeros_like(far_sum)
        for t in range(pairs):
            here = slice(t * PAIR, (t + 1) * PAIR)
            window = slice(t * PAIR + BLK, t * PAIR + BLK + SPAN * BLK)
            others = max(whole - (t * PAIR + BLK), 0)
            end = SPAN * BLK
            mine = slice(t * PAIR + BLK + others - whole, t * PAIR + BLK + end - whole)
            keys = jnp.concatenate([k_pool[window, :], k_pool[2 * whole :, :]], axis=0)
            vals = jnp.concatenate([v_pool[window, :], v_pool[2 * whole :, :]], axis=0)
            query, grad = qd_ref[0, here, :], qd_ref[1, here, :]
            s = masked_scores(keys, query, bias_rows(bias_ref, t, range(SPAN + slots)), masks)
            probs = jnp.exp2(s - stats_ref[t, 2 * head : 2 * head + 1, :])
            delta = stats_ref[t, 2 * head + 1 : 2 * head + 2, :]
            ds = (probs * (dot(vals, grad, NT) - delta)).astype(jnp.bfloat16)
            low = probs.astype(jnp.bfloat16)
            dq_ref[here, :] = (dot(ds, keys, TN) * SCALE).astype(jnp.bfloat16)
            grad_ref[0, mine, :] += dot(ds[others:end], query, NN)
            grad_ref[1, mine, :] += dot(low[others:end], grad, NN)
            far_sum[0] += dot(ds[end:], query, NN)
            far_sum[1] += dot(low[end:], grad, NN)
        for index, ref in enumerate(far_outs):
            slot = jnp.maximum(at_group - index - 2, 0) // 2
            start = pl.multiple_of(slot * BLK, BLK)
            ref[...] = before_refs[index][...]
            lanes = slice(head * HD, (head + 1) * HD)
            ref[0, :, lanes] = (far_sum[0, pl.ds(start, BLK), :] * SCALE).astype(jnp.bfloat16)
            ref[1, :, lanes] = far_sum[1, pl.ds(start, BLK), :].astype(jnp.bfloat16)

    span = (SPAN + slots) * BLK
    outs = call(
        body, (meta,), (bias, stats, qd, own, prev, *far, *before),
        [shape((whole, HD)), shape((2, whole, HD), jnp.float32)]
        + [shape((2, BLK, width))] * len(far),
        [
            pltpu.VMEM((everything, HD), jnp.bfloat16),
            pltpu.VMEM((everything, HD), jnp.bfloat16),
            pltpu.VMEM((2, slots * BLK, HD), jnp.float32),
        ],
        cost(8 * whole * span * HD * 2, 4 * 1024 * 1024, whole * span),
        f"attention_back_{head}", 24,
    )
    return outs[0], outs[1], outs[2:]


def backward_next(grads, qd, own, bias, stats, meta):
    whole, width = qd.shape[1:]
    heads = width // HD
    pairs = whole // PAIR

    def body(meta_ref, bias_ref, stats_ref, *refs):
        (grad_refs, (qd_ref, own_ref, out)), refs = split_refs(refs, (heads, 3))
        strided = pl.ds(pl.multiple_of(meta_ref[2] * BLK, BLK), BLK)
        for h in range(heads):
            lanes = slice(h * HD, (h + 1) * HD)
            out[0, :, lanes] = grad_refs[h][0]
            out[1, :, lanes] = grad_refs[h][1]
            for t in range(pairs):
                here = slice(t * PAIR, (t + 1) * PAIR)
                window = slice(t * PAIR + BLK, whole)
                near = (whole - BLK) // BLK - t * (PAIR // BLK)
                keys = jnp.concatenate([own_ref[0, window, lanes], own_ref[0, strided, lanes]], axis=0)
                vals = jnp.concatenate([own_ref[1, window, lanes], own_ref[1, strided, lanes]], axis=0)
                query, grad = qd_ref[0, here, lanes], qd_ref[1, here, lanes]
                rows_here = bias_rows(bias_ref, t, list(range(near)) + [SPAN])
                s = masked_scores(keys, query, rows_here, None)
                probs = jnp.exp2(s - stats_ref[t, 2 * h : 2 * h + 1, :])
                delta = stats_ref[t, 2 * h + 1 : 2 * h + 2, :]
                ds = (probs * (dot(vals, grad, NT) - delta)).astype(jnp.bfloat16)
                dk = dot(ds, query, NN)
                dv = dot(probs.astype(jnp.bfloat16), grad, NN)
                out[0, window, lanes] += dk[: near * BLK]
                out[1, window, lanes] += dv[: near * BLK]
                out[0, strided, lanes] += dk[near * BLK :]
                out[1, strided, lanes] += dv[near * BLK :]
        out[0] = out[0] * SCALE

    return call(
        body, (meta,), (bias, stats, *grads, qd, own),
        [shape((2, whole, width), jnp.float32)], [],
        cost(8 * whole * 5 * BLK * width, 7 * 1024 * 1024, whole * 5 * BLK * heads),
        "attention_back_next", 24,
    )[0]


def combine(dq, own, far, meta, group, rows):
    whole, width = own.shape[1:]

    def body(meta_ref, own_ref, *refs):
        (dq_refs, far_refs, outs, (acc,)), refs = split_refs(refs, (len(dq), len(far), group, 1))
        me, offset = meta_ref[0], meta_ref[2]
        acc[...] = own_ref[...]
        at = pl.multiple_of(offset * BLK, BLK)
        for ref in far_refs:
            acc[:, pl.ds(at, BLK), :] += ref[...].astype(jnp.float32)
        for k in range(group):
            here = pl.ds(pl.multiple_of((me ^ k) * rows, rows), rows)
            for h in range(len(dq)):
                outs[k][0, :, h * HD : (h + 1) * HD] = dq_refs[h][here, :]
            outs[k][1] = acc[0, here, :].astype(jnp.bfloat16)
            outs[k][2] = acc[1, here, :].astype(jnp.bfloat16)

    return call(
        body, (meta,), (own, *dq, *far), [shape((3, rows, width))] * group,
        [pltpu.VMEM((2, whole, width), jnp.float32)],
        cost(0, 4 * 1024 * 1024), "combine",
    )


def project(head, mine, theirs, attn, before, meta, group, parts):
    height, whole = mine.shape
    each = 2 * height // parts
    full = group * HD
    more = parts // 2 - 1

    def body(meta_ref, mine_ref, theirs_ref, *refs):
        (attn_refs, before_refs, outs), refs = split_refs(refs, (group, len(before), 6))
        keep, first, odds, evens, pool, total = outs
        for ref in before_refs:
            first[:head] = ref[...]
        me, at_group, core = meta_ref[0], meta_ref[1], meta_ref[3]
        for k in range(group):
            at = pl.multiple_of((me ^ k) * HD, HD)
            pool[:, pl.ds(at, HD)] = attn_refs[k][...]
        upper = pl.ds(pl.multiple_of(core * height, height), height)
        lower = pl.ds(pl.multiple_of((1 - core) * height, height), height)
        total[upper, :] = dot(mine_ref[...], pool[...], NN)
        total[lower, :] = dot(theirs_ref[...], pool[...], NN)
        for m in range(parts):
            part = total[pl.ds(pl.multiple_of((at_group ^ m) * each, each), each), :]
            if m == 0:
                keep[...] = part
            elif m == 1:
                first[head] = part.astype(jnp.bfloat16)
            elif m % 2 == 1:
                odds[m // 2 - 1] = part.astype(jnp.bfloat16)
            else:
                evens[m // 2 - 1] = part

    return call(
        body, (meta,), (mine, theirs, *attn, *before),
        [
            shape((each, full), jnp.float32),
            shape((head + 1, each, full)),
            shape((more, each, full)),
            shape((more, each, full), jnp.float32),
        ],
        [pltpu.VMEM((whole, full), jnp.bfloat16), pltpu.VMEM((2 * height, full), jnp.float32)],
        cost(4 * height * whole * full, 6 * 1024 * 1024), f"project_{head}",
    )


def halve(head, evens, arrived):
    count, each, full = evens.shape
    more = (count - 1) // 2

    def body(evens_ref, arrived_ref, first, *rest):
        for m in range(1, count + 1):
            summed = evens_ref[m - 1] + arrived_ref[m - 1].astype(jnp.float32)
            if m == 1:
                first[...] = summed.astype(jnp.bfloat16)
            elif m % 2 == 1:
                rest[0][m // 2 - 1] = summed.astype(jnp.bfloat16)
            else:
                rest[1][m // 2 - 1] = summed

    others = [shape((more, each, full)), shape((more, each, full), jnp.float32)]
    return call(
        body, (), (evens, arrived), [shape((each, full))] + (others if more else []), [],
        cost(0, 3 * 1024 * 1024), f"halve_{head}",
    )


def finish(keep, neighbour, arrived, group):
    heads = len(keep)
    count = len(arrived[0])
    each = keep[0].shape[0]

    def body(*refs):
        (keep_refs, arrived_refs, (first, out)), refs = split_refs(refs, (heads, heads * count, 2))
        for h in range(heads):
            total = keep_refs[h][...] + first[h].astype(jnp.float32)
            for ref in arrived_refs[h * count : (h + 1) * count]:
                total = total + ref[...].astype(jnp.float32)
            for j in range(group):
                at = (j * heads + h) * HD
                out[:, at : at + HD] = total[:, j * HD : (j + 1) * HD]

    flat = [piece for pieces in arrived for piece in pieces]
    return call(
        body, (), (*keep, *flat, neighbour),
        [shape((each, group * heads * HD), jnp.float32)], [],
        cost(0, 3 * 1024 * 1024), "finish",
    )[0]


def unpack(pieces, meta, group):
    rows, width = pieces[0].shape[1:]

    def body(meta_ref, *refs):
        me = meta_ref[0]
        outs, sems = refs[group:-1], refs[-1]
        copies = []
        for k in range(group):
            at = pl.ds(pl.multiple_of((me ^ k) * width, width), width)
            for which in range(3):
                target = outs[which].at[:, at]
                copies.append(
                    pltpu.make_async_copy(refs[k].at[which], target, sems.at[k, which])
                )
        copied(*copies)

    return pl.pallas_call(
        body,
        out_shape=[shape((rows, group * width))] * 3,
        in_specs=[SMEM] + [ANY] * group,
        out_specs=[ANY] * 3,
        scratch_shapes=[pltpu.SemaphoreType.DMA((group, 3))],
        compiler_params=params(16),
        cost_estimate=cost(0, 3 * MIB),
        name="unpack",
    )(meta, *pieces)


def after(value, *others):
    return lax.optimization_barrier((value, *others))[0]


def local(devices, queries, keys, values, out_grad, proj_weight, layout):
    rows, columns = queries.shape
    group = LOCAL * BLK // rows
    parts = devices // group
    width = columns // group
    heads = width // HD
    blocks = layout.shape[0]
    slots = blocks // STRIDE
    position = lax.axis_index("seq")
    me, at_group = position % group, position // group
    core = lax.axis_index("head")
    offset = layout[blocks - 1, 0] % STRIDE
    place = jnp.stack([me, at_group, core]).astype(jnp.int32)
    meta = jnp.stack([me, at_group, offset, core]).astype(jnp.int32)

    def swap(piece, k):
        route = [(i, (i // group) * group + ((i % group) ^ k)) for i in range(devices)]
        return lax.ppermute(piece, "seq", route)

    def shifted(piece, distance):
        route = [
            (i, i + distance * group)
            for i in range(devices)
            if 0 <= i + distance * group < devices
        ]
        return lax.ppermute(piece, "seq", route)

    def swap_groups(piece, bit):
        route = [(i, ((i // group) ^ bit) * group + i % group) for i in range(devices)]
        return lax.ppermute(piece, "seq", route)

    def summary_route(distance, back):
        route = [
            (i, i + distance * group)
            for i in range(devices - distance * group)
            if (i // group) % 2 == 0
        ]
        return [(b, a) for a, b in route] if back else route

    def exchange(pieces):
        return [pieces[0]] + [swap(pieces[k], k) for k in range(1, group)]

    def add_up(head, odds, evens, before, token):
        arrivals, bit = [], 2
        odds = after(odds, *jax.tree.leaves(before))
        while True:
            first, *more = halve(head, evens, odds)
            token = after(token, first)
            arrivals.append(swap_groups(first, bit))
            if not more:
                return arrivals, token
            odds, evens = swap_groups(more[0], bit), more[1]
            bit *= 2

    kv = pack_kv(keys, values, place, group, width)
    own_kv = exchange(kv)
    early = after(place, own_kv[1], own_kv[2])
    qd_cut = grads_packed(queries, out_grad, proj_weight, early, group, parts)
    pool, strided = assemble_kv(own_kv, after(meta, qd_cut[0]), group)
    prev = shifted(pool, 1)
    qd_pieces = exchange(qd_cut)
    far = [
        lax.ppermute(strided, "seq", summary_route(distance, False))
        for distance in range(2, parts)
    ]
    bias, bias_next = masks_of(layout, after(meta, strided), parts, slots)
    qd, mine = assemble(qd_pieces, after(meta, bias, prev, *far), group)
    theirs = lax.ppermute(mine, "head", [(0, 1), (1, 0)])
    next_qd = shifted(qd, -1)

    stats = jnp.zeros((LOCAL // 2, 2 * heads, PAIR), jnp.float32)
    order = meta
    attn = []
    for h in range(heads):
        got, stats = forward(h, qd, pool, prev, far, bias, stats, order, group, slots)
        attn.append([got] + [swap(got, k) for k in range(1, group)])
        order = after(meta, got, theirs)

    dq, grads, keep, finals, firsts = [], [], [], [], []
    far_grads = [jnp.zeros((2, BLK, width), jnp.bfloat16) for _ in far]
    order = after(meta, stats, theirs)
    for h in range(heads):
        got = backward(
            h, qd, pool, prev, far, far_grads, bias, stats, order, group, slots
        )
        dq.append(got[0])
        grads.append(got[1])
        far_grads = got[2]
        order = after(order, got[0])
        if h > 0:
            order = after(order, next_stats)
            sums, order = add_up(h - 1, odds, evens, got[0], order)
            finals.append(sums)
        kept, first, odds, evens = project(
            h, mine, theirs, attn[h], firsts, order, group, parts
        )
        keep.append(kept)
        firsts = [first]
        odds = swap_groups(odds, 1)
        order = after(meta, first)
        if h == 0:
            next_stats = shifted(after(stats, next_qd, first), -1)
    neighbour = swap_groups(first, 1)
    far_back = [
        lax.ppermute(piece, "seq", summary_route(index + 2, True))
        for index, piece in enumerate(far_grads)
    ]
    order = after(order, finals[0])
    own_grad = backward_next(grads, next_qd, pool, bias_next, next_stats, order)
    sums, order = add_up(heads - 1, odds, evens, (own_grad, finals[0]), meta)
    finals.append(sums)
    final = exchange(combine(dq, own_grad, far_back, order, group, rows))
    query_grad, key_grad, value_grad = unpack(final, meta, group)
    proj_grad = finish(keep, neighbour, finals, group)
    return (query_grad, key_grad, value_grad, proj_grad)


def solution(mesh):
    split = P(("dp", "seq"), "head")
    return jax.shard_map(
        functools.partial(local, mesh.shape["seq"]),
        mesh=mesh,
        in_specs=(split, split, split, P(("dp", "seq"), None), P(None, "head"), P()),
        out_specs=(split, split, split, split),
        check_vma=False,
    )
```

```python
import functools
import math

import jax
import jax.numpy as jnp
from jax import lax
from jax.experimental import pallas as pl
from jax.experimental.pallas import tpu as pltpu
from jax.sharding import PartitionSpec as P

HD = 128
BLK = 128
LOCAL = 8
STRIDE = 16
PAIR = 2 * BLK
SPAN = LOCAL + 1
SCALE = HD ** (-0.5)
SCALE2 = SCALE * math.log2(math.e)
MIB = 1024 * 1024

NT = (((1,), (1,)), ((), ()))
NN = (((1,), (0,)), ((), ()))
TN = (((0,), (0,)), ((), ()))
SMEM = pl.BlockSpec(memory_space=pltpu.SMEM)
VMEM = pl.BlockSpec(memory_space=pltpu.VMEM)
HBM = pl.BlockSpec(memory_space=pltpu.HBM)
ANY = pl.BlockSpec(memory_space=pl.ANY)


def shape(dims, dtype=jnp.bfloat16):
    return jax.ShapeDtypeStruct(dims, dtype)


def dot(a, b, dims):
    return lax.dot_general(a, b, dims, preferred_element_type=jnp.float32)


def params(size):
    return pltpu.CompilerParams(vmem_limit_bytes=size * MIB)


def cost(flops, size, exps=0):
    return pl.CostEstimate(flops=1, bytes_accessed=1, transcendentals=0)


def call(body, scalars, arrays, outs, scratch, estimate, name, size=16):
    return pl.pallas_call(
        body,
        out_shape=outs,
        in_specs=[SMEM] * len(scalars) + [VMEM] * len(arrays),
        out_specs=[VMEM] * len(outs),
        scratch_shapes=scratch,
        compiler_params=params(size),
        cost_estimate=estimate,
        name=name,
    )(*scalars, *arrays)


def one_head(refs, head):
    return [ref.at[(slice(None),) * (ref.ndim - 1) + (pl.ds(head * HD, HD),)] for ref in refs]


def split_refs(refs, counts):
    refs, taken = list(refs), []
    for count in counts:
        taken.append(refs[:count])
        refs = refs[count:]
    return taken, refs


def copied(*copies):
    for copy in copies:
        copy.start()
    for copy in copies:
        copy.wait()


def pack_kv(keys, values, meta, group, width):
    rows = keys.shape[0]

    def body(meta_ref, k_ref, v_ref, *refs):
        outs, (k_in, v_in, sems) = refs[:group], refs[group:]
        me = meta_ref[0]
        copied(
            pltpu.make_async_copy(k_ref, k_in, sems.at[0]),
            pltpu.make_async_copy(v_ref, v_in, sems.at[1]),
        )
        for k in range(group):
            at = pl.ds(pl.multiple_of((me ^ k) * width, width), width)
            outs[k][0] = k_in[:, at]
            outs[k][1] = v_in[:, at]

    return pl.pallas_call(
        body,
        out_shape=[shape((2, rows, width))] * group,
        in_specs=[SMEM, HBM, HBM],
        out_specs=[VMEM] * group,
        scratch_shapes=[
            pltpu.VMEM(keys.shape, jnp.bfloat16),
            pltpu.VMEM(keys.shape, jnp.bfloat16),
            pltpu.SemaphoreType.DMA((2,)),
        ],
        compiler_params=params(60),
        cost_estimate=cost(0, 4 * keys.size * 2),
        name="pack_kv",
    )(meta, keys, values)


def grads_packed(queries, out_grad, proj_weight, meta, group, parts):
    rows, depth = out_grad.shape
    columns = queries.shape[1]
    width = columns // group
    each = depth // (group * parts)
    half = parts // 2
    chunks = 8
    step = depth // chunks
    assert rows == width

    def body(meta_ref, q_ref, og_ref, w_ref, *refs):
        outs, (q, og, w, total, sems, w_sems) = refs[:group], refs[group:]
        me, core = meta_ref[0], meta_ref[2]
        og_copy = pltpu.make_async_copy(og_ref, og, sems.at[0])
        q_copy = pltpu.make_async_copy(q_ref, q, sems.at[1])
        og_copy.start()
        w_copies = []
        for c in range(chunks):
            at = slice(c * step, (c + 1) * step)
            w_copies.append(pltpu.make_async_copy(w_ref.at[at, :], w.at[at, :], w_sems.at[c]))
            w_copies[c].start()
        q_copy.start()
        og_copy.wait()
        for k in range(group):
            for part in range(half):
                at = ((core * half + part) * group + (me ^ k)) * each
                at = pl.multiple_of(at, each)
                to = 2 * rows + part * each
                outs[k][to : to + each, :] = og[:, pl.ds(at, each)].T
        for c in range(chunks):
            at = slice(c * step, (c + 1) * step)
            w_copies[c].wait()
            got = dot(og[:, at], w[at, :], NN)
            if c == 0:
                total[...] = got
            else:
                total[...] += got
        q_copy.wait()
        for k in range(group):
            at = pl.ds(pl.multiple_of((me ^ k) * width, width), width)
            outs[k][:rows, :] = q[:, at]
            outs[k][rows : 2 * rows, :] = total[:, at].astype(jnp.bfloat16)

    return pl.pallas_call(
        body,
        out_shape=[shape((2 * rows + half * each, rows))] * group,
        in_specs=[SMEM, HBM, HBM, HBM],
        out_specs=[VMEM] * group,
        scratch_shapes=[
            pltpu.VMEM((rows, columns), jnp.bfloat16),
            pltpu.VMEM((rows, depth), jnp.bfloat16),
            pltpu.VMEM((depth, columns), jnp.bfloat16),
            pltpu.VMEM((rows, columns), jnp.float32),
            pltpu.SemaphoreType.DMA((2,)),
            pltpu.SemaphoreType.DMA((chunks,)),
        ],
        compiler_params=params(60),
        cost_estimate=cost(2 * rows * depth * columns, 12 * 1024 * 1024),
        name="attn_grad",
    )(meta, queries, out_grad, proj_weight)


def assemble_kv(pieces, meta, group):
    rows, width = pieces[0].shape[1:]

    def body(meta_ref, *refs):
        me = meta_ref[0]
        pool, strided, sems = refs[group:]
        copies = []
        for k in range(group):
            at = pl.ds(pl.multiple_of((me ^ k) * rows, rows), rows)
            copies.append(pltpu.make_async_copy(refs[k], pool.at[:, at, :], sems.at[k]))
        copied(*copies)
        strided[...] = pool[:, pl.ds(pl.multiple_of(meta_ref[2] * BLK, BLK), BLK), :]

    return pl.pallas_call(
        body,
        out_shape=[
            shape((2, group * rows, width)),
            shape((2, BLK, width)),
        ],
        in_specs=[SMEM] + [ANY] * group,
        out_specs=[VMEM] * 2,
        scratch_shapes=[pltpu.SemaphoreType.DMA((group,))],
        compiler_params=params(16),
        cost_estimate=cost(0, 3 * MIB),
        name="assemble_kv",
    )(meta, *pieces)


def assemble(pieces, meta, group):
    rows = pieces[0].shape[1]
    height = pieces[0].shape[0] - 2 * rows

    def body(meta_ref, *refs):
        me = meta_ref[0]
        qd, og = refs[group:]
        for k in range(group):
            at = pl.ds(pl.multiple_of((me ^ k) * rows, rows), rows)
            qd[0, at, :] = refs[k][:rows, :]
            qd[1, at, :] = refs[k][rows : 2 * rows, :]
            og[:, at] = refs[k][2 * rows :, :]

    return call(
        body, (meta,), tuple(pieces),
        [shape((2, group * rows, rows)), shape((height, group * rows))], [],
        cost(0, 4 * MIB), "assemble",
    )


def masks_of(layout, meta, parts, slots):
    width = layout.shape[1]
    pairs = LOCAL // 2

    def body(meta_ref, table, own_ref, next_ref):
        at_group = meta_ref[1]
        low_half = lax.broadcasted_iota(jnp.int32, (1, PAIR), 1) < BLK

        def bits_of(group_at, row):
            block = group_at * LOCAL + row
            base = block - row % 2 - (LOCAL - 1)
            at = jnp.minimum(block, table.shape[0] - 1)
            bits = jnp.int32(0)
            for c in range(width):
                entry = table[at, c]
                near = entry >= jnp.maximum(block - (LOCAL - 1), 0)
                place = jnp.where(near, entry - base, SPAN + jnp.maximum(entry, 0) // STRIDE)
                bit = jnp.left_shift(jnp.int32(1), place)
                bits = bits | jnp.where(entry >= 0, bit, 0)
            return jnp.where(group_at < parts, bits, 0)

        def row_of(first, second, place):
            one = jnp.where((jnp.right_shift(first, place) & 1) == 1, 0.0, -jnp.inf)
            two = jnp.where((jnp.right_shift(second, place) & 1) == 1, 0.0, -jnp.inf)
            return jnp.where(low_half, one, two).astype(jnp.float32)

        for t in range(pairs):
            first, second = bits_of(at_group, 2 * t), bits_of(at_group, 2 * t + 1)
            for place in range(SPAN + slots):
                own_ref[t, place : place + 1, :] = row_of(first, second, place)
            first, second = bits_of(at_group + 1, 2 * t), bits_of(at_group + 1, 2 * t + 1)
            for place in range(SPAN):
                next_ref[t, place : place + 1, :] = row_of(first, second, place)
            even = at_group % 2 == 0
            place = SPAN + at_group // 2
            first, second = jnp.where(even, first, 0), jnp.where(even, second, 0)
            next_ref[t, SPAN : SPAN + 1, :] = row_of(first, second, place)

    return call(
        body, (meta, layout), (),
        [
            shape((pairs, SPAN + slots, PAIR), jnp.float32),
            shape((pairs, SPAN + 1, PAIR), jnp.float32),
        ],
        [], cost(0, 128 * 1024), "masks",
    )


def fill_pools(meta_ref, own, prev, far, k_pool, v_pool, slots):
    at_group, offset = meta_ref[1], meta_ref[2]
    whole = own.shape[1]
    k_pool[:whole, :] = prev[0]
    v_pool[:whole, :] = prev[1]
    k_pool[whole : 2 * whole, :] = own[0]
    v_pool[whole : 2 * whole, :] = own[1]
    tail = jnp.zeros((slots * BLK, k_pool.shape[1]), k_pool.dtype)
    k_pool[2 * whole :, :] = tail
    v_pool[2 * whole :, :] = tail

    @pl.when(at_group % 2 == 1)
    def _():
        to = pl.multiple_of(2 * whole + (at_group // 2) * BLK, BLK)
        start = pl.multiple_of(offset * BLK, BLK)
        k_pool[pl.ds(to, BLK), :] = k_pool[pl.ds(start, BLK), :]
        v_pool[pl.ds(to, BLK), :] = v_pool[pl.ds(start, BLK), :]

    for index, ref in enumerate(far):
        distance = index + 2

        @pl.when((at_group >= distance) & ((at_group - distance) % 2 == 0))
        def _():
            to = pl.multiple_of(2 * whole + ((at_group - distance) // 2) * BLK, BLK)
            k_pool[pl.ds(to, BLK), :] = ref[0]
            v_pool[pl.ds(to, BLK), :] = ref[1]


def causal_masks():
    key_at = lax.broadcasted_iota(jnp.int32, (BLK, PAIR), 0)
    query_at = lax.broadcasted_iota(jnp.int32, (BLK, PAIR), 1)
    first = (key_at <= query_at) | (query_at >= BLK)
    second = key_at <= query_at - BLK
    return first, second


def masked_scores(keys, query, bias, masks):
    raw = dot(keys, query, NT) * SCALE2
    tiles = []
    for j in range(keys.shape[0] // BLK):
        tile = raw[j * BLK : (j + 1) * BLK] + bias[j]
        if masks is not None and j in (LOCAL - 1, LOCAL):
            tile = jnp.where(masks[j - LOCAL + 1], tile, -jnp.inf)
        tiles.append(tile)
    return jnp.concatenate(tiles, axis=0)


def bias_rows(bias_ref, t, picked):
    return [bias_ref[t, j : j + 1, :] for j in picked]


def forward(head, qd, own, prev, far, bias, stats, meta, group, slots):
    whole = qd.shape[1]
    pairs = whole // PAIR
    counts = (3, len(far))

    def body(meta_ref, bias_ref, before_ref, *refs):
        (around, far_refs), refs = split_refs(refs, counts)
        qd_ref, *around = one_head(around, head)
        far_refs = one_head(far_refs, head)
        out_ref, stats_ref, k_pool, v_pool = refs
        fill_pools(meta_ref, *around, far_refs, k_pool, v_pool, slots)
        stats_ref[...] = before_ref[...]
        masks = causal_masks()
        for t in range(pairs):
            here = slice(t * PAIR, (t + 1) * PAIR)
            window = slice(t * PAIR + BLK, t * PAIR + BLK + SPAN * BLK)
            keys = jnp.concatenate([k_pool[window, :], k_pool[2 * whole :, :]], axis=0)
            vals = jnp.concatenate([v_pool[window, :], v_pool[2 * whole :, :]], axis=0)
            s = masked_scores(keys, qd_ref[0, here, :], bias_rows(bias_ref, t, range(SPAN + slots)), masks)
            top = jnp.max(s, axis=0, keepdims=True)
            e = jnp.exp2(s - top)
            total = jnp.sum(e, axis=0, keepdims=True)
            low = (e * (1.0 / total)).astype(jnp.bfloat16)
            out = dot(low, vals, TN).astype(jnp.bfloat16)
            out_ref[here, :] = out
            product = out.astype(jnp.float32) * qd_ref[1, here, :].astype(jnp.float32)
            stats_ref[t, 2 * head : 2 * head + 1, :] = top + jnp.log2(total)
            stats_ref[t, 2 * head + 1 : 2 * head + 2, :] = jnp.sum(product.T, axis=0, keepdims=True)

    span = (SPAN + slots) * BLK
    return call(
        body, (meta,), (bias, stats, qd, own, prev, *far),
        [shape((whole, HD)), shape(stats.shape, jnp.float32)],
        [pltpu.VMEM((2 * whole + slots * BLK, HD), jnp.bfloat16)] * 2,
        cost(4 * whole * span * HD * 2, 3 * 1024 * 1024, whole * span),
        f"attention_{head}", 24,
    )


def backward(head, qd, own, prev, far, before, bias, stats, meta, group, slots):
    whole, width = qd.shape[1:]
    pairs = whole // PAIR
    counts = (3, len(far), len(before))
    everything = 2 * whole + slots * BLK

    def body(meta_ref, bias_ref, stats_ref, *refs):
        (around, far_refs, before_refs), refs = split_refs(refs, counts)
        qd_ref, *around = one_head(around, head)
        far_refs = one_head(far_refs, head)
        ((dq_ref, grad_ref), far_outs), refs = split_refs(refs, (2, len(far)))
        k_pool, v_pool, far_sum = refs
        at_group = meta_ref[1]
        fill_pools(meta_ref, *around, far_refs, k_pool, v_pool, slots)
        masks = causal_masks()
        grad_ref[...] = jnp.zeros_like(grad_ref)
        far_sum[...] = jnp.zeros_like(far_sum)
        for t in range(pairs):
            here = slice(t * PAIR, (t + 1) * PAIR)
            window = slice(t * PAIR + BLK, t * PAIR + BLK + SPAN * BLK)
            others = max(whole - (t * PAIR + BLK), 0)
            end = SPAN * BLK
            mine = slice(t * PAIR + BLK + others - whole, t * PAIR + BLK + end - whole)
            keys = jnp.concatenate([k_pool[window, :], k_pool[2 * whole :, :]], axis=0)
            vals = jnp.concatenate([v_pool[window, :], v_pool[2 * whole :, :]], axis=0)
            query, grad = qd_ref[0, here, :], qd_ref[1, here, :]
            s = masked_scores(keys, query, bias_rows(bias_ref, t, range(SPAN + slots)), masks)
            probs = jnp.exp2(s - stats_ref[t, 2 * head : 2 * head + 1, :])
            delta = stats_ref[t, 2 * head + 1 : 2 * head + 2, :]
            ds = (probs * (dot(vals, grad, NT) - delta)).astype(jnp.bfloat16)
            low = probs.astype(jnp.bfloat16)
            dq_ref[here, :] = (dot(ds, keys, TN) * SCALE).astype(jnp.bfloat16)
            grad_ref[0, mine, :] += dot(ds[others:end], query, NN)
            grad_ref[1, mine, :] += dot(low[others:end], grad, NN)
            far_sum[0] += dot(ds[end:], query, NN)
            far_sum[1] += dot(low[end:], grad, NN)
        for index, ref in enumerate(far_outs):
            slot = jnp.maximum(at_group - index - 2, 0) // 2
            start = pl.multiple_of(slot * BLK, BLK)
            ref[...] = before_refs[index][...]
            lanes = slice(head * HD, (head + 1) * HD)
            ref[0, :, lanes] = (far_sum[0, pl.ds(start, BLK), :] * SCALE).astype(jnp.bfloat16)
            ref[1, :, lanes] = far_sum[1, pl.ds(start, BLK), :].astype(jnp.bfloat16)

    span = (SPAN + slots) * BLK
    outs = call(
        body, (meta,), (bias, stats, qd, own, prev, *far, *before),
        [shape((whole, HD)), shape((2, whole, HD), jnp.float32)]
        + [shape((2, BLK, width))] * len(far),
        [
            pltpu.VMEM((everything, HD), jnp.bfloat16),
            pltpu.VMEM((everything, HD), jnp.bfloat16),
            pltpu.VMEM((2, slots * BLK, HD), jnp.float32),
        ],
        cost(8 * whole * span * HD * 2, 4 * 1024 * 1024, whole * span),
        f"attention_back_{head}", 24,
    )
    return outs[0], outs[1], outs[2:]


def backward_next(grads, qd, own, bias, stats, meta):
    whole, width = qd.shape[1:]
    heads = width // HD
    pairs = whole // PAIR

    def body(meta_ref, bias_ref, stats_ref, *refs):
        (grad_refs, (qd_ref, own_ref, out)), refs = split_refs(refs, (heads, 3))
        strided = pl.ds(pl.multiple_of(meta_ref[2] * BLK, BLK), BLK)
        for h in range(heads):
            lanes = slice(h * HD, (h + 1) * HD)
            out[0, :, lanes] = grad_refs[h][0]
            out[1, :, lanes] = grad_refs[h][1]
            for t in range(pairs):
                here = slice(t * PAIR, (t + 1) * PAIR)
                window = slice(t * PAIR + BLK, whole)
                near = (whole - BLK) // BLK - t * (PAIR // BLK)
                keys = jnp.concatenate([own_ref[0, window, lanes], own_ref[0, strided, lanes]], axis=0)
                vals = jnp.concatenate([own_ref[1, window, lanes], own_ref[1, strided, lanes]], axis=0)
                query, grad = qd_ref[0, here, lanes], qd_ref[1, here, lanes]
                rows_here = bias_rows(bias_ref, t, list(range(near)) + [SPAN])
                s = masked_scores(keys, query, rows_here, None)
                probs = jnp.exp2(s - stats_ref[t, 2 * h : 2 * h + 1, :])
                delta = stats_ref[t, 2 * h + 1 : 2 * h + 2, :]
                ds = (probs * (dot(vals, grad, NT) - delta)).astype(jnp.bfloat16)
                dk = dot(ds, query, NN)
                dv = dot(probs.astype(jnp.bfloat16), grad, NN)
                out[0, window, lanes] += dk[: near * BLK]
                out[1, window, lanes] += dv[: near * BLK]
                out[0, strided, lanes] += dk[near * BLK :]
                out[1, strided, lanes] += dv[near * BLK :]
        out[0] = out[0] * SCALE

    return call(
        body, (meta,), (bias, stats, *grads, qd, own),
        [shape((2, whole, width), jnp.float32)], [],
        cost(8 * whole * 5 * BLK * width, 7 * 1024 * 1024, whole * 5 * BLK * heads),
        "attention_back_next", 24,
    )[0]


def combine(dq, own, far, meta, group, rows):
    whole, width = own.shape[1:]

    def body(meta_ref, own_ref, *refs):
        (dq_refs, far_refs, outs, (acc,)), refs = split_refs(refs, (len(dq), len(far), group, 1))
        me, offset = meta_ref[0], meta_ref[2]
        acc[...] = own_ref[...]
        at = pl.multiple_of(offset * BLK, BLK)
        for ref in far_refs:
            acc[:, pl.ds(at, BLK), :] += ref[...].astype(jnp.float32)
        for k in range(group):
            here = pl.ds(pl.multiple_of((me ^ k) * rows, rows), rows)
            for h in range(len(dq)):
                outs[k][0, :, h * HD : (h + 1) * HD] = dq_refs[h][here, :]
            outs[k][1] = acc[0, here, :].astype(jnp.bfloat16)
            outs[k][2] = acc[1, here, :].astype(jnp.bfloat16)

    return call(
        body, (meta,), (own, *dq, *far), [shape((3, rows, width))] * group,
        [pltpu.VMEM((2, whole, width), jnp.float32)],
        cost(0, 4 * 1024 * 1024), "combine",
    )


def project(head, mine, theirs, attn, before, meta, group, parts):
    height, whole = mine.shape
    each = 2 * height // parts
    full = group * HD
    more = parts // 2 - 1

    def body(meta_ref, mine_ref, theirs_ref, *refs):
        (attn_refs, before_refs, outs), refs = split_refs(refs, (group, len(before), 6))
        keep, first, odds, evens, pool, total = outs
        for ref in before_refs:
            first[:head] = ref[...]
        me, at_group, core = meta_ref[0], meta_ref[1], meta_ref[3]
        for k in range(group):
            at = pl.multiple_of((me ^ k) * HD, HD)
            pool[:, pl.ds(at, HD)] = attn_refs[k][...]
        upper = pl.ds(pl.multiple_of(core * height, height), height)
        lower = pl.ds(pl.multiple_of((1 - core) * height, height), height)
        total[upper, :] = dot(mine_ref[...], pool[...], NN)
        total[lower, :] = dot(theirs_ref[...], pool[...], NN)
        for m in range(parts):
            part = total[pl.ds(pl.multiple_of((at_group ^ m) * each, each), each), :]
            if m == 0:
                keep[...] = part
            elif m == 1:
                first[head] = part.astype(jnp.bfloat16)
            elif m % 2 == 1:
                odds[m // 2 - 1] = part.astype(jnp.bfloat16)
            else:
                evens[m // 2 - 1] = part

    return call(
        body, (meta,), (mine, theirs, *attn, *before),
        [
            shape((each, full), jnp.float32),
            shape((head + 1, each, full)),
            shape((more, each, full)),
            shape((more, each, full), jnp.float32),
        ],
        [pltpu.VMEM((whole, full), jnp.bfloat16), pltpu.VMEM((2 * height, full), jnp.float32)],
        cost(4 * height * whole * full, 6 * 1024 * 1024), f"project_{head}",
    )


def halve(head, evens, arrived):
    count, each, full = evens.shape
    more = (count - 1) // 2

    def body(evens_ref, arrived_ref, first, *rest):
        for m in range(1, count + 1):
            summed = evens_ref[m - 1] + arrived_ref[m - 1].astype(jnp.float32)
            if m == 1:
                first[...] = summed.astype(jnp.bfloat16)
            elif m % 2 == 1:
                rest[0][m // 2 - 1] = summed.astype(jnp.bfloat16)
            else:
                rest[1][m // 2 - 1] = summed

    others = [shape((more, each, full)), shape((more, each, full), jnp.float32)]
    return call(
        body, (), (evens, arrived), [shape((each, full))] + (others if more else []), [],
        cost(0, 3 * 1024 * 1024), f"halve_{head}",
    )


def finish(keep, neighbour, arrived, group):
    heads = len(keep)
    count = len(arrived[0])
    each = keep[0].shape[0]

    def body(*refs):
        (keep_refs, arrived_refs, (first, out)), refs = split_refs(refs, (heads, heads * count, 2))
        for h in range(heads):
            total = keep_refs[h][...] + first[h].astype(jnp.float32)
            for ref in arrived_refs[h * count : (h + 1) * count]:
                total = total + ref[...].astype(jnp.float32)
            for j in range(group):
                at = (j * heads + h) * HD
                out[:, at : at + HD] = total[:, j * HD : (j + 1) * HD]

    flat = [piece for pieces in arrived for piece in pieces]
    return call(
        body, (), (*keep, *flat, neighbour),
        [shape((each, group * heads * HD), jnp.float32)], [],
        cost(0, 3 * 1024 * 1024), "finish",
    )[0]


def unpack(pieces, meta, group):
    rows, width = pieces[0].shape[1:]

    def body(meta_ref, *refs):
        me = meta_ref[0]
        outs, sems = refs[group:-1], refs[-1]
        copies = []
        for k in range(group):
            at = pl.ds(pl.multiple_of((me ^ k) * width, width), width)
            for which in range(3):
                target = outs[which].at[:, at]
                copies.append(
                    pltpu.make_async_copy(refs[k].at[which], target, sems.at[k, which])
                )
        copied(*copies)

    return pl.pallas_call(
        body,
        out_shape=[shape((rows, group * width))] * 3,
        in_specs=[SMEM] + [ANY] * group,
        out_specs=[ANY] * 3,
        scratch_shapes=[pltpu.SemaphoreType.DMA((group, 3))],
        compiler_params=params(16),
        cost_estimate=cost(0, 3 * MIB),
        name="unpack",
    )(meta, *pieces)


def after(value, *others):
    return lax.optimization_barrier((value, *others))[0]


def local(devices, queries, keys, values, out_grad, proj_weight, layout):
    rows, columns = queries.shape
    group = LOCAL * BLK // rows
    parts = devices // group
    width = columns // group
    heads = width // HD
    blocks = layout.shape[0]
    slots = blocks // STRIDE
    position = lax.axis_index("seq")
    me, at_group = position % group, position // group
    core = lax.axis_index("head")
    offset = layout[blocks - 1, 0] % STRIDE
    place = jnp.stack([me, at_group, core]).astype(jnp.int32)
    meta = jnp.stack([me, at_group, offset, core]).astype(jnp.int32)

    def swap(piece, k):
        route = [(i, (i // group) * group + ((i % group) ^ k)) for i in range(devices)]
        return lax.ppermute(piece, "seq", route)

    def shifted(piece, distance):
        route = [
            (i, i + distance * group)
            for i in range(devices)
            if 0 <= i + distance * group < devices
        ]
        return lax.ppermute(piece, "seq", route)

    def swap_groups(piece, bit):
        route = [(i, ((i // group) ^ bit) * group + i % group) for i in range(devices)]
        return lax.ppermute(piece, "seq", route)

    def summary_route(distance, back):
        route = [
            (i, i + distance * group)
            for i in range(devices - distance * group)
            if (i // group) % 2 == 0
        ]
        return [(b, a) for a, b in route] if back else route

    def exchange(pieces):
        return [pieces[0]] + [swap(pieces[k], k) for k in range(1, group)]

    def add_up(head, odds, evens, before, token):
        arrivals, bit = [], 2
        odds = after(odds, *jax.tree.leaves(before))
        while True:
            first, *more = halve(head, evens, odds)
            token = after(token, first)
            done = first
            arrivals.append(swap_groups(first, bit))
            if not more:
                return arrivals, token, done
            odds, evens = swap_groups(more[0], bit), more[1]
            bit *= 2

    kv = pack_kv(keys, values, place, group, width)
    own_kv = exchange(kv)
    early = after(place, own_kv[1])
    qd_cut = grads_packed(queries, out_grad, proj_weight, early, group, parts)
    pool, strided = assemble_kv(own_kv, after(meta, qd_cut[0]), group)
    prev = shifted(pool, 1)
    qd_pieces = exchange(qd_cut)
    later = after(strided, qd_pieces[1])
    far = [
        lax.ppermute(
            strided if distance == 2 else later, "seq", summary_route(distance, False)
        )
        for distance in range(2, parts)
    ]
    bias, bias_next = masks_of(layout, after(meta, strided), parts, slots)
    qd, mine = assemble(qd_pieces, after(meta, bias, prev, *far), group)
    theirs = lax.ppermute(mine, "head", [(0, 1), (1, 0)])
    next_qd = shifted(qd, -1)

    stats = jnp.zeros((LOCAL // 2, 2 * heads, PAIR), jnp.float32)
    order = meta
    attn = []
    for h in range(heads):
        got, stats = forward(h, qd, pool, prev, far, bias, stats, order, group, slots)
        attn.append([got] + [swap(got, k) for k in range(1, group)])
        order = after(meta, got, theirs)

    dq, grads, keep, finals = [], [], [], []
    far_grads = [jnp.zeros((2, BLK, width), jnp.bfloat16) for _ in far]
    order, first = after(meta, stats, theirs), []
    for h in range(heads):
        got = backward(h, qd, pool, prev, far, far_grads, bias, stats, order, group, slots)
        dq.append(got[0])
        grads.append(got[1])
        far_grads = got[2]
        order = after(meta, got[0])
        if h > 0:
            order = after(order, next_stats)
        kept, first, odds, evens = project(h, mine, theirs, attn[h], first, order, group, parts)
        keep.append(kept)
        first, odds = [first], swap_groups(odds, 1)
        order = after(meta, *first)
        if h == 0:
            next_stats = shifted(after(stats, next_qd, *first), -1)
        if h < heads - 1:
            sums, order, _ = add_up(h, odds, evens, first, order)
            finals.append(sums)
    far_back = [
        lax.ppermute(piece, "seq", summary_route(index + 2, True))
        for index, piece in enumerate(far_grads)
    ]
    order = after(order, finals[0])
    own_grad = backward_next(grads, next_qd, pool, bias_next, next_stats, order)
    final_cut = combine(dq, own_grad, far_back, meta, group, rows)
    final = exchange(final_cut)
    sums, _, _ = add_up(heads - 1, odds, evens, final_cut, meta)
    finals.append(sums)
    neighbour = swap_groups(after(first[0], final_cut[0]), 1)
    proj_grad = finish(keep, neighbour, finals, group)
    query_grad, key_grad, value_grad = unpack(final, meta, group)
    return (query_grad, key_grad, value_grad, proj_grad)


def solution(mesh):
    split = P(("dp", "seq"), "head")
    return jax.shard_map(
        functools.partial(local, mesh.shape["seq"]),
        mesh=mesh,
        in_specs=(split, split, split, P(("dp", "seq"), None), P(None, "head"), P()),
        out_specs=(split, split, split, split),
        check_vma=False,
    )
```

```python
import functools
import math

import jax
import jax.numpy as jnp
from jax import lax
from jax.experimental import pallas as pl
from jax.experimental.pallas import tpu as pltpu
from jax.sharding import PartitionSpec as P

HD = 128
BLK = 128
LOCAL = 8
STRIDE = 16
PAIR = 2 * BLK
SPAN = LOCAL + 1
SCALE = HD ** (-0.5)
SCALE2 = SCALE * math.log2(math.e)
MIB = 1024 * 1024

NT = (((1,), (1,)), ((), ()))
NN = (((1,), (0,)), ((), ()))
TN = (((0,), (0,)), ((), ()))
SMEM = pl.BlockSpec(memory_space=pltpu.SMEM)
VMEM = pl.BlockSpec(memory_space=pltpu.VMEM)
HBM = pl.BlockSpec(memory_space=pltpu.HBM)
ANY = pl.BlockSpec(memory_space=pl.ANY)


def shape(dims, dtype=jnp.bfloat16):
    return jax.ShapeDtypeStruct(dims, dtype)


def dot(a, b, dims):
    return lax.dot_general(a, b, dims, preferred_element_type=jnp.float32)


def params(size):
    return pltpu.CompilerParams(vmem_limit_bytes=size * MIB)


def cost(flops, size, exps=0):
    return pl.CostEstimate(flops=1, bytes_accessed=1, transcendentals=0)


def call(body, scalars, arrays, outs, scratch, estimate, name, size=16):
    return pl.pallas_call(
        body,
        out_shape=outs,
        in_specs=[SMEM] * len(scalars) + [VMEM] * len(arrays),
        out_specs=[VMEM] * len(outs),
        scratch_shapes=scratch,
        compiler_params=params(size),
        cost_estimate=estimate,
        name=name,
    )(*scalars, *arrays)


def one_head(refs, head):
    return [ref.at[(slice(None),) * (ref.ndim - 1) + (pl.ds(head * HD, HD),)] for ref in refs]


def split_refs(refs, counts):
    refs, taken = list(refs), []
    for count in counts:
        taken.append(refs[:count])
        refs = refs[count:]
    return taken, refs


def copied(*copies):
    for copy in copies:
        copy.start()
    for copy in copies:
        copy.wait()


def pack_kv(keys, values, meta, group, width):
    rows = keys.shape[0]

    def body(meta_ref, k_ref, v_ref, *refs):
        outs, (k_in, v_in, sems) = refs[:group], refs[group:]
        me = meta_ref[0]
        copied(
            pltpu.make_async_copy(k_ref, k_in, sems.at[0]),
            pltpu.make_async_copy(v_ref, v_in, sems.at[1]),
        )
        for k in range(group):
            at = pl.ds(pl.multiple_of((me ^ k) * width, width), width)
            outs[k][0] = k_in[:, at]
            outs[k][1] = v_in[:, at]

    return pl.pallas_call(
        body,
        out_shape=[shape((2, rows, width))] * group,
        in_specs=[SMEM, HBM, HBM],
        out_specs=[VMEM] * group,
        scratch_shapes=[
            pltpu.VMEM(keys.shape, jnp.bfloat16),
            pltpu.VMEM(keys.shape, jnp.bfloat16),
            pltpu.SemaphoreType.DMA((2,)),
        ],
        compiler_params=params(60),
        cost_estimate=cost(0, 4 * keys.size * 2),
        name="pack_kv",
    )(meta, keys, values)


def grads_packed(queries, out_grad, proj_weight, meta, group, parts):
    rows, depth = out_grad.shape
    columns = queries.shape[1]
    width = columns // group
    each = depth // (group * parts)
    half = parts // 2
    chunks = 8
    step = depth // chunks
    assert rows == width

    def body(meta_ref, q_ref, og_ref, w_ref, *refs):
        outs, (q, og, w, total, sems, w_sems) = refs[:group], refs[group:]
        me, core = meta_ref[0], meta_ref[2]
        og_copy = pltpu.make_async_copy(og_ref, og, sems.at[0])
        q_copy = pltpu.make_async_copy(q_ref, q, sems.at[1])
        og_copy.start()
        w_copies = []
        for c in range(chunks):
            at = slice(c * step, (c + 1) * step)
            w_copies.append(pltpu.make_async_copy(w_ref.at[at, :], w.at[at, :], w_sems.at[c]))
            w_copies[c].start()
        q_copy.start()
        og_copy.wait()
        for k in range(group):
            for part in range(half):
                at = ((core * half + part) * group + (me ^ k)) * each
                at = pl.multiple_of(at, each)
                to = 2 * rows + part * each
                outs[k][to : to + each, :] = og[:, pl.ds(at, each)].T
        for c in range(chunks):
            at = slice(c * step, (c + 1) * step)
            w_copies[c].wait()
            got = dot(og[:, at], w[at, :], NN)
            if c == 0:
                total[...] = got
            else:
                total[...] += got
        q_copy.wait()
        for k in range(group):
            at = pl.ds(pl.multiple_of((me ^ k) * width, width), width)
            outs[k][:rows, :] = q[:, at]
            outs[k][rows : 2 * rows, :] = total[:, at].astype(jnp.bfloat16)

    return pl.pallas_call(
        body,
        out_shape=[shape((2 * rows + half * each, rows))] * group,
        in_specs=[SMEM, HBM, HBM, HBM],
        out_specs=[VMEM] * group,
        scratch_shapes=[
            pltpu.VMEM((rows, columns), jnp.bfloat16),
            pltpu.VMEM((rows, depth), jnp.bfloat16),
            pltpu.VMEM((depth, columns), jnp.bfloat16),
            pltpu.VMEM((rows, columns), jnp.float32),
            pltpu.SemaphoreType.DMA((2,)),
            pltpu.SemaphoreType.DMA((chunks,)),
        ],
        compiler_params=params(60),
        cost_estimate=cost(2 * rows * depth * columns, 12 * 1024 * 1024),
        name="attn_grad",
    )(meta, queries, out_grad, proj_weight)


def assemble_kv(pieces, meta, group):
    rows, width = pieces[0].shape[1:]

    def body(meta_ref, *refs):
        me = meta_ref[0]
        pool, strided, sems = refs[group:]
        copies = []
        for k in range(group):
            at = pl.ds(pl.multiple_of((me ^ k) * rows, rows), rows)
            copies.append(pltpu.make_async_copy(refs[k], pool.at[:, at, :], sems.at[k]))
        copied(*copies)
        strided[...] = pool[:, pl.ds(pl.multiple_of(meta_ref[2] * BLK, BLK), BLK), :]

    return pl.pallas_call(
        body,
        out_shape=[
            shape((2, group * rows, width)),
            shape((2, BLK, width)),
        ],
        in_specs=[SMEM] + [ANY] * group,
        out_specs=[VMEM] * 2,
        scratch_shapes=[pltpu.SemaphoreType.DMA((group,))],
        compiler_params=params(16),
        cost_estimate=cost(0, 3 * MIB),
        name="assemble_kv",
    )(meta, *pieces)


def assemble(pieces, meta, group):
    rows = pieces[0].shape[1]
    height = pieces[0].shape[0] - 2 * rows

    def body(meta_ref, *refs):
        me = meta_ref[0]
        qd, og, sems = refs[group:]
        copies = []
        for k in range(group):
            at = pl.ds(pl.multiple_of((me ^ k) * rows, rows), rows)
            parts = (
                (pl.ds(0, rows), qd.at[0, at, :]),
                (pl.ds(rows, rows), qd.at[1, at, :]),
                (pl.ds(2 * rows, height), og.at[:, at]),
            )
            for which, (source, target) in enumerate(parts):
                copies.append(
                    pltpu.make_async_copy(refs[k].at[source, :], target, sems.at[k, which])
                )
        copied(*copies)

    return pl.pallas_call(
        body,
        out_shape=[shape((2, group * rows, rows)), shape((height, group * rows))],
        in_specs=[SMEM] + [ANY] * group,
        out_specs=[VMEM] * 2,
        scratch_shapes=[pltpu.SemaphoreType.DMA((group, 3))],
        compiler_params=params(16),
        cost_estimate=cost(0, 4 * MIB),
        name="assemble",
    )(meta, *pieces)


def masks_of(layout, meta, parts, slots):
    width = layout.shape[1]
    pairs = LOCAL // 2

    def body(meta_ref, table, own_ref, next_ref):
        at_group = meta_ref[1]
        low_half = lax.broadcasted_iota(jnp.int32, (1, PAIR), 1) < BLK

        def bits_of(group_at, row):
            block = group_at * LOCAL + row
            base = block - row % 2 - (LOCAL - 1)
            at = jnp.minimum(block, table.shape[0] - 1)
            bits = jnp.int32(0)
            for c in range(width):
                entry = table[at, c]
                near = entry >= jnp.maximum(block - (LOCAL - 1), 0)
                place = jnp.where(near, entry - base, SPAN + jnp.maximum(entry, 0) // STRIDE)
                bit = jnp.left_shift(jnp.int32(1), place)
                bits = bits | jnp.where(entry >= 0, bit, 0)
            return jnp.where(group_at < parts, bits, 0)

        def row_of(first, second, place):
            one = jnp.where((jnp.right_shift(first, place) & 1) == 1, 0.0, -jnp.inf)
            two = jnp.where((jnp.right_shift(second, place) & 1) == 1, 0.0, -jnp.inf)
            return jnp.where(low_half, one, two).astype(jnp.float32)

        for t in range(pairs):
            first, second = bits_of(at_group, 2 * t), bits_of(at_group, 2 * t + 1)
            for place in range(SPAN + slots):
                own_ref[t, place : place + 1, :] = row_of(first, second, place)
            first, second = bits_of(at_group + 1, 2 * t), bits_of(at_group + 1, 2 * t + 1)
            for place in range(SPAN):
                next_ref[t, place : place + 1, :] = row_of(first, second, place)
            even = at_group % 2 == 0
            place = SPAN + at_group // 2
            first, second = jnp.where(even, first, 0), jnp.where(even, second, 0)
            next_ref[t, SPAN : SPAN + 1, :] = row_of(first, second, place)

    return call(
        body, (meta, layout), (),
        [
            shape((pairs, SPAN + slots, PAIR), jnp.float32),
            shape((pairs, SPAN + 1, PAIR), jnp.float32),
        ],
        [], cost(0, 128 * 1024), "masks",
    )


def fill_pools(meta_ref, own, prev, far, k_pool, v_pool, slots):
    at_group, offset = meta_ref[1], meta_ref[2]
    whole = own.shape[1]
    k_pool[:whole, :] = prev[0]
    v_pool[:whole, :] = prev[1]
    k_pool[whole : 2 * whole, :] = own[0]
    v_pool[whole : 2 * whole, :] = own[1]
    tail = jnp.zeros((slots * BLK, k_pool.shape[1]), k_pool.dtype)
    k_pool[2 * whole :, :] = tail
    v_pool[2 * whole :, :] = tail

    @pl.when(at_group % 2 == 1)
    def _():
        to = pl.multiple_of(2 * whole + (at_group // 2) * BLK, BLK)
        start = pl.multiple_of(offset * BLK, BLK)
        k_pool[pl.ds(to, BLK), :] = k_pool[pl.ds(start, BLK), :]
        v_pool[pl.ds(to, BLK), :] = v_pool[pl.ds(start, BLK), :]

    for index, ref in enumerate(far):
        distance = index + 2

        @pl.when((at_group >= distance) & ((at_group - distance) % 2 == 0))
        def _():
            to = pl.multiple_of(2 * whole + ((at_group - distance) // 2) * BLK, BLK)
            k_pool[pl.ds(to, BLK), :] = ref[0]
            v_pool[pl.ds(to, BLK), :] = ref[1]


def causal_masks():
    key_at = lax.broadcasted_iota(jnp.int32, (BLK, PAIR), 0)
    query_at = lax.broadcasted_iota(jnp.int32, (BLK, PAIR), 1)
    first = (key_at <= query_at) | (query_at >= BLK)
    second = key_at <= query_at - BLK
    return first, second


def masked_scores(keys, query, bias, masks):
    raw = dot(keys, query, NT) * SCALE2
    tiles = []
    for j in range(keys.shape[0] // BLK):
        tile = raw[j * BLK : (j + 1) * BLK] + bias[j]
        if masks is not None and j in (LOCAL - 1, LOCAL):
            tile = jnp.where(masks[j - LOCAL + 1], tile, -jnp.inf)
        tiles.append(tile)
    return jnp.concatenate(tiles, axis=0)


def bias_rows(bias_ref, t, picked):
    return [bias_ref[t, j : j + 1, :] for j in picked]


def forward(head, qd, own, prev, far, bias, stats, meta, group, slots):
    whole = qd.shape[1]
    pairs = whole // PAIR
    counts = (3, len(far))

    def body(meta_ref, bias_ref, before_ref, *refs):
        (around, far_refs), refs = split_refs(refs, counts)
        qd_ref, *around = one_head(around, head)
        far_refs = one_head(far_refs, head)
        out_ref, stats_ref, k_pool, v_pool = refs
        fill_pools(meta_ref, *around, far_refs, k_pool, v_pool, slots)
        stats_ref[...] = before_ref[...]
        masks = causal_masks()
        for t in range(pairs):
            here = slice(t * PAIR, (t + 1) * PAIR)
            window = slice(t * PAIR + BLK, t * PAIR + BLK + SPAN * BLK)
            keys = jnp.concatenate([k_pool[window, :], k_pool[2 * whole :, :]], axis=0)
            vals = jnp.concatenate([v_pool[window, :], v_pool[2 * whole :, :]], axis=0)
            s = masked_scores(keys, qd_ref[0, here, :], bias_rows(bias_ref, t, range(SPAN + slots)), masks)
            top = jnp.max(s, axis=0, keepdims=True)
            e = jnp.exp2(s - top)
            total = jnp.sum(e, axis=0, keepdims=True)
            low = (e * (1.0 / total)).astype(jnp.bfloat16)
            out = dot(low, vals, TN).astype(jnp.bfloat16)
            out_ref[here, :] = out
            product = out.astype(jnp.float32) * qd_ref[1, here, :].astype(jnp.float32)
            stats_ref[t, 2 * head : 2 * head + 1, :] = top + jnp.log2(total)
            stats_ref[t, 2 * head + 1 : 2 * head + 2, :] = jnp.sum(product.T, axis=0, keepdims=True)

    span = (SPAN + slots) * BLK
    return call(
        body, (meta,), (bias, stats, qd, own, prev, *far),
        [shape((whole, HD)), shape(stats.shape, jnp.float32)],
        [pltpu.VMEM((2 * whole + slots * BLK, HD), jnp.bfloat16)] * 2,
        cost(4 * whole * span * HD * 2, 3 * 1024 * 1024, whole * span),
        f"attention_{head}", 24,
    )


def backward(head, qd, own, prev, far, before, bias, stats, meta, group, slots):
    whole, width = qd.shape[1:]
    pairs = whole // PAIR
    counts = (3, len(far), len(before))
    everything = 2 * whole + slots * BLK

    def body(meta_ref, bias_ref, stats_ref, *refs):
        (around, far_refs, before_refs), refs = split_refs(refs, counts)
        qd_ref, *around = one_head(around, head)
        far_refs = one_head(far_refs, head)
        ((dq_ref, grad_ref), far_outs), refs = split_refs(refs, (2, len(far)))
        k_pool, v_pool, far_sum = refs
        at_group = meta_ref[1]
        fill_pools(meta_ref, *around, far_refs, k_pool, v_pool, slots)
        masks = causal_masks()
        grad_ref[...] = jnp.zeros_like(grad_ref)
        far_sum[...] = jnp.zeros_like(far_sum)
        for t in range(pairs):
            here = slice(t * PAIR, (t + 1) * PAIR)
            window = slice(t * PAIR + BLK, t * PAIR + BLK + SPAN * BLK)
            others = max(whole - (t * PAIR + BLK), 0)
            end = SPAN * BLK
            mine = slice(t * PAIR + BLK + others - whole, t * PAIR + BLK + end - whole)
            keys = jnp.concatenate([k_pool[window, :], k_pool[2 * whole :, :]], axis=0)
            vals = jnp.concatenate([v_pool[window, :], v_pool[2 * whole :, :]], axis=0)
            query, grad = qd_ref[0, here, :], qd_ref[1, here, :]
            s = masked_scores(keys, query, bias_rows(bias_ref, t, range(SPAN + slots)), masks)
            probs = jnp.exp2(s - stats_ref[t, 2 * head : 2 * head + 1, :])
            delta = stats_ref[t, 2 * head + 1 : 2 * head + 2, :]
            ds = (probs * (dot(vals, grad, NT) - delta)).astype(jnp.bfloat16)
            low = probs.astype(jnp.bfloat16)
            dq_ref[here, :] = (dot(ds, keys, TN) * SCALE).astype(jnp.bfloat16)
            grad_ref[0, mine, :] += dot(ds[others:end], query, NN)
            grad_ref[1, mine, :] += dot(low[others:end], grad, NN)
            far_sum[0] += dot(ds[end:], query, NN)
            far_sum[1] += dot(low[end:], grad, NN)
        for index, ref in enumerate(far_outs):
            slot = jnp.maximum(at_group - index - 2, 0) // 2
            start = pl.multiple_of(slot * BLK, BLK)
            ref[...] = before_refs[index][...]
            lanes = slice(head * HD, (head + 1) * HD)
            ref[0, :, lanes] = (far_sum[0, pl.ds(start, BLK), :] * SCALE).astype(jnp.bfloat16)
            ref[1, :, lanes] = far_sum[1, pl.ds(start, BLK), :].astype(jnp.bfloat16)

    span = (SPAN + slots) * BLK
    outs = call(
        body, (meta,), (bias, stats, qd, own, prev, *far, *before),
        [shape((whole, HD)), shape((2, whole, HD), jnp.float32)]
        + [shape((2, BLK, width))] * len(far),
        [
            pltpu.VMEM((everything, HD), jnp.bfloat16),
            pltpu.VMEM((everything, HD), jnp.bfloat16),
            pltpu.VMEM((2, slots * BLK, HD), jnp.float32),
        ],
        cost(8 * whole * span * HD * 2, 4 * 1024 * 1024, whole * span),
        f"attention_back_{head}", 24,
    )
    return outs[0], outs[1], outs[2:]


def backward_next(grads, qd, own, bias, stats, meta):
    whole, width = qd.shape[1:]
    heads = width // HD
    pairs = whole // PAIR

    def body(meta_ref, bias_ref, stats_ref, *refs):
        (grad_refs, (qd_ref, own_ref, out)), refs = split_refs(refs, (heads, 3))
        strided = pl.ds(pl.multiple_of(meta_ref[2] * BLK, BLK), BLK)
        for h in range(heads):
            lanes = slice(h * HD, (h + 1) * HD)
            out[0, :, lanes] = grad_refs[h][0]
            out[1, :, lanes] = grad_refs[h][1]
            for t in range(pairs):
                here = slice(t * PAIR, (t + 1) * PAIR)
                window = slice(t * PAIR + BLK, whole)
                near = (whole - BLK) // BLK - t * (PAIR // BLK)
                keys = jnp.concatenate([own_ref[0, window, lanes], own_ref[0, strided, lanes]], axis=0)
                vals = jnp.concatenate([own_ref[1, window, lanes], own_ref[1, strided, lanes]], axis=0)
                query, grad = qd_ref[0, here, lanes], qd_ref[1, here, lanes]
                rows_here = bias_rows(bias_ref, t, list(range(near)) + [SPAN])
                s = masked_scores(keys, query, rows_here, None)
                probs = jnp.exp2(s - stats_ref[t, 2 * h : 2 * h + 1, :])
                delta = stats_ref[t, 2 * h + 1 : 2 * h + 2, :]
                ds = (probs * (dot(vals, grad, NT) - delta)).astype(jnp.bfloat16)
                dk = dot(ds, query, NN)
                dv = dot(probs.astype(jnp.bfloat16), grad, NN)
                out[0, window, lanes] += dk[: near * BLK]
                out[1, window, lanes] += dv[: near * BLK]
                out[0, strided, lanes] += dk[near * BLK :]
                out[1, strided, lanes] += dv[near * BLK :]
        out[0] = out[0] * SCALE

    return call(
        body, (meta,), (bias, stats, *grads, qd, own),
        [shape((2, whole, width), jnp.float32)], [],
        cost(8 * whole * 5 * BLK * width, 7 * 1024 * 1024, whole * 5 * BLK * heads),
        "attention_back_next", 24,
    )[0]


def combine(dq, own, far, meta, group, rows):
    whole, width = own.shape[1:]

    def body(meta_ref, own_ref, *refs):
        (dq_refs, far_refs, outs, (acc,)), refs = split_refs(refs, (len(dq), len(far), group, 1))
        me, offset = meta_ref[0], meta_ref[2]
        acc[...] = own_ref[...]
        at = pl.multiple_of(offset * BLK, BLK)
        for ref in far_refs:
            acc[:, pl.ds(at, BLK), :] += ref[...].astype(jnp.float32)
        for k in range(group):
            here = pl.ds(pl.multiple_of((me ^ k) * rows, rows), rows)
            for h in range(len(dq)):
                outs[k][0, :, h * HD : (h + 1) * HD] = dq_refs[h][here, :]
            outs[k][1] = acc[0, here, :].astype(jnp.bfloat16)
            outs[k][2] = acc[1, here, :].astype(jnp.bfloat16)

    return call(
        body, (meta,), (own, *dq, *far), [shape((3, rows, width))] * group,
        [pltpu.VMEM((2, whole, width), jnp.float32)],
        cost(0, 4 * 1024 * 1024), "combine",
    )


def project(head, mine, theirs, attn, before, meta, group, parts):
    height, whole = mine.shape
    each = 2 * height // parts
    full = group * HD
    more = parts // 2 - 1

    def body(meta_ref, mine_ref, theirs_ref, *refs):
        (attn_refs, before_refs, outs), refs = split_refs(refs, (group, len(before), 6))
        keep, first, odds, evens, pool, total = outs
        for ref in before_refs:
            first[:head] = ref[...]
        me, at_group, core = meta_ref[0], meta_ref[1], meta_ref[3]
        for k in range(group):
            at = pl.multiple_of((me ^ k) * HD, HD)
            pool[:, pl.ds(at, HD)] = attn_refs[k][...]
        upper = pl.ds(pl.multiple_of(core * height, height), height)
        lower = pl.ds(pl.multiple_of((1 - core) * height, height), height)
        total[upper, :] = dot(mine_ref[...], pool[...], NN)
        total[lower, :] = dot(theirs_ref[...], pool[...], NN)
        for m in range(parts):
            part = total[pl.ds(pl.multiple_of((at_group ^ m) * each, each), each), :]
            if m == 0:
                keep[...] = part
            elif m == 1:
                first[head] = part.astype(jnp.bfloat16)
            elif m % 2 == 1:
                odds[m // 2 - 1] = part.astype(jnp.bfloat16)
            else:
                evens[m // 2 - 1] = part

    return call(
        body, (meta,), (mine, theirs, *attn, *before),
        [
            shape((each, full), jnp.float32),
            shape((head + 1, each, full)),
            shape((more, each, full)),
            shape((more, each, full), jnp.float32),
        ],
        [pltpu.VMEM((whole, full), jnp.bfloat16), pltpu.VMEM((2 * height, full), jnp.float32)],
        cost(4 * height * whole * full, 6 * 1024 * 1024), f"project_{head}",
    )


def halve(head, evens, arrived):
    count, each, full = evens.shape
    more = (count - 1) // 2

    def body(evens_ref, arrived_ref, first, *rest):
        for m in range(1, count + 1):
            summed = evens_ref[m - 1] + arrived_ref[m - 1].astype(jnp.float32)
            if m == 1:
                first[...] = summed.astype(jnp.bfloat16)
            elif m % 2 == 1:
                rest[0][m // 2 - 1] = summed.astype(jnp.bfloat16)
            else:
                rest[1][m // 2 - 1] = summed

    others = [shape((more, each, full)), shape((more, each, full), jnp.float32)]
    return call(
        body, (), (evens, arrived), [shape((each, full))] + (others if more else []), [],
        cost(0, 3 * 1024 * 1024), f"halve_{head}",
    )


def finish(keep, neighbour, arrived, group):
    heads = len(keep)
    count = len(arrived[0])
    each = keep[0].shape[0]

    def body(*refs):
        (keep_refs, arrived_refs, (first, out)), refs = split_refs(refs, (heads, heads * count, 2))
        for h in range(heads):
            total = keep_refs[h][...] + first[h].astype(jnp.float32)
            for ref in arrived_refs[h * count : (h + 1) * count]:
                total = total + ref[...].astype(jnp.float32)
            for j in range(group):
                at = (j * heads + h) * HD
                out[:, at : at + HD] = total[:, j * HD : (j + 1) * HD]

    flat = [piece for pieces in arrived for piece in pieces]
    return call(
        body, (), (*keep, *flat, neighbour),
        [shape((each, group * heads * HD), jnp.float32)], [],
        cost(0, 3 * 1024 * 1024), "finish",
    )[0]


def unpack(pieces, meta, group):
    rows, width = pieces[0].shape[1:]

    def body(meta_ref, *refs):
        me = meta_ref[0]
        outs, sems = refs[group:-1], refs[-1]
        copies = []
        for k in range(group):
            at = pl.ds(pl.multiple_of((me ^ k) * width, width), width)
            for which in range(3):
                target = outs[which].at[:, at]
                copies.append(
                    pltpu.make_async_copy(refs[k].at[which], target, sems.at[k, which])
                )
        copied(*copies)

    return pl.pallas_call(
        body,
        out_shape=[shape((rows, group * width))] * 3,
        in_specs=[SMEM] + [ANY] * group,
        out_specs=[ANY] * 3,
        scratch_shapes=[pltpu.SemaphoreType.DMA((group, 3))],
        compiler_params=params(16),
        cost_estimate=cost(0, 3 * MIB),
        name="unpack",
    )(meta, *pieces)


def after(value, *others):
    return lax.optimization_barrier((value, *others))[0]


def local(devices, queries, keys, values, out_grad, proj_weight, layout):
    rows, columns = queries.shape
    group = LOCAL * BLK // rows
    parts = devices // group
    width = columns // group
    heads = width // HD
    blocks = layout.shape[0]
    slots = blocks // STRIDE
    position = lax.axis_index("seq")
    me, at_group = position % group, position // group
    core = lax.axis_index("head")
    offset = layout[blocks - 1, 0] % STRIDE
    place = jnp.stack([me, at_group, core]).astype(jnp.int32)
    meta = jnp.stack([me, at_group, offset, core]).astype(jnp.int32)

    def swap(piece, k):
        route = [(i, (i // group) * group + ((i % group) ^ k)) for i in range(devices)]
        return lax.ppermute(piece, "seq", route)

    def shifted(piece, distance):
        route = [
            (i, i + distance * group)
            for i in range(devices)
            if 0 <= i + distance * group < devices
        ]
        return lax.ppermute(piece, "seq", route)

    def swap_groups(piece, bit):
        route = [(i, ((i // group) ^ bit) * group + i % group) for i in range(devices)]
        return lax.ppermute(piece, "seq", route)

    def summary_route(distance, back):
        route = [
            (i, i + distance * group)
            for i in range(devices - distance * group)
            if (i // group) % 2 == 0
        ]
        return [(b, a) for a, b in route] if back else route

    def exchange(pieces):
        return [pieces[0]] + [swap(pieces[k], k) for k in range(1, group)]

    def add_up(head, odds, evens, before, token):
        arrivals, bit = [], 2
        odds = after(odds, *jax.tree.leaves(before))
        while True:
            first, *more = halve(head, evens, odds)
            token = after(token, first)
            done = first
            arrivals.append(swap_groups(first, bit))
            if not more:
                return arrivals, token, done
            odds, evens = swap_groups(more[0], bit), more[1]
            bit *= 2

    kv = pack_kv(keys, values, place, group, width)
    own_kv = exchange(kv)
    early = after(place, own_kv[1])
    qd_cut = grads_packed(queries, out_grad, proj_weight, early, group, parts)
    pool, strided = assemble_kv(own_kv, after(meta, qd_cut[0]), group)
    prev = shifted(pool, 1)
    qd_pieces = exchange(qd_cut)
    later = after(strided, qd_pieces[1])
    far = [
        lax.ppermute(
            strided if distance == 2 else later, "seq", summary_route(distance, False)
        )
        for distance in range(2, parts)
    ]
    bias, bias_next = masks_of(layout, after(meta, strided), parts, slots)
    qd, mine = assemble(qd_pieces, after(meta, bias, prev, *far), group)
    theirs = lax.ppermute(mine, "head", [(0, 1), (1, 0)])
    next_qd = shifted(qd, -1)

    stats = jnp.zeros((LOCAL // 2, 2 * heads, PAIR), jnp.float32)
    order = meta
    attn = []
    for h in range(heads):
        got, stats = forward(h, qd, pool, prev, far, bias, stats, order, group, slots)
        attn.append([got] + [swap(got, k) for k in range(1, group)])
        order = after(meta, got, theirs)

    dq, grads, keep, finals = [], [], [], []
    far_grads = [jnp.zeros((2, BLK, width), jnp.bfloat16) for _ in far]
    order, first = after(meta, stats, theirs), []
    for h in range(heads):
        got = backward(h, qd, pool, prev, far, far_grads, bias, stats, order, group, slots)
        dq.append(got[0])
        grads.append(got[1])
        far_grads = got[2]
        order = after(meta, got[0])
        kept, first, odds, evens = project(h, mine, theirs, attn[h], first, order, group, parts)
        keep.append(kept)
        first, odds = [first], swap_groups(odds, 1)
        order = after(meta, *first)
        if h == 0:
            next_stats = shifted(after(stats, next_qd, *first), -1)
        if h < heads - 1:
            sums, order, _ = add_up(h, odds, evens, first, order)
            finals.append(sums)
    far_back = [
        lax.ppermute(piece, "seq", summary_route(index + 2, True))
        for index, piece in enumerate(far_grads)
    ]
    order = after(order, finals[0])
    own_grad = backward_next(grads, next_qd, pool, bias_next, next_stats, order)
    final_cut = combine(dq, own_grad, far_back, meta, group, rows)
    final = exchange(final_cut)
    sums, _, _ = add_up(heads - 1, odds, evens, final_cut, meta)
    finals.append(sums)
    neighbour = swap_groups(after(first[0], final_cut[0]), 1)
    proj_grad = finish(keep, neighbour, finals, group)
    query_grad, key_grad, value_grad = unpack(final, meta, group)
    return (query_grad, key_grad, value_grad, proj_grad)


def solution(mesh):
    split = P(("dp", "seq"), "head")
    return jax.shard_map(
        functools.partial(local, mesh.shape["seq"]),
        mesh=mesh,
        in_specs=(split, split, split, P(("dp", "seq"), None), P(None, "head"), P()),
        out_specs=(split, split, split, split),
        check_vma=False,
    )
```

```python
import functools
import math

import jax
import jax.numpy as jnp
from jax import lax
from jax.experimental import pallas as pl
from jax.experimental.pallas import tpu as pltpu
from jax.sharding import PartitionSpec as P

HD = 128
BLK = 128
LOCAL = 8
STRIDE = 16
PAIR = 2 * BLK
SPAN = LOCAL + 1
SCALE = HD ** (-0.5)
SCALE2 = SCALE * math.log2(math.e)
MIB = 1024 * 1024

NT = (((1,), (1,)), ((), ()))
NN = (((1,), (0,)), ((), ()))
TN = (((0,), (0,)), ((), ()))
SMEM = pl.BlockSpec(memory_space=pltpu.SMEM)
VMEM = pl.BlockSpec(memory_space=pltpu.VMEM)
HBM = pl.BlockSpec(memory_space=pltpu.HBM)
ANY = pl.BlockSpec(memory_space=pl.ANY)


def shape(dims, dtype=jnp.bfloat16):
    return jax.ShapeDtypeStruct(dims, dtype)


def dot(a, b, dims):
    return lax.dot_general(a, b, dims, preferred_element_type=jnp.float32)


def params(size):
    return pltpu.CompilerParams(vmem_limit_bytes=size * MIB)


def cost(flops, size, exps=0):
    return pl.CostEstimate(flops=1, bytes_accessed=1, transcendentals=0)


def call(body, scalars, arrays, outs, scratch, estimate, name, size=16):
    return pl.pallas_call(
        body,
        out_shape=outs,
        in_specs=[SMEM] * len(scalars) + [VMEM] * len(arrays),
        out_specs=[VMEM] * len(outs),
        scratch_shapes=scratch,
        compiler_params=params(size),
        cost_estimate=estimate,
        name=name,
    )(*scalars, *arrays)


def one_head(refs, head):
    return [ref.at[(slice(None),) * (ref.ndim - 1) + (pl.ds(head * HD, HD),)] for ref in refs]


def split_refs(refs, counts):
    refs, taken = list(refs), []
    for count in counts:
        taken.append(refs[:count])
        refs = refs[count:]
    return taken, refs


def copied(*copies):
    for copy in copies:
        copy.start()
    for copy in copies:
        copy.wait()


def pack_kv(keys, values, meta, group, width):
    rows = keys.shape[0]

    def body(meta_ref, k_ref, v_ref, *refs):
        outs, (k_in, v_in, sems) = refs[:group], refs[group:]
        me = meta_ref[0]
        copied(
            pltpu.make_async_copy(k_ref, k_in, sems.at[0]),
            pltpu.make_async_copy(v_ref, v_in, sems.at[1]),
        )
        for k in range(group):
            at = pl.ds(pl.multiple_of((me ^ k) * width, width), width)
            outs[k][0] = k_in[:, at]
            outs[k][1] = v_in[:, at]

    return pl.pallas_call(
        body,
        out_shape=[shape((2, rows, width))] * group,
        in_specs=[SMEM, HBM, HBM],
        out_specs=[VMEM] * group,
        scratch_shapes=[
            pltpu.VMEM(keys.shape, jnp.bfloat16),
            pltpu.VMEM(keys.shape, jnp.bfloat16),
            pltpu.SemaphoreType.DMA((2,)),
        ],
        compiler_params=params(60),
        cost_estimate=cost(0, 4 * keys.size * 2),
        name="pack_kv",
    )(meta, keys, values)


def grads_packed(queries, out_grad, proj_weight, meta, group, parts):
    rows, depth = out_grad.shape
    columns = queries.shape[1]
    width = columns // group
    each = depth // (group * parts)
    half = parts // 2
    chunks = 8
    step = depth // chunks
    assert rows == width

    def body(meta_ref, q_ref, og_ref, w_ref, *refs):
        outs, (q, og, w, total, sems, w_sems) = refs[:group], refs[group:]
        me, core = meta_ref[0], meta_ref[2]
        og_copy = pltpu.make_async_copy(og_ref, og, sems.at[0])
        q_copy = pltpu.make_async_copy(q_ref, q, sems.at[1])
        og_copy.start()
        w_copies = []
        for c in range(chunks):
            at = slice(c * step, (c + 1) * step)
            w_copies.append(pltpu.make_async_copy(w_ref.at[at, :], w.at[at, :], w_sems.at[c]))
            w_copies[c].start()
        q_copy.start()
        og_copy.wait()
        for k in range(group):
            for part in range(half):
                at = ((core * half + part) * group + (me ^ k)) * each
                at = pl.multiple_of(at, each)
                to = 2 * rows + part * each
                outs[k][to : to + each, :] = og[:, pl.ds(at, each)].T
        for c in range(chunks):
            at = slice(c * step, (c + 1) * step)
            w_copies[c].wait()
            got = dot(og[:, at], w[at, :], NN)
            if c == 0:
                total[...] = got
            else:
                total[...] += got
        q_copy.wait()
        for k in range(group):
            at = pl.ds(pl.multiple_of((me ^ k) * width, width), width)
            outs[k][:rows, :] = q[:, at]
            outs[k][rows : 2 * rows, :] = total[:, at].astype(jnp.bfloat16)

    return pl.pallas_call(
        body,
        out_shape=[shape((2 * rows + half * each, rows))] * group,
        in_specs=[SMEM, HBM, HBM, HBM],
        out_specs=[VMEM] * group,
        scratch_shapes=[
            pltpu.VMEM((rows, columns), jnp.bfloat16),
            pltpu.VMEM((rows, depth), jnp.bfloat16),
            pltpu.VMEM((depth, columns), jnp.bfloat16),
            pltpu.VMEM((rows, columns), jnp.float32),
            pltpu.SemaphoreType.DMA((2,)),
            pltpu.SemaphoreType.DMA((chunks,)),
        ],
        compiler_params=params(60),
        cost_estimate=cost(2 * rows * depth * columns, 12 * 1024 * 1024),
        name="attn_grad",
    )(meta, queries, out_grad, proj_weight)


def assemble_kv(pieces, meta, group):
    rows, width = pieces[0].shape[1:]

    def body(meta_ref, *refs):
        me = meta_ref[0]
        pool, strided, sems = refs[group:]
        copies = []
        for k in range(group):
            at = pl.ds(pl.multiple_of((me ^ k) * rows, rows), rows)
            copies.append(pltpu.make_async_copy(refs[k], pool.at[:, at, :], sems.at[k]))
        copied(*copies)
        strided[...] = pool[:, pl.ds(pl.multiple_of(meta_ref[2] * BLK, BLK), BLK), :]

    return pl.pallas_call(
        body,
        out_shape=[
            shape((2, group * rows, width)),
            shape((2, BLK, width)),
        ],
        in_specs=[SMEM] + [ANY] * group,
        out_specs=[VMEM] * 2,
        scratch_shapes=[pltpu.SemaphoreType.DMA((group,))],
        compiler_params=params(16),
        cost_estimate=cost(0, 3 * MIB),
        name="assemble_kv",
    )(meta, *pieces)


def assemble(pieces, meta, group):
    rows = pieces[0].shape[1]
    height = pieces[0].shape[0] - 2 * rows

    def body(meta_ref, *refs):
        me = meta_ref[0]
        qd, og = refs[group:]
        for k in range(group):
            at = pl.ds(pl.multiple_of((me ^ k) * rows, rows), rows)
            qd[0, at, :] = refs[k][:rows, :]
            qd[1, at, :] = refs[k][rows : 2 * rows, :]
            og[:, at] = refs[k][2 * rows :, :]

    return call(
        body, (meta,), tuple(pieces),
        [shape((2, group * rows, rows)), shape((height, group * rows))], [],
        cost(0, 4 * MIB), "assemble",
    )


def masks_of(layout, meta, parts, slots):
    width = layout.shape[1]
    pairs = LOCAL // 2

    def body(meta_ref, table, own_ref, next_ref):
        at_group = meta_ref[1]
        low_half = lax.broadcasted_iota(jnp.int32, (1, PAIR), 1) < BLK

        def bits_of(group_at, row):
            block = group_at * LOCAL + row
            base = block - row % 2 - (LOCAL - 1)
            at = jnp.minimum(block, table.shape[0] - 1)
            bits = jnp.int32(0)
            for c in range(width):
                entry = table[at, c]
                near = entry >= jnp.maximum(block - (LOCAL - 1), 0)
                place = jnp.where(near, entry - base, SPAN + jnp.maximum(entry, 0) // STRIDE)
                bit = jnp.left_shift(jnp.int32(1), place)
                bits = bits | jnp.where(entry >= 0, bit, 0)
            return jnp.where(group_at < parts, bits, 0)

        def row_of(first, second, place):
            one = jnp.where((jnp.right_shift(first, place) & 1) == 1, 0.0, -jnp.inf)
            two = jnp.where((jnp.right_shift(second, place) & 1) == 1, 0.0, -jnp.inf)
            return jnp.where(low_half, one, two).astype(jnp.float32)

        for t in range(pairs):
            first, second = bits_of(at_group, 2 * t), bits_of(at_group, 2 * t + 1)
            for place in range(SPAN + slots):
                own_ref[t, place : place + 1, :] = row_of(first, second, place)
            first, second = bits_of(at_group + 1, 2 * t), bits_of(at_group + 1, 2 * t + 1)
            for place in range(SPAN):
                next_ref[t, place : place + 1, :] = row_of(first, second, place)
            even = at_group % 2 == 0
            place = SPAN + at_group // 2
            first, second = jnp.where(even, first, 0), jnp.where(even, second, 0)
            next_ref[t, SPAN : SPAN + 1, :] = row_of(first, second, place)

    return call(
        body, (meta, layout), (),
        [
            shape((pairs, SPAN + slots, PAIR), jnp.float32),
            shape((pairs, SPAN + 1, PAIR), jnp.float32),
        ],
        [], cost(0, 128 * 1024), "masks",
    )


def fill_pools(meta_ref, own, prev, far, k_pool, v_pool, slots):
    at_group, offset = meta_ref[1], meta_ref[2]
    whole = own.shape[1]
    k_pool[:whole, :] = prev[0]
    v_pool[:whole, :] = prev[1]
    k_pool[whole : 2 * whole, :] = own[0]
    v_pool[whole : 2 * whole, :] = own[1]
    tail = jnp.zeros((slots * BLK, k_pool.shape[1]), k_pool.dtype)
    k_pool[2 * whole :, :] = tail
    v_pool[2 * whole :, :] = tail

    @pl.when(at_group % 2 == 1)
    def _():
        to = pl.multiple_of(2 * whole + (at_group // 2) * BLK, BLK)
        start = pl.multiple_of(offset * BLK, BLK)
        k_pool[pl.ds(to, BLK), :] = k_pool[pl.ds(start, BLK), :]
        v_pool[pl.ds(to, BLK), :] = v_pool[pl.ds(start, BLK), :]

    for index, ref in enumerate(far):
        distance = index + 2

        @pl.when((at_group >= distance) & ((at_group - distance) % 2 == 0))
        def _():
            to = pl.multiple_of(2 * whole + ((at_group - distance) // 2) * BLK, BLK)
            k_pool[pl.ds(to, BLK), :] = ref[0]
            v_pool[pl.ds(to, BLK), :] = ref[1]


def causal_masks():
    key_at = lax.broadcasted_iota(jnp.int32, (BLK, PAIR), 0)
    query_at = lax.broadcasted_iota(jnp.int32, (BLK, PAIR), 1)
    first = (key_at <= query_at) | (query_at >= BLK)
    second = key_at <= query_at - BLK
    return first, second


def masked_scores(keys, query, bias, masks):
    raw = dot(keys, query, NT) * SCALE2
    tiles = []
    for j in range(keys.shape[0] // BLK):
        tile = raw[j * BLK : (j + 1) * BLK] + bias[j]
        if masks is not None and j in (LOCAL - 1, LOCAL):
            tile = jnp.where(masks[j - LOCAL + 1], tile, -jnp.inf)
        tiles.append(tile)
    return jnp.concatenate(tiles, axis=0)


def bias_rows(bias_ref, t, picked):
    return [bias_ref[t, j : j + 1, :] for j in picked]


def forward(head, qd, own, prev, far, bias, stats, meta, group, slots):
    whole = qd.shape[1]
    pairs = whole // PAIR
    counts = (3, len(far))

    def body(meta_ref, bias_ref, before_ref, *refs):
        (around, far_refs), refs = split_refs(refs, counts)
        qd_ref, *around = one_head(around, head)
        far_refs = one_head(far_refs, head)
        out_ref, stats_ref, k_pool, v_pool = refs
        fill_pools(meta_ref, *around, far_refs, k_pool, v_pool, slots)
        stats_ref[...] = before_ref[...]
        masks = causal_masks()
        for t in range(pairs):
            here = slice(t * PAIR, (t + 1) * PAIR)
            window = slice(t * PAIR + BLK, t * PAIR + BLK + SPAN * BLK)
            keys = jnp.concatenate([k_pool[window, :], k_pool[2 * whole :, :]], axis=0)
            vals = jnp.concatenate([v_pool[window, :], v_pool[2 * whole :, :]], axis=0)
            s = masked_scores(keys, qd_ref[0, here, :], bias_rows(bias_ref, t, range(SPAN + slots)), masks)
            top = jnp.max(s, axis=0, keepdims=True)
            e = jnp.exp2(s - top)
            total = jnp.sum(e, axis=0, keepdims=True)
            low = (e * (1.0 / total)).astype(jnp.bfloat16)
            out = dot(low, vals, TN).astype(jnp.bfloat16)
            out_ref[here, :] = out
            product = out.astype(jnp.float32) * qd_ref[1, here, :].astype(jnp.float32)
            stats_ref[t, 2 * head : 2 * head + 1, :] = top + jnp.log2(total)
            stats_ref[t, 2 * head + 1 : 2 * head + 2, :] = jnp.sum(product.T, axis=0, keepdims=True)

    span = (SPAN + slots) * BLK
    return call(
        body, (meta,), (bias, stats, qd, own, prev, *far),
        [shape((whole, HD)), shape(stats.shape, jnp.float32)],
        [pltpu.VMEM((2 * whole + slots * BLK, HD), jnp.bfloat16)] * 2,
        cost(4 * whole * span * HD * 2, 3 * 1024 * 1024, whole * span),
        f"attention_{head}", 24,
    )


def backward(head, qd, own, prev, far, before, bias, stats, meta, group, slots):
    whole, width = qd.shape[1:]
    pairs = whole // PAIR
    counts = (3, len(far), len(before))
    everything = 2 * whole + slots * BLK

    def body(meta_ref, bias_ref, stats_ref, *refs):
        (around, far_refs, before_refs), refs = split_refs(refs, counts)
        qd_ref, *around = one_head(around, head)
        far_refs = one_head(far_refs, head)
        ((dq_ref, grad_ref), far_outs), refs = split_refs(refs, (2, len(far)))
        k_pool, v_pool, far_sum = refs
        at_group = meta_ref[1]
        fill_pools(meta_ref, *around, far_refs, k_pool, v_pool, slots)
        masks = causal_masks()
        grad_ref[...] = jnp.zeros_like(grad_ref)
        far_sum[...] = jnp.zeros_like(far_sum)
        for t in range(pairs):
            here = slice(t * PAIR, (t + 1) * PAIR)
            window = slice(t * PAIR + BLK, t * PAIR + BLK + SPAN * BLK)
            others = max(whole - (t * PAIR + BLK), 0)
            end = SPAN * BLK
            mine = slice(t * PAIR + BLK + others - whole, t * PAIR + BLK + end - whole)
            keys = jnp.concatenate([k_pool[window, :], k_pool[2 * whole :, :]], axis=0)
            vals = jnp.concatenate([v_pool[window, :], v_pool[2 * whole :, :]], axis=0)
            query, grad = qd_ref[0, here, :], qd_ref[1, here, :]
            s = masked_scores(keys, query, bias_rows(bias_ref, t, range(SPAN + slots)), masks)
            probs = jnp.exp2(s - stats_ref[t, 2 * head : 2 * head + 1, :])
            delta = stats_ref[t, 2 * head + 1 : 2 * head + 2, :]
            ds = (probs * (dot(vals, grad, NT) - delta)).astype(jnp.bfloat16)
            low = probs.astype(jnp.bfloat16)
            dq_ref[here, :] = (dot(ds, keys, TN) * SCALE).astype(jnp.bfloat16)
            grad_ref[0, mine, :] += dot(ds[others:end], query, NN)
            grad_ref[1, mine, :] += dot(low[others:end], grad, NN)
            far_sum[0] += dot(ds[end:], query, NN)
            far_sum[1] += dot(low[end:], grad, NN)
        for index, ref in enumerate(far_outs):
            slot = jnp.maximum(at_group - index - 2, 0) // 2
            start = pl.multiple_of(slot * BLK, BLK)
            ref[...] = before_refs[index][...]
            lanes = slice(head * HD, (head + 1) * HD)
            ref[0, :, lanes] = (far_sum[0, pl.ds(start, BLK), :] * SCALE).astype(jnp.bfloat16)
            ref[1, :, lanes] = far_sum[1, pl.ds(start, BLK), :].astype(jnp.bfloat16)

    span = (SPAN + slots) * BLK
    outs = call(
        body, (meta,), (bias, stats, qd, own, prev, *far, *before),
        [shape((whole, HD)), shape((2, whole, HD), jnp.float32)]
        + [shape((2, BLK, width))] * len(far),
        [
            pltpu.VMEM((everything, HD), jnp.bfloat16),
            pltpu.VMEM((everything, HD), jnp.bfloat16),
            pltpu.VMEM((2, slots * BLK, HD), jnp.float32),
        ],
        cost(8 * whole * span * HD * 2, 4 * 1024 * 1024, whole * span),
        f"attention_back_{head}", 24,
    )
    return outs[0], outs[1], outs[2:]


def backward_next(grads, qd, own, bias, stats, meta):
    whole, width = qd.shape[1:]
    heads = width // HD
    pairs = whole // PAIR

    def body(meta_ref, bias_ref, stats_ref, *refs):
        (grad_refs, (qd_ref, own_ref, out)), refs = split_refs(refs, (heads, 3))
        strided = pl.ds(pl.multiple_of(meta_ref[2] * BLK, BLK), BLK)
        for h in range(heads):
            lanes = slice(h * HD, (h + 1) * HD)
            out[0, :, lanes] = grad_refs[h][0]
            out[1, :, lanes] = grad_refs[h][1]
            for t in range(pairs):
                here = slice(t * PAIR, (t + 1) * PAIR)
                window = slice(t * PAIR + BLK, whole)
                near = (whole - BLK) // BLK - t * (PAIR // BLK)
                keys = jnp.concatenate([own_ref[0, window, lanes], own_ref[0, strided, lanes]], axis=0)
                vals = jnp.concatenate([own_ref[1, window, lanes], own_ref[1, strided, lanes]], axis=0)
                query, grad = qd_ref[0, here, lanes], qd_ref[1, here, lanes]
                rows_here = bias_rows(bias_ref, t, list(range(near)) + [SPAN])
                s = masked_scores(keys, query, rows_here, None)
                probs = jnp.exp2(s - stats_ref[t, 2 * h : 2 * h + 1, :])
                delta = stats_ref[t, 2 * h + 1 : 2 * h + 2, :]
                ds = (probs * (dot(vals, grad, NT) - delta)).astype(jnp.bfloat16)
                dk = dot(ds, query, NN)
                dv = dot(probs.astype(jnp.bfloat16), grad, NN)
                out[0, window, lanes] += dk[: near * BLK]
                out[1, window, lanes] += dv[: near * BLK]
                out[0, strided, lanes] += dk[near * BLK :]
                out[1, strided, lanes] += dv[near * BLK :]
        out[0] = out[0] * SCALE

    return call(
        body, (meta,), (bias, stats, *grads, qd, own),
        [shape((2, whole, width), jnp.float32)], [],
        cost(8 * whole * 5 * BLK * width, 7 * 1024 * 1024, whole * 5 * BLK * heads),
        "attention_back_next", 24,
    )[0]


def combine(dq, own, far, meta, group, rows):
    whole, width = own.shape[1:]

    def body(meta_ref, own_ref, *refs):
        (dq_refs, far_refs, outs, (acc,)), refs = split_refs(refs, (len(dq), len(far), group, 1))
        me, offset = meta_ref[0], meta_ref[2]
        acc[...] = own_ref[...]
        at = pl.multiple_of(offset * BLK, BLK)
        for ref in far_refs:
            acc[:, pl.ds(at, BLK), :] += ref[...].astype(jnp.float32)
        for k in range(group):
            here = pl.ds(pl.multiple_of((me ^ k) * rows, rows), rows)
            for h in range(len(dq)):
                outs[k][0, :, h * HD : (h + 1) * HD] = dq_refs[h][here, :]
            outs[k][1] = acc[0, here, :].astype(jnp.bfloat16)
            outs[k][2] = acc[1, here, :].astype(jnp.bfloat16)

    return call(
        body, (meta,), (own, *dq, *far), [shape((3, rows, width))] * group,
        [pltpu.VMEM((2, whole, width), jnp.float32)],
        cost(0, 4 * 1024 * 1024), "combine",
    )


def project(head, mine, theirs, attn, before, meta, group, parts):
    height, whole = mine.shape
    each = 2 * height // parts
    full = group * HD
    more = parts // 2 - 1

    def body(meta_ref, mine_ref, theirs_ref, *refs):
        (attn_refs, before_refs, outs), refs = split_refs(refs, (group, len(before), 6))
        keep, first, odds, evens, pool, total = outs
        for ref in before_refs:
            first[:head] = ref[...]
        me, at_group, core = meta_ref[0], meta_ref[1], meta_ref[3]
        for k in range(group):
            at = pl.multiple_of((me ^ k) * HD, HD)
            pool[:, pl.ds(at, HD)] = attn_refs[k][...]
        upper = pl.ds(pl.multiple_of(core * height, height), height)
        lower = pl.ds(pl.multiple_of((1 - core) * height, height), height)
        total[upper, :] = dot(mine_ref[...], pool[...], NN)
        total[lower, :] = dot(theirs_ref[...], pool[...], NN)
        for m in range(parts):
            part = total[pl.ds(pl.multiple_of((at_group ^ m) * each, each), each), :]
            if m == 0:
                keep[...] = part
            elif m == 1:
                first[head] = part.astype(jnp.bfloat16)
            elif m % 2 == 1:
                odds[m // 2 - 1] = part.astype(jnp.bfloat16)
            else:
                evens[m // 2 - 1] = part

    return call(
        body, (meta,), (mine, theirs, *attn, *before),
        [
            shape((each, full), jnp.float32),
            shape((head + 1, each, full)),
            shape((more, each, full)),
            shape((more, each, full), jnp.float32),
        ],
        [pltpu.VMEM((whole, full), jnp.bfloat16), pltpu.VMEM((2 * height, full), jnp.float32)],
        cost(4 * height * whole * full, 6 * 1024 * 1024), f"project_{head}",
    )


def halve(head, evens, arrived):
    count, each, full = evens.shape
    more = (count - 1) // 2

    def body(evens_ref, arrived_ref, first, *rest):
        for m in range(1, count + 1):
            summed = evens_ref[m - 1] + arrived_ref[m - 1].astype(jnp.float32)
            if m == 1:
                first[...] = summed.astype(jnp.bfloat16)
            elif m % 2 == 1:
                rest[0][m // 2 - 1] = summed.astype(jnp.bfloat16)
            else:
                rest[1][m // 2 - 1] = summed

    others = [shape((more, each, full)), shape((more, each, full), jnp.float32)]
    return call(
        body, (), (evens, arrived), [shape((each, full))] + (others if more else []), [],
        cost(0, 3 * 1024 * 1024), f"halve_{head}",
    )


def finish(keep, neighbour, arrived, group):
    heads = len(keep)
    count = len(arrived[0])
    each = keep[0].shape[0]

    def body(*refs):
        (keep_refs, arrived_refs, (first, out)), refs = split_refs(refs, (heads, heads * count, 2))
        for h in range(heads):
            total = keep_refs[h][...] + first[h].astype(jnp.float32)
            for ref in arrived_refs[h * count : (h + 1) * count]:
                total = total + ref[...].astype(jnp.float32)
            for j in range(group):
                at = (j * heads + h) * HD
                out[:, at : at + HD] = total[:, j * HD : (j + 1) * HD]

    flat = [piece for pieces in arrived for piece in pieces]
    return call(
        body, (), (*keep, *flat, neighbour),
        [shape((each, group * heads * HD), jnp.float32)], [],
        cost(0, 3 * 1024 * 1024), "finish",
    )[0]


def unpack(pieces, meta, group):
    rows, width = pieces[0].shape[1:]

    def body(meta_ref, *refs):
        me = meta_ref[0]
        outs, sems = refs[group:-1], refs[-1]
        copies = []
        for k in range(group):
            at = pl.ds(pl.multiple_of((me ^ k) * width, width), width)
            for which in range(3):
                target = outs[which].at[:, at]
                copies.append(
                    pltpu.make_async_copy(refs[k].at[which], target, sems.at[k, which])
                )
        copied(*copies)

    return pl.pallas_call(
        body,
        out_shape=[shape((rows, group * width))] * 3,
        in_specs=[SMEM] + [ANY] * group,
        out_specs=[ANY] * 3,
        scratch_shapes=[pltpu.SemaphoreType.DMA((group, 3))],
        compiler_params=params(16),
        cost_estimate=cost(0, 3 * MIB),
        name="unpack",
    )(meta, *pieces)


def after(value, *others):
    return lax.optimization_barrier((value, *others))[0]


def local(devices, queries, keys, values, out_grad, proj_weight, layout):
    rows, columns = queries.shape
    group = LOCAL * BLK // rows
    parts = devices // group
    width = columns // group
    heads = width // HD
    blocks = layout.shape[0]
    slots = blocks // STRIDE
    position = lax.axis_index("seq")
    me, at_group = position % group, position // group
    core = lax.axis_index("head")
    offset = layout[blocks - 1, 0] % STRIDE
    place = jnp.stack([me, at_group, core]).astype(jnp.int32)
    meta = jnp.stack([me, at_group, offset, core]).astype(jnp.int32)

    def swap(piece, k):
        route = [(i, (i // group) * group + ((i % group) ^ k)) for i in range(devices)]
        return lax.ppermute(piece, "seq", route)

    def shifted(piece, distance):
        route = [
            (i, i + distance * group)
            for i in range(devices)
            if 0 <= i + distance * group < devices
        ]
        return lax.ppermute(piece, "seq", route)

    def swap_groups(piece, bit):
        route = [(i, ((i // group) ^ bit) * group + i % group) for i in range(devices)]
        return lax.ppermute(piece, "seq", route)

    def summary_route(distance, back):
        route = [
            (i, i + distance * group)
            for i in range(devices - distance * group)
            if (i // group) % 2 == 0
        ]
        return [(b, a) for a, b in route] if back else route

    def exchange(pieces):
        return [pieces[0]] + [swap(pieces[k], k) for k in range(1, group)]

    def add_up(head, odds, evens, before, token):
        arrivals, bit = [], 2
        odds = after(odds, *jax.tree.leaves(before))
        while True:
            first, *more = halve(head, evens, odds)
            token = after(token, first)
            done = first
            arrivals.append(swap_groups(first, bit))
            if not more:
                return arrivals, token, done
            odds, evens = swap_groups(more[0], bit), more[1]
            bit *= 2

    kv = pack_kv(keys, values, place, group, width)
    own_kv = exchange(kv)
    early = after(place, own_kv[1])
    qd_cut = grads_packed(queries, out_grad, proj_weight, early, group, parts)
    pool, strided = assemble_kv(own_kv, after(meta, qd_cut[0]), group)
    prev = shifted(pool, 1)
    qd_pieces = exchange(qd_cut)
    later = after(strided, qd_pieces[1])
    far = [
        lax.ppermute(
            strided if distance == 2 else later, "seq", summary_route(distance, False)
        )
        for distance in range(2, parts)
    ]
    bias, bias_next = masks_of(layout, after(meta, strided), parts, slots)
    qd, mine = assemble(qd_pieces, after(meta, bias, prev, *far), group)
    theirs = lax.ppermute(mine, "head", [(0, 1), (1, 0)])
    next_qd = shifted(qd, -1)

    stats = jnp.zeros((LOCAL // 2, 2 * heads, PAIR), jnp.float32)
    order = meta
    attn = []
    for h in range(heads):
        got, stats = forward(h, qd, pool, prev, far, bias, stats, order, group, slots)
        attn.append([got] + [swap(got, k) for k in range(1, group)])
        order = after(meta, got, theirs)

    dq, grads, keep, finals = [], [], [], []
    far_grads = [jnp.zeros((2, BLK, width), jnp.bfloat16) for _ in far]
    order, first = after(meta, stats, theirs), []
    for h in range(heads):
        got = backward(h, qd, pool, prev, far, far_grads, bias, stats, order, group, slots)
        dq.append(got[0])
        grads.append(got[1])
        far_grads = got[2]
        order = after(meta, got[0])
        kept, first, odds, evens = project(h, mine, theirs, attn[h], first, order, group, parts)
        keep.append(kept)
        first, odds = [first], swap_groups(odds, 1)
        order = after(meta, *first)
        if h == 0:
            next_stats = shifted(after(stats, next_qd, *first), -1)
        if h < heads - 1:
            sums, order, _ = add_up(h, odds, evens, (first, next_stats), order)
            finals.append(sums)
    far_back = [
        lax.ppermute(piece, "seq", summary_route(index + 2, True))
        for index, piece in enumerate(far_grads)
    ]
    order = after(order, finals[0])
    own_grad = backward_next(grads, next_qd, pool, bias_next, next_stats, order)
    final_cut = combine(dq, own_grad, far_back, meta, group, rows)
    final = exchange(final_cut)
    sums, _, _ = add_up(heads - 1, odds, evens, final_cut, meta)
    finals.append(sums)
    neighbour = swap_groups(after(first[0], final_cut[0]), 1)
    proj_grad = finish(keep, neighbour, finals, group)
    query_grad, key_grad, value_grad = unpack(final, meta, group)
    return (query_grad, key_grad, value_grad, proj_grad)


def solution(mesh):
    split = P(("dp", "seq"), "head")
    return jax.shard_map(
        functools.partial(local, mesh.shape["seq"]),
        mesh=mesh,
        in_specs=(split, split, split, P(("dp", "seq"), None), P(None, "head"), P()),
        out_specs=(split, split, split, split),
        check_vma=False,
    )
```

```python
import functools
import math

import jax
import jax.numpy as jnp
from jax import lax
from jax.experimental import pallas as pl
from jax.experimental.pallas import tpu as pltpu
from jax.sharding import PartitionSpec as P

HD = 128
BLK = 128
LOCAL = 8
STRIDE = 16
PAIR = 2 * BLK
SPAN = LOCAL + 1
SCALE = HD ** (-0.5)
SCALE2 = SCALE * math.log2(math.e)
MIB = 1024 * 1024

NT = (((1,), (1,)), ((), ()))
NN = (((1,), (0,)), ((), ()))
TN = (((0,), (0,)), ((), ()))
SMEM = pl.BlockSpec(memory_space=pltpu.SMEM)
VMEM = pl.BlockSpec(memory_space=pltpu.VMEM)
HBM = pl.BlockSpec(memory_space=pltpu.HBM)
ANY = pl.BlockSpec(memory_space=pl.ANY)


def shape(dims, dtype=jnp.bfloat16):
    return jax.ShapeDtypeStruct(dims, dtype)


def dot(a, b, dims):
    return lax.dot_general(a, b, dims, preferred_element_type=jnp.float32)


def params(size):
    return pltpu.CompilerParams(vmem_limit_bytes=size * MIB)


def cost(flops, size, exps=0):
    return pl.CostEstimate(flops=1, bytes_accessed=1, transcendentals=0)


def call(body, scalars, arrays, outs, scratch, estimate, name, size=16):
    return pl.pallas_call(
        body,
        out_shape=outs,
        in_specs=[SMEM] * len(scalars) + [VMEM] * len(arrays),
        out_specs=[VMEM] * len(outs),
        scratch_shapes=scratch,
        compiler_params=params(size),
        cost_estimate=estimate,
        name=name,
    )(*scalars, *arrays)


def one_head(refs, head):
    return [ref.at[(slice(None),) * (ref.ndim - 1) + (pl.ds(head * HD, HD),)] for ref in refs]


def split_refs(refs, counts):
    refs, taken = list(refs), []
    for count in counts:
        taken.append(refs[:count])
        refs = refs[count:]
    return taken, refs


def copied(*copies):
    for copy in copies:
        copy.start()
    for copy in copies:
        copy.wait()


def pack_kv(keys, values, meta, group, width):
    rows = keys.shape[0]

    def body(meta_ref, k_ref, v_ref, *refs):
        outs, (k_in, v_in, sems) = refs[:group], refs[group:]
        me = meta_ref[0]
        copied(
            pltpu.make_async_copy(k_ref, k_in, sems.at[0]),
            pltpu.make_async_copy(v_ref, v_in, sems.at[1]),
        )
        for k in range(group):
            at = pl.ds(pl.multiple_of((me ^ k) * width, width), width)
            outs[k][0] = k_in[:, at]
            outs[k][1] = v_in[:, at]

    return pl.pallas_call(
        body,
        out_shape=[shape((2, rows, width))] * group,
        in_specs=[SMEM, HBM, HBM],
        out_specs=[VMEM] * group,
        scratch_shapes=[
            pltpu.VMEM(keys.shape, jnp.bfloat16),
            pltpu.VMEM(keys.shape, jnp.bfloat16),
            pltpu.SemaphoreType.DMA((2,)),
        ],
        compiler_params=params(60),
        cost_estimate=cost(0, 4 * keys.size * 2),
        name="pack_kv",
    )(meta, keys, values)


def grads_packed(queries, out_grad, proj_weight, meta, group, parts):
    rows, depth = out_grad.shape
    columns = queries.shape[1]
    width = columns // group
    each = depth // (group * parts)
    half = parts // 2
    chunks = 8
    step = depth // chunks
    assert rows == width

    def body(meta_ref, q_ref, og_ref, w_ref, *refs):
        outs, (q, og, w, total, sems, w_sems) = refs[:group], refs[group:]
        me, core = meta_ref[0], meta_ref[2]
        og_copy = pltpu.make_async_copy(og_ref, og, sems.at[0])
        q_copy = pltpu.make_async_copy(q_ref, q, sems.at[1])
        og_copy.start()
        w_copies = []
        for c in range(chunks):
            at = slice(c * step, (c + 1) * step)
            w_copies.append(pltpu.make_async_copy(w_ref.at[at, :], w.at[at, :], w_sems.at[c]))
            w_copies[c].start()
        q_copy.start()
        og_copy.wait()
        for k in range(group):
            for part in range(half):
                at = ((core * half + part) * group + (me ^ k)) * each
                at = pl.multiple_of(at, each)
                to = 2 * rows + part * each
                outs[k][to : to + each, :] = og[:, pl.ds(at, each)].T
        for c in range(chunks):
            at = slice(c * step, (c + 1) * step)
            w_copies[c].wait()
            got = dot(og[:, at], w[at, :], NN)
            if c == 0:
                total[...] = got
            else:
                total[...] += got
        q_copy.wait()
        for k in range(group):
            at = pl.ds(pl.multiple_of((me ^ k) * width, width), width)
            outs[k][:rows, :] = q[:, at]
            outs[k][rows : 2 * rows, :] = total[:, at].astype(jnp.bfloat16)

    return pl.pallas_call(
        body,
        out_shape=[shape((2 * rows + half * each, rows))] * group,
        in_specs=[SMEM, HBM, HBM, HBM],
        out_specs=[VMEM] * group,
        scratch_shapes=[
            pltpu.VMEM((rows, columns), jnp.bfloat16),
            pltpu.VMEM((rows, depth), jnp.bfloat16),
            pltpu.VMEM((depth, columns), jnp.bfloat16),
            pltpu.VMEM((rows, columns), jnp.float32),
            pltpu.SemaphoreType.DMA((2,)),
            pltpu.SemaphoreType.DMA((chunks,)),
        ],
        compiler_params=params(60),
        cost_estimate=cost(2 * rows * depth * columns, 12 * 1024 * 1024),
        name="attn_grad",
    )(meta, queries, out_grad, proj_weight)


def assemble_kv(pieces, meta, group):
    rows, width = pieces[0].shape[1:]

    def body(meta_ref, *refs):
        me = meta_ref[0]
        pool, strided, sems = refs[group:]
        copies = []
        for k in range(group):
            at = pl.ds(pl.multiple_of((me ^ k) * rows, rows), rows)
            copies.append(pltpu.make_async_copy(refs[k], pool.at[:, at, :], sems.at[k]))
        copied(*copies)
        strided[...] = pool[:, pl.ds(pl.multiple_of(meta_ref[2] * BLK, BLK), BLK), :]

    return pl.pallas_call(
        body,
        out_shape=[
            shape((2, group * rows, width)),
            shape((2, BLK, width)),
        ],
        in_specs=[SMEM] + [ANY] * group,
        out_specs=[VMEM] * 2,
        scratch_shapes=[pltpu.SemaphoreType.DMA((group,))],
        compiler_params=params(16),
        cost_estimate=cost(0, 3 * MIB),
        name="assemble_kv",
    )(meta, *pieces)


def assemble(pieces, meta, group):
    rows = pieces[0].shape[1]
    height = pieces[0].shape[0] - 2 * rows

    def body(meta_ref, *refs):
        me = meta_ref[0]
        qd, og = refs[group:]
        for k in range(group):
            at = pl.ds(pl.multiple_of((me ^ k) * rows, rows), rows)
            qd[0, at, :] = refs[k][:rows, :]
            qd[1, at, :] = refs[k][rows : 2 * rows, :]
            og[:, at] = refs[k][2 * rows :, :]

    return call(
        body, (meta,), tuple(pieces),
        [shape((2, group * rows, rows)), shape((height, group * rows))], [],
        cost(0, 4 * MIB), "assemble",
    )


def masks_of(layout, meta, parts, slots):
    width = layout.shape[1]
    pairs = LOCAL // 2

    def body(meta_ref, table, own_ref, next_ref):
        at_group = meta_ref[1]
        low_half = lax.broadcasted_iota(jnp.int32, (1, PAIR), 1) < BLK

        def bits_of(group_at, row):
            block = group_at * LOCAL + row
            base = block - row % 2 - (LOCAL - 1)
            at = jnp.minimum(block, table.shape[0] - 1)
            bits = jnp.int32(0)
            for c in range(width):
                entry = table[at, c]
                near = entry >= jnp.maximum(block - (LOCAL - 1), 0)
                place = jnp.where(near, entry - base, SPAN + jnp.maximum(entry, 0) // STRIDE)
                bit = jnp.left_shift(jnp.int32(1), place)
                bits = bits | jnp.where(entry >= 0, bit, 0)
            return jnp.where(group_at < parts, bits, 0)

        def row_of(first, second, place):
            one = jnp.where((jnp.right_shift(first, place) & 1) == 1, 0.0, -jnp.inf)
            two = jnp.where((jnp.right_shift(second, place) & 1) == 1, 0.0, -jnp.inf)
            return jnp.where(low_half, one, two).astype(jnp.float32)

        for t in range(pairs):
            first, second = bits_of(at_group, 2 * t), bits_of(at_group, 2 * t + 1)
            for place in range(SPAN + slots):
                own_ref[t, place : place + 1, :] = row_of(first, second, place)
            first, second = bits_of(at_group + 1, 2 * t), bits_of(at_group + 1, 2 * t + 1)
            for place in range(SPAN):
                next_ref[t, place : place + 1, :] = row_of(first, second, place)
            even = at_group % 2 == 0
            place = SPAN + at_group // 2
            first, second = jnp.where(even, first, 0), jnp.where(even, second, 0)
            next_ref[t, SPAN : SPAN + 1, :] = row_of(first, second, place)

    return call(
        body, (meta, layout), (),
        [
            shape((pairs, SPAN + slots, PAIR), jnp.float32),
            shape((pairs, SPAN + 1, PAIR), jnp.float32),
        ],
        [], cost(0, 128 * 1024), "masks",
    )


def fill_pools(meta_ref, own, prev, far, k_pool, v_pool, slots):
    at_group, offset = meta_ref[1], meta_ref[2]
    whole = own.shape[1]
    k_pool[:whole, :] = prev[0]
    v_pool[:whole, :] = prev[1]
    k_pool[whole : 2 * whole, :] = own[0]
    v_pool[whole : 2 * whole, :] = own[1]
    tail = jnp.zeros((slots * BLK, k_pool.shape[1]), k_pool.dtype)
    k_pool[2 * whole :, :] = tail
    v_pool[2 * whole :, :] = tail

    @pl.when(at_group % 2 == 1)
    def _():
        to = pl.multiple_of(2 * whole + (at_group // 2) * BLK, BLK)
        start = pl.multiple_of(offset * BLK, BLK)
        k_pool[pl.ds(to, BLK), :] = k_pool[pl.ds(start, BLK), :]
        v_pool[pl.ds(to, BLK), :] = v_pool[pl.ds(start, BLK), :]

    for index, ref in enumerate(far):
        distance = index + 2

        @pl.when((at_group >= distance) & ((at_group - distance) % 2 == 0))
        def _():
            to = pl.multiple_of(2 * whole + ((at_group - distance) // 2) * BLK, BLK)
            k_pool[pl.ds(to, BLK), :] = ref[0]
            v_pool[pl.ds(to, BLK), :] = ref[1]


def causal_masks():
    key_at = lax.broadcasted_iota(jnp.int32, (BLK, PAIR), 0)
    query_at = lax.broadcasted_iota(jnp.int32, (BLK, PAIR), 1)
    first = (key_at <= query_at) | (query_at >= BLK)
    second = key_at <= query_at - BLK
    return first, second


def masked_scores(keys, query, bias, masks):
    raw = dot(keys, query, NT) * SCALE2
    tiles = []
    for j in range(keys.shape[0] // BLK):
        tile = raw[j * BLK : (j + 1) * BLK] + bias[j]
        if masks is not None and j in (LOCAL - 1, LOCAL):
            tile = jnp.where(masks[j - LOCAL + 1], tile, -jnp.inf)
        tiles.append(tile)
    return jnp.concatenate(tiles, axis=0)


def bias_rows(bias_ref, t, picked):
    return [bias_ref[t, j : j + 1, :] for j in picked]


def forward(head, qd, own, prev, far, bias, stats, meta, group, slots):
    whole = qd.shape[1]
    pairs = whole // PAIR
    counts = (3, len(far))

    def body(meta_ref, bias_ref, before_ref, *refs):
        (around, far_refs), refs = split_refs(refs, counts)
        qd_ref, *around = one_head(around, head)
        far_refs = one_head(far_refs, head)
        out_ref, stats_ref, k_pool, v_pool = refs
        fill_pools(meta_ref, *around, far_refs, k_pool, v_pool, slots)
        stats_ref[...] = before_ref[...]
        masks = causal_masks()
        for t in range(pairs):
            here = slice(t * PAIR, (t + 1) * PAIR)
            window = slice(t * PAIR + BLK, t * PAIR + BLK + SPAN * BLK)
            keys = jnp.concatenate([k_pool[window, :], k_pool[2 * whole :, :]], axis=0)
            vals = jnp.concatenate([v_pool[window, :], v_pool[2 * whole :, :]], axis=0)
            s = masked_scores(keys, qd_ref[0, here, :], bias_rows(bias_ref, t, range(SPAN + slots)), masks)
            top = jnp.max(s, axis=0, keepdims=True)
            e = jnp.exp2(s - top)
            total = jnp.sum(e, axis=0, keepdims=True)
            low = (e * (1.0 / total)).astype(jnp.bfloat16)
            out = dot(low, vals, TN).astype(jnp.bfloat16)
            out_ref[here, :] = out
            product = out.astype(jnp.float32) * qd_ref[1, here, :].astype(jnp.float32)
            stats_ref[t, 2 * head : 2 * head + 1, :] = top + jnp.log2(total)
            stats_ref[t, 2 * head + 1 : 2 * head + 2, :] = jnp.sum(product.T, axis=0, keepdims=True)

    span = (SPAN + slots) * BLK
    return call(
        body, (meta,), (bias, stats, qd, own, prev, *far),
        [shape((whole, HD)), shape(stats.shape, jnp.float32)],
        [pltpu.VMEM((2 * whole + slots * BLK, HD), jnp.bfloat16)] * 2,
        cost(4 * whole * span * HD * 2, 3 * 1024 * 1024, whole * span),
        f"attention_{head}", 24,
    )


def backward(head, qd, own, prev, far, before, carry, bias, stats, meta, group, slots):
    whole, width = qd.shape[1:]
    pairs = whole // PAIR
    counts = (3, len(far), len(before), len(carry))
    rows = whole // group
    cut = group if carry else 1
    everything = 2 * whole + slots * BLK

    def body(meta_ref, bias_ref, stats_ref, *refs):
        (around, far_refs, before_refs, carry_refs), refs = split_refs(refs, counts)
        qd_ref, *around = one_head(around, head)
        far_refs = one_head(far_refs, head)
        ((grad_ref,), far_outs, dq_outs), refs = split_refs(refs, (1, len(far), cut))
        k_pool, v_pool, far_sum, dq_ref = refs
        at_group = meta_ref[1]
        fill_pools(meta_ref, *around, far_refs, k_pool, v_pool, slots)
        masks = causal_masks()
        grad_ref[...] = jnp.zeros_like(grad_ref)
        far_sum[...] = jnp.zeros_like(far_sum)
        for t in range(pairs):
            here = slice(t * PAIR, (t + 1) * PAIR)
            window = slice(t * PAIR + BLK, t * PAIR + BLK + SPAN * BLK)
            others = max(whole - (t * PAIR + BLK), 0)
            end = SPAN * BLK
            mine = slice(t * PAIR + BLK + others - whole, t * PAIR + BLK + end - whole)
            keys = jnp.concatenate([k_pool[window, :], k_pool[2 * whole :, :]], axis=0)
            vals = jnp.concatenate([v_pool[window, :], v_pool[2 * whole :, :]], axis=0)
            query, grad = qd_ref[0, here, :], qd_ref[1, here, :]
            s = masked_scores(keys, query, bias_rows(bias_ref, t, range(SPAN + slots)), masks)
            probs = jnp.exp2(s - stats_ref[t, 2 * head : 2 * head + 1, :])
            delta = stats_ref[t, 2 * head + 1 : 2 * head + 2, :]
            ds = (probs * (dot(vals, grad, NT) - delta)).astype(jnp.bfloat16)
            low = probs.astype(jnp.bfloat16)
            dq_ref[here, :] = (dot(ds, keys, TN) * SCALE).astype(jnp.bfloat16)
            grad_ref[0, mine, :] += dot(ds[others:end], query, NN)
            grad_ref[1, mine, :] += dot(low[others:end], grad, NN)
            far_sum[0] += dot(ds[end:], query, NN)
            far_sum[1] += dot(low[end:], grad, NN)
        if carry:
            for k in range(group):
                piece = pl.ds(pl.multiple_of((meta_ref[0] ^ k) * rows, rows), rows)
                dq_outs[k][whole:, :] = dq_ref[piece, :]
                dq_outs[k][:whole, :] = carry_refs[0][...]
        else:
            dq_outs[0][...] = dq_ref[...]
        for index, ref in enumerate(far_outs):
            slot = jnp.maximum(at_group - index - 2, 0) // 2
            start = pl.multiple_of(slot * BLK, BLK)
            ref[...] = before_refs[index][...]
            lanes = slice(head * HD, (head + 1) * HD)
            ref[0, :, lanes] = (far_sum[0, pl.ds(start, BLK), :] * SCALE).astype(jnp.bfloat16)
            ref[1, :, lanes] = far_sum[1, pl.ds(start, BLK), :].astype(jnp.bfloat16)

    span = (SPAN + slots) * BLK
    outs = call(
        body, (meta,), (bias, stats, qd, own, prev, *far, *before, *carry),
        [shape((2, whole, HD), jnp.float32)]
        + [shape((2, BLK, width))] * len(far)
        + [shape((whole + rows if carry else whole, HD))] * cut,
        [
            pltpu.VMEM((everything, HD), jnp.bfloat16),
            pltpu.VMEM((everything, HD), jnp.bfloat16),
            pltpu.VMEM((2, slots * BLK, HD), jnp.float32),
            pltpu.VMEM((whole, HD), jnp.bfloat16),
        ],
        cost(8 * whole * span * HD * 2, 4 * 1024 * 1024, whole * span),
        f"attention_back_{head}", 24,
    )
    return outs[0], outs[1 : 1 + len(far)], outs[1 + len(far) :]


def backward_next(grads, qd, own, bias, stats, meta):
    whole, width = qd.shape[1:]
    heads = width // HD
    pairs = whole // PAIR

    def body(meta_ref, bias_ref, stats_ref, *refs):
        (grad_refs, (qd_ref, own_ref, out)), refs = split_refs(refs, (heads, 3))
        strided = pl.ds(pl.multiple_of(meta_ref[2] * BLK, BLK), BLK)
        for h in range(heads):
            lanes = slice(h * HD, (h + 1) * HD)
            out[0, :, lanes] = grad_refs[h][0]
            out[1, :, lanes] = grad_refs[h][1]
            for t in range(pairs):
                here = slice(t * PAIR, (t + 1) * PAIR)
                window = slice(t * PAIR + BLK, whole)
                near = (whole - BLK) // BLK - t * (PAIR // BLK)
                keys = jnp.concatenate([own_ref[0, window, lanes], own_ref[0, strided, lanes]], axis=0)
                vals = jnp.concatenate([own_ref[1, window, lanes], own_ref[1, strided, lanes]], axis=0)
                query, grad = qd_ref[0, here, lanes], qd_ref[1, here, lanes]
                rows_here = bias_rows(bias_ref, t, list(range(near)) + [SPAN])
                s = masked_scores(keys, query, rows_here, None)
                probs = jnp.exp2(s - stats_ref[t, 2 * h : 2 * h + 1, :])
                delta = stats_ref[t, 2 * h + 1 : 2 * h + 2, :]
                ds = (probs * (dot(vals, grad, NT) - delta)).astype(jnp.bfloat16)
                dk = dot(ds, query, NN)
                dv = dot(probs.astype(jnp.bfloat16), grad, NN)
                out[0, window, lanes] += dk[: near * BLK]
                out[1, window, lanes] += dv[: near * BLK]
                out[0, strided, lanes] += dk[near * BLK :]
                out[1, strided, lanes] += dv[near * BLK :]
        out[0] = out[0] * SCALE

    return call(
        body, (meta,), (bias, stats, *grads, qd, own),
        [shape((2, whole, width), jnp.float32)], [],
        cost(8 * whole * 5 * BLK * width, 7 * 1024 * 1024, whole * 5 * BLK * heads),
        "attention_back_next", 24,
    )[0]


def combine(dq, own, far, meta, group, rows):
    whole, width = own.shape[1:]
    heads = width // HD

    def body(meta_ref, dq_ref, own_ref, *refs):
        (far_refs, outs, (acc,)), refs = split_refs(refs, (len(far), group, 1))
        me, offset = meta_ref[0], meta_ref[2]
        acc[...] = own_ref[...]
        at = pl.multiple_of(offset * BLK, BLK)
        for ref in far_refs:
            acc[:, pl.ds(at, BLK), :] += ref[...].astype(jnp.float32)
        for k in range(group):
            here = pl.ds(pl.multiple_of((me ^ k) * rows, rows), rows)
            outs[k][0] = dq_ref[here, :]
            for which in range(2):
                for h in range(heads):
                    lanes = slice(h * HD, (h + 1) * HD)
                    outs[k][1 + which * heads + h] = acc[which, here, lanes].astype(jnp.bfloat16)

    return call(
        body, (meta,), (dq, own, *far), [shape((1 + 2 * heads, rows, HD))] * group,
        [pltpu.VMEM((2, whole, width), jnp.float32)],
        cost(0, 4 * 1024 * 1024), "combine",
    )


def project(head, mine, theirs, attn, before, meta, group, parts):
    height, whole = mine.shape
    each = 2 * height // parts
    full = group * HD
    more = parts // 2 - 1

    def body(meta_ref, mine_ref, theirs_ref, *refs):
        (attn_refs, before_refs, outs), refs = split_refs(refs, (group, len(before), 6))
        keep, first, odds, evens, pool, total = outs
        for ref in before_refs:
            first[:head] = ref[...]
        me, at_group, core = meta_ref[0], meta_ref[1], meta_ref[3]
        for k in range(group):
            at = pl.multiple_of((me ^ k) * HD, HD)
            pool[:, pl.ds(at, HD)] = attn_refs[k][:whole, :]
        upper = pl.ds(pl.multiple_of(core * height, height), height)
        lower = pl.ds(pl.multiple_of((1 - core) * height, height), height)
        total[upper, :] = dot(mine_ref[...], pool[...], NN)
        total[lower, :] = dot(theirs_ref[...], pool[...], NN)
        for m in range(parts):
            part = total[pl.ds(pl.multiple_of((at_group ^ m) * each, each), each), :]
            if m == 0:
                keep[...] = part
            elif m == 1:
                first[head] = part.astype(jnp.bfloat16)
            elif m % 2 == 1:
                odds[m // 2 - 1] = part.astype(jnp.bfloat16)
            else:
                evens[m // 2 - 1] = part

    return call(
        body, (meta,), (mine, theirs, *attn, *before),
        [
            shape((each, full), jnp.float32),
            shape((head + 1, each, full)),
            shape((more, each, full)),
            shape((more, each, full), jnp.float32),
        ],
        [pltpu.VMEM((whole, full), jnp.bfloat16), pltpu.VMEM((2 * height, full), jnp.float32)],
        cost(4 * height * whole * full, 6 * 1024 * 1024), f"project_{head}",
    )


def halve(head, evens, arrived):
    count, each, full = evens.shape
    more = (count - 1) // 2

    def body(evens_ref, arrived_ref, first, *rest):
        for m in range(1, count + 1):
            summed = evens_ref[m - 1] + arrived_ref[m - 1].astype(jnp.float32)
            if m == 1:
                first[...] = summed.astype(jnp.bfloat16)
            elif m % 2 == 1:
                rest[0][m // 2 - 1] = summed.astype(jnp.bfloat16)
            else:
                rest[1][m // 2 - 1] = summed

    others = [shape((more, each, full)), shape((more, each, full), jnp.float32)]
    return call(
        body, (), (evens, arrived), [shape((each, full))] + (others if more else []), [],
        cost(0, 3 * 1024 * 1024), f"halve_{head}",
    )


def finish(keep, neighbour, arrived, group):
    heads = len(keep)
    count = len(arrived[0])
    each = keep[0].shape[0]

    def body(*refs):
        (keep_refs, arrived_refs, (first, out)), refs = split_refs(refs, (heads, heads * count, 2))
        for h in range(heads):
            total = keep_refs[h][...] + first[h].astype(jnp.float32)
            for ref in arrived_refs[h * count : (h + 1) * count]:
                total = total + ref[...].astype(jnp.float32)
            for j in range(group):
                at = (j * heads + h) * HD
                out[:, at : at + HD] = total[:, j * HD : (j + 1) * HD]

    flat = [piece for pieces in arrived for piece in pieces]
    return call(
        body, (), (*keep, *flat, neighbour),
        [shape((each, group * heads * HD), jnp.float32)], [],
        cost(0, 3 * 1024 * 1024), "finish",
    )[0]


def unpack(early, pieces, meta, group):
    count, rows, _ = pieces[0].shape
    heads = (count - 1) // 2
    whole = early[0].shape[0] - rows

    def body(meta_ref, *refs):
        (early_refs, piece_refs, outs, (sems,)), refs = split_refs(refs, (group, group, 3, 1))
        me = meta_ref[0]
        copies = []
        for k in range(group):
            sources = [early_refs[k].at[pl.ds(whole, rows), :]]
            sources += [piece_refs[k].at[which] for which in range(count)]
            for which, source in enumerate(sources):
                at = (me ^ k) * heads * HD + (which % heads) * HD
                target = outs[which // heads].at[:, pl.ds(pl.multiple_of(at, HD), HD)]
                copies.append(pltpu.make_async_copy(source, target, sems.at[k, which]))
        copied(*copies)

    return pl.pallas_call(
        body,
        out_shape=[shape((rows, group * heads * HD))] * 3,
        in_specs=[SMEM] + [ANY] * (2 * group),
        out_specs=[ANY] * 3,
        scratch_shapes=[pltpu.SemaphoreType.DMA((group, count + 1))],
        compiler_params=params(16),
        cost_estimate=cost(0, 3 * MIB),
        name="unpack",
    )(meta, *early, *pieces)


def after(value, *others):
    return lax.optimization_barrier((value, *others))[0]


def local(devices, queries, keys, values, out_grad, proj_weight, layout):
    rows, columns = queries.shape
    group = LOCAL * BLK // rows
    parts = devices // group
    width = columns // group
    heads = width // HD
    blocks = layout.shape[0]
    slots = blocks // STRIDE
    position = lax.axis_index("seq")
    me, at_group = position % group, position // group
    core = lax.axis_index("head")
    offset = layout[blocks - 1, 0] % STRIDE
    place = jnp.stack([me, at_group, core]).astype(jnp.int32)
    meta = jnp.stack([me, at_group, offset, core]).astype(jnp.int32)

    def swap(piece, k):
        route = [(i, (i // group) * group + ((i % group) ^ k)) for i in range(devices)]
        return lax.ppermute(piece, "seq", route)

    def shifted(piece, distance):
        route = [
            (i, i + distance * group)
            for i in range(devices)
            if 0 <= i + distance * group < devices
        ]
        return lax.ppermute(piece, "seq", route)

    def swap_groups(piece, bit):
        route = [(i, ((i // group) ^ bit) * group + i % group) for i in range(devices)]
        return lax.ppermute(piece, "seq", route)

    def summary_route(distance, back):
        route = [
            (i, i + distance * group)
            for i in range(devices - distance * group)
            if (i // group) % 2 == 0
        ]
        return [(b, a) for a, b in route] if back else route

    def exchange(pieces):
        return [pieces[0]] + [swap(pieces[k], k) for k in range(1, group)]

    def add_up(head, odds, evens, before, token):
        arrivals, bit = [], 2
        odds = after(odds, *jax.tree.leaves(before))
        while True:
            first, *more = halve(head, evens, odds)
            token = after(token, first)
            done = first
            arrivals.append(swap_groups(first, bit))
            if not more:
                return arrivals, token, done
            odds, evens = swap_groups(more[0], bit), more[1]
            bit *= 2

    kv = pack_kv(keys, values, place, group, width)
    own_kv = exchange(kv)
    early = after(place, own_kv[1])
    qd_cut = grads_packed(queries, out_grad, proj_weight, early, group, parts)
    pool, strided = assemble_kv(own_kv, after(meta, qd_cut[0]), group)
    prev = shifted(pool, 1)
    qd_pieces = exchange(qd_cut)
    later = after(strided, qd_pieces[1])
    far = [
        lax.ppermute(
            strided if distance == 2 else later, "seq", summary_route(distance, False)
        )
        for distance in range(2, parts)
    ]
    bias, bias_next = masks_of(layout, after(meta, strided), parts, slots)
    qd, mine = assemble(qd_pieces, after(meta, bias, prev, *far), group)
    theirs = lax.ppermute(mine, "head", [(0, 1), (1, 0)])
    next_qd = shifted(qd, -1)

    stats = jnp.zeros((LOCAL // 2, 2 * heads, PAIR), jnp.float32)
    order = meta
    attn = []
    for h in range(heads):
        got, stats = forward(h, qd, pool, prev, far, bias, stats, order, group, slots)
        attn.append(got)
        if h == 0:
            attn[0] = [got] + [swap(got, k) for k in range(1, group)]
        order = after(meta, got, theirs)

    assert heads == 2
    grads, keep, finals = [], [], []
    far_grads = [jnp.zeros((2, BLK, width), jnp.bfloat16) for _ in far]
    order, first = after(meta, stats, theirs), []
    for h in range(heads):
        carry = attn[1:] if h == 0 else []
        got = backward(
            h, qd, pool, prev, far, far_grads, carry, bias, stats, order, group, slots
        )
        grads.append(got[0])
        far_grads = got[1]
        if h == 0:
            attn[1] = early_dq = exchange(got[2])
        else:
            dq = got[2][0]
        order = after(meta, got[0])
        kept, first, odds, evens = project(h, mine, theirs, attn[h], first, order, group, parts)
        keep.append(kept)
        first, odds = [first], swap_groups(odds, 1)
        order = after(meta, *first)
        if h == 0:
            next_stats = shifted(after(stats, next_qd, *first), -1)
        if h < heads - 1:
            sums, order, _ = add_up(h, odds, evens, (first, next_stats), order)
            finals.append(sums)
    far_back = [
        lax.ppermute(piece, "seq", summary_route(index + 2, True))
        for index, piece in enumerate(far_grads)
    ]
    order = after(order, finals[0])
    own_grad = backward_next(grads, next_qd, pool, bias_next, next_stats, order)
    final_cut = combine(dq, own_grad, far_back, meta, group, rows)
    final = exchange(final_cut)
    sums, _, _ = add_up(heads - 1, odds, evens, final_cut, meta)
    finals.append(sums)
    neighbour = swap_groups(after(first[0], final_cut[0]), 1)
    proj_grad = finish(keep, neighbour, finals, group)
    query_grad, key_grad, value_grad = unpack(early_dq, final, meta, group)
    return (query_grad, key_grad, value_grad, proj_grad)


def solution(mesh):
    split = P(("dp", "seq"), "head")
    return jax.shard_map(
        functools.partial(local, mesh.shape["seq"]),
        mesh=mesh,
        in_specs=(split, split, split, P(("dp", "seq"), None), P(None, "head"), P()),
        out_specs=(split, split, split, split),
        check_vma=False,
    )
```

```python
import functools
import math

import jax
import jax.numpy as jnp
from jax import lax
from jax.experimental import pallas as pl
from jax.experimental.pallas import tpu as pltpu
from jax.sharding import PartitionSpec as P

HD = 128
BLK = 128
LOCAL = 8
STRIDE = 16
PAIR = 2 * BLK
SPAN = LOCAL + 1
SCALE = HD ** (-0.5)
SCALE2 = SCALE * math.log2(math.e)
MIB = 1024 * 1024

NT = (((1,), (1,)), ((), ()))
NN = (((1,), (0,)), ((), ()))
TN = (((0,), (0,)), ((), ()))
SMEM = pl.BlockSpec(memory_space=pltpu.SMEM)
VMEM = pl.BlockSpec(memory_space=pltpu.VMEM)
HBM = pl.BlockSpec(memory_space=pltpu.HBM)
ANY = pl.BlockSpec(memory_space=pl.ANY)


def shape(dims, dtype=jnp.bfloat16):
    return jax.ShapeDtypeStruct(dims, dtype)


def dot(a, b, dims):
    return lax.dot_general(a, b, dims, preferred_element_type=jnp.float32)


def params(size):
    return pltpu.CompilerParams(vmem_limit_bytes=size * MIB)


def cost(flops, size, exps=0):
    return pl.CostEstimate(flops=1, bytes_accessed=1, transcendentals=0)


def call(body, scalars, arrays, outs, scratch, estimate, name, size=16):
    return pl.pallas_call(
        body,
        out_shape=outs,
        in_specs=[SMEM] * len(scalars) + [VMEM] * len(arrays),
        out_specs=[VMEM] * len(outs),
        scratch_shapes=scratch,
        compiler_params=params(size),
        cost_estimate=estimate,
        name=name,
    )(*scalars, *arrays)


def one_head(refs, head):
    return [ref.at[(slice(None),) * (ref.ndim - 1) + (pl.ds(head * HD, HD),)] for ref in refs]


def split_refs(refs, counts):
    refs, taken = list(refs), []
    for count in counts:
        taken.append(refs[:count])
        refs = refs[count:]
    return taken, refs


def copied(*copies):
    for copy in copies:
        copy.start()
    for copy in copies:
        copy.wait()


def pack_kv(keys, values, meta, group, width):
    rows = keys.shape[0]

    def body(meta_ref, k_ref, v_ref, *refs):
        outs, (k_in, v_in, sems) = refs[:group], refs[group:]
        me = meta_ref[0]
        copied(
            pltpu.make_async_copy(k_ref, k_in, sems.at[0]),
            pltpu.make_async_copy(v_ref, v_in, sems.at[1]),
        )
        for k in range(group):
            at = pl.ds(pl.multiple_of((me ^ k) * width, width), width)
            outs[k][0] = k_in[:, at]
            outs[k][1] = v_in[:, at]

    return pl.pallas_call(
        body,
        out_shape=[shape((2, rows, width))] * group,
        in_specs=[SMEM, HBM, HBM],
        out_specs=[VMEM] * group,
        scratch_shapes=[
            pltpu.VMEM(keys.shape, jnp.bfloat16),
            pltpu.VMEM(keys.shape, jnp.bfloat16),
            pltpu.SemaphoreType.DMA((2,)),
        ],
        compiler_params=params(60),
        cost_estimate=cost(0, 4 * keys.size * 2),
        name="pack_kv",
    )(meta, keys, values)


def grads_packed(queries, out_grad, proj_weight, meta, group, parts):
    rows, depth = out_grad.shape
    columns = queries.shape[1]
    width = columns // group
    each = depth // (group * parts)
    half = parts // 2
    chunks = 8
    step = depth // chunks
    assert rows == width

    def body(meta_ref, q_ref, og_ref, w_ref, *refs):
        outs, (q, og, w, total, sems, w_sems) = refs[:group], refs[group:]
        me, core = meta_ref[0], meta_ref[2]
        og_copy = pltpu.make_async_copy(og_ref, og, sems.at[0])
        q_copy = pltpu.make_async_copy(q_ref, q, sems.at[1])
        og_copy.start()
        w_copies = []
        for c in range(chunks):
            at = slice(c * step, (c + 1) * step)
            w_copies.append(pltpu.make_async_copy(w_ref.at[at, :], w.at[at, :], w_sems.at[c]))
            w_copies[c].start()
        q_copy.start()
        og_copy.wait()
        for k in range(group):
            for part in range(half):
                at = ((core * half + part) * group + (me ^ k)) * each
                at = pl.multiple_of(at, each)
                to = 2 * rows + part * each
                outs[k][to : to + each, :] = og[:, pl.ds(at, each)].T
        for c in range(chunks):
            at = slice(c * step, (c + 1) * step)
            w_copies[c].wait()
            got = dot(og[:, at], w[at, :], NN)
            if c == 0:
                total[...] = got
            else:
                total[...] += got
        q_copy.wait()
        for k in range(group):
            at = pl.ds(pl.multiple_of((me ^ k) * width, width), width)
            outs[k][:rows, :] = q[:, at]
            outs[k][rows : 2 * rows, :] = total[:, at].astype(jnp.bfloat16)

    return pl.pallas_call(
        body,
        out_shape=[shape((2 * rows + half * each, rows))] * group,
        in_specs=[SMEM, HBM, HBM, HBM],
        out_specs=[VMEM] * group,
        scratch_shapes=[
            pltpu.VMEM((rows, columns), jnp.bfloat16),
            pltpu.VMEM((rows, depth), jnp.bfloat16),
            pltpu.VMEM((depth, columns), jnp.bfloat16),
            pltpu.VMEM((rows, columns), jnp.float32),
            pltpu.SemaphoreType.DMA((2,)),
            pltpu.SemaphoreType.DMA((chunks,)),
        ],
        compiler_params=params(60),
        cost_estimate=cost(2 * rows * depth * columns, 12 * 1024 * 1024),
        name="attn_grad",
    )(meta, queries, out_grad, proj_weight)


def assemble_kv(pieces, meta, group):
    rows, width = pieces[0].shape[1:]

    def body(meta_ref, *refs):
        me = meta_ref[0]
        pool, strided, sems = refs[group:]
        copies = []
        for k in range(group):
            at = pl.ds(pl.multiple_of((me ^ k) * rows, rows), rows)
            copies.append(pltpu.make_async_copy(refs[k], pool.at[:, at, :], sems.at[k]))
        copied(*copies)
        strided[...] = pool[:, pl.ds(pl.multiple_of(meta_ref[2] * BLK, BLK), BLK), :]

    return pl.pallas_call(
        body,
        out_shape=[
            shape((2, group * rows, width)),
            shape((2, BLK, width)),
        ],
        in_specs=[SMEM] + [ANY] * group,
        out_specs=[VMEM] * 2,
        scratch_shapes=[pltpu.SemaphoreType.DMA((group,))],
        compiler_params=params(16),
        cost_estimate=cost(0, 3 * MIB),
        name="assemble_kv",
    )(meta, *pieces)


def assemble(pieces, meta, group):
    rows = pieces[0].shape[1]
    height = pieces[0].shape[0] - 2 * rows

    def body(meta_ref, *refs):
        me = meta_ref[0]
        qd, og = refs[group:]
        for k in range(group):
            at = pl.ds(pl.multiple_of((me ^ k) * rows, rows), rows)
            qd[0, at, :] = refs[k][:rows, :]
            qd[1, at, :] = refs[k][rows : 2 * rows, :]
            og[:, at] = refs[k][2 * rows :, :]

    return call(
        body, (meta,), tuple(pieces),
        [shape((2, group * rows, rows)), shape((height, group * rows))], [],
        cost(0, 4 * MIB), "assemble",
    )


def masks_of(layout, meta, parts, slots):
    width = layout.shape[1]
    pairs = LOCAL // 2

    def body(meta_ref, table, own_ref, next_ref):
        at_group = meta_ref[1]
        low_half = lax.broadcasted_iota(jnp.int32, (1, PAIR), 1) < BLK

        def bits_of(group_at, row):
            block = group_at * LOCAL + row
            base = block - row % 2 - (LOCAL - 1)
            at = jnp.minimum(block, table.shape[0] - 1)
            bits = jnp.int32(0)
            for c in range(width):
                entry = table[at, c]
                near = entry >= jnp.maximum(block - (LOCAL - 1), 0)
                place = jnp.where(near, entry - base, SPAN + jnp.maximum(entry, 0) // STRIDE)
                bit = jnp.left_shift(jnp.int32(1), place)
                bits = bits | jnp.where(entry >= 0, bit, 0)
            return jnp.where(group_at < parts, bits, 0)

        def row_of(first, second, place):
            one = jnp.where((jnp.right_shift(first, place) & 1) == 1, 0.0, -jnp.inf)
            two = jnp.where((jnp.right_shift(second, place) & 1) == 1, 0.0, -jnp.inf)
            return jnp.where(low_half, one, two).astype(jnp.float32)

        for t in range(pairs):
            first, second = bits_of(at_group, 2 * t), bits_of(at_group, 2 * t + 1)
            for place in range(SPAN + slots):
                own_ref[t, place : place + 1, :] = row_of(first, second, place)
            first, second = bits_of(at_group + 1, 2 * t), bits_of(at_group + 1, 2 * t + 1)
            for place in range(SPAN):
                next_ref[t, place : place + 1, :] = row_of(first, second, place)
            even = at_group % 2 == 0
            place = SPAN + at_group // 2
            first, second = jnp.where(even, first, 0), jnp.where(even, second, 0)
            next_ref[t, SPAN : SPAN + 1, :] = row_of(first, second, place)

    return call(
        body, (meta, layout), (),
        [
            shape((pairs, SPAN + slots, PAIR), jnp.float32),
            shape((pairs, SPAN + 1, PAIR), jnp.float32),
        ],
        [], cost(0, 128 * 1024), "masks",
    )


def fill_pools(meta_ref, own, prev, far, k_pool, v_pool, slots):
    at_group, offset = meta_ref[1], meta_ref[2]
    whole = own.shape[1]
    k_pool[:whole, :] = prev[0]
    v_pool[:whole, :] = prev[1]
    k_pool[whole : 2 * whole, :] = own[0]
    v_pool[whole : 2 * whole, :] = own[1]
    tail = jnp.zeros((slots * BLK, k_pool.shape[1]), k_pool.dtype)
    k_pool[2 * whole :, :] = tail
    v_pool[2 * whole :, :] = tail

    @pl.when(at_group % 2 == 1)
    def _():
        to = pl.multiple_of(2 * whole + (at_group // 2) * BLK, BLK)
        start = pl.multiple_of(offset * BLK, BLK)
        k_pool[pl.ds(to, BLK), :] = k_pool[pl.ds(start, BLK), :]
        v_pool[pl.ds(to, BLK), :] = v_pool[pl.ds(start, BLK), :]

    for index, ref in enumerate(far):
        distance = index + 2

        @pl.when((at_group >= distance) & ((at_group - distance) % 2 == 0))
        def _():
            to = pl.multiple_of(2 * whole + ((at_group - distance) // 2) * BLK, BLK)
            k_pool[pl.ds(to, BLK), :] = ref[0]
            v_pool[pl.ds(to, BLK), :] = ref[1]


def causal_masks():
    key_at = lax.broadcasted_iota(jnp.int32, (BLK, PAIR), 0)
    query_at = lax.broadcasted_iota(jnp.int32, (BLK, PAIR), 1)
    first = (key_at <= query_at) | (query_at >= BLK)
    second = key_at <= query_at - BLK
    return first, second


def masked_scores(keys, query, bias, masks):
    raw = dot(keys, query, NT) * SCALE2
    tiles = []
    for j in range(keys.shape[0] // BLK):
        tile = raw[j * BLK : (j + 1) * BLK] + bias[j]
        if masks is not None and j in (LOCAL - 1, LOCAL):
            tile = jnp.where(masks[j - LOCAL + 1], tile, -jnp.inf)
        tiles.append(tile)
    return jnp.concatenate(tiles, axis=0)


def bias_rows(bias_ref, t, picked):
    return [bias_ref[t, j : j + 1, :] for j in picked]


def forward(head, qd, own, prev, far, bias, stats, meta, group, slots):
    whole = qd.shape[1]
    pairs = whole // PAIR
    counts = (3, len(far))

    def body(meta_ref, bias_ref, before_ref, *refs):
        (around, far_refs), refs = split_refs(refs, counts)
        qd_ref, *around = one_head(around, head)
        far_refs = one_head(far_refs, head)
        out_ref, stats_ref, k_pool, v_pool = refs
        fill_pools(meta_ref, *around, far_refs, k_pool, v_pool, slots)
        stats_ref[...] = before_ref[...]
        masks = causal_masks()
        for t in range(pairs):
            here = slice(t * PAIR, (t + 1) * PAIR)
            window = slice(t * PAIR + BLK, t * PAIR + BLK + SPAN * BLK)
            keys = jnp.concatenate([k_pool[window, :], k_pool[2 * whole :, :]], axis=0)
            vals = jnp.concatenate([v_pool[window, :], v_pool[2 * whole :, :]], axis=0)
            s = masked_scores(keys, qd_ref[0, here, :], bias_rows(bias_ref, t, range(SPAN + slots)), masks)
            top = jnp.max(s, axis=0, keepdims=True)
            e = jnp.exp2(s - top)
            total = jnp.sum(e, axis=0, keepdims=True)
            low = (e * (1.0 / total)).astype(jnp.bfloat16)
            out = dot(low, vals, TN).astype(jnp.bfloat16)
            out_ref[here, :] = out
            product = out.astype(jnp.float32) * qd_ref[1, here, :].astype(jnp.float32)
            stats_ref[t, 2 * head : 2 * head + 1, :] = top + jnp.log2(total)
            stats_ref[t, 2 * head + 1 : 2 * head + 2, :] = jnp.sum(product.T, axis=0, keepdims=True)

    span = (SPAN + slots) * BLK
    return call(
        body, (meta,), (bias, stats, qd, own, prev, *far),
        [shape((whole, HD)), shape(stats.shape, jnp.float32)],
        [pltpu.VMEM((2 * whole + slots * BLK, HD), jnp.bfloat16)] * 2,
        cost(4 * whole * span * HD * 2, 3 * 1024 * 1024, whole * span),
        f"attention_{head}", 24,
    )


def backward(head, qd, own, prev, far, before, carry, bias, stats, meta, group, slots):
    whole, width = qd.shape[1:]
    pairs = whole // PAIR
    counts = (3, len(far), len(before), len(carry))
    rows = whole // group
    cut = group if carry else 1
    everything = 2 * whole + slots * BLK

    def body(meta_ref, bias_ref, stats_ref, *refs):
        (around, far_refs, before_refs, carry_refs), refs = split_refs(refs, counts)
        qd_ref, *around = one_head(around, head)
        far_refs = one_head(far_refs, head)
        ((grad_ref,), far_outs, dq_outs), refs = split_refs(refs, (1, len(far), cut))
        k_pool, v_pool, far_sum, dq_ref = refs
        at_group = meta_ref[1]
        fill_pools(meta_ref, *around, far_refs, k_pool, v_pool, slots)
        masks = causal_masks()
        grad_ref[...] = jnp.zeros_like(grad_ref)
        far_sum[...] = jnp.zeros_like(far_sum)
        for t in range(pairs):
            here = slice(t * PAIR, (t + 1) * PAIR)
            window = slice(t * PAIR + BLK, t * PAIR + BLK + SPAN * BLK)
            others = max(whole - (t * PAIR + BLK), 0)
            end = SPAN * BLK
            mine = slice(t * PAIR + BLK + others - whole, t * PAIR + BLK + end - whole)
            keys = jnp.concatenate([k_pool[window, :], k_pool[2 * whole :, :]], axis=0)
            vals = jnp.concatenate([v_pool[window, :], v_pool[2 * whole :, :]], axis=0)
            query, grad = qd_ref[0, here, :], qd_ref[1, here, :]
            s = masked_scores(keys, query, bias_rows(bias_ref, t, range(SPAN + slots)), masks)
            probs = jnp.exp2(s - stats_ref[t, 2 * head : 2 * head + 1, :])
            delta = stats_ref[t, 2 * head + 1 : 2 * head + 2, :]
            ds = (probs * (dot(vals, grad, NT) - delta)).astype(jnp.bfloat16)
            low = probs.astype(jnp.bfloat16)
            dq_ref[here, :] = (dot(ds, keys, TN) * SCALE).astype(jnp.bfloat16)
            grad_ref[0, mine, :] += dot(ds[others:end], query, NN)
            grad_ref[1, mine, :] += dot(low[others:end], grad, NN)
            far_sum[0] += dot(ds[end:], query, NN)
            far_sum[1] += dot(low[end:], grad, NN)
        if carry:
            for k in range(group):
                piece = pl.ds(pl.multiple_of((meta_ref[0] ^ k) * rows, rows), rows)
                dq_outs[k][whole:, :] = dq_ref[piece, :]
                dq_outs[k][:whole, :] = carry_refs[0][...]
        else:
            dq_outs[0][...] = dq_ref[...]
        for index, ref in enumerate(far_outs):
            slot = jnp.maximum(at_group - index - 2, 0) // 2
            start = pl.multiple_of(slot * BLK, BLK)
            ref[...] = before_refs[index][...]
            lanes = slice(head * HD, (head + 1) * HD)
            ref[0, :, lanes] = (far_sum[0, pl.ds(start, BLK), :] * SCALE).astype(jnp.bfloat16)
            ref[1, :, lanes] = far_sum[1, pl.ds(start, BLK), :].astype(jnp.bfloat16)

    span = (SPAN + slots) * BLK
    outs = call(
        body, (meta,), (bias, stats, qd, own, prev, *far, *before, *carry),
        [shape((2, whole, HD), jnp.float32)]
        + [shape((2, BLK, width))] * len(far)
        + [shape((whole + rows if carry else whole, HD))] * cut,
        [
            pltpu.VMEM((everything, HD), jnp.bfloat16),
            pltpu.VMEM((everything, HD), jnp.bfloat16),
            pltpu.VMEM((2, slots * BLK, HD), jnp.float32),
            pltpu.VMEM((whole, HD), jnp.bfloat16),
        ],
        cost(8 * whole * span * HD * 2, 4 * 1024 * 1024, whole * span),
        f"attention_back_{head}", 24,
    )
    return outs[0], outs[1 : 1 + len(far)], outs[1 + len(far) :]


def backward_next(grads, qd, own, bias, stats, meta):
    whole, width = qd.shape[1:]
    heads = width // HD
    pairs = whole // PAIR

    def body(meta_ref, bias_ref, stats_ref, *refs):
        (grad_refs, (qd_ref, own_ref, out)), refs = split_refs(refs, (heads, 3))
        strided = pl.ds(pl.multiple_of(meta_ref[2] * BLK, BLK), BLK)
        for h in range(heads):
            lanes = slice(h * HD, (h + 1) * HD)
            out[0, :, lanes] = grad_refs[h][0]
            out[1, :, lanes] = grad_refs[h][1]
            for t in range(pairs):
                here = slice(t * PAIR, (t + 1) * PAIR)
                window = slice(t * PAIR + BLK, whole)
                near = (whole - BLK) // BLK - t * (PAIR // BLK)
                keys = jnp.concatenate([own_ref[0, window, lanes], own_ref[0, strided, lanes]], axis=0)
                vals = jnp.concatenate([own_ref[1, window, lanes], own_ref[1, strided, lanes]], axis=0)
                query, grad = qd_ref[0, here, lanes], qd_ref[1, here, lanes]
                rows_here = bias_rows(bias_ref, t, list(range(near)) + [SPAN])
                s = masked_scores(keys, query, rows_here, None)
                probs = jnp.exp2(s - stats_ref[t, 2 * h : 2 * h + 1, :])
                delta = stats_ref[t, 2 * h + 1 : 2 * h + 2, :]
                ds = (probs * (dot(vals, grad, NT) - delta)).astype(jnp.bfloat16)
                dk = dot(ds, query, NN)
                dv = dot(probs.astype(jnp.bfloat16), grad, NN)
                out[0, window, lanes] += dk[: near * BLK]
                out[1, window, lanes] += dv[: near * BLK]
                out[0, strided, lanes] += dk[near * BLK :]
                out[1, strided, lanes] += dv[near * BLK :]
        out[0] = out[0] * SCALE

    return call(
        body, (meta,), (bias, stats, *grads, qd, own),
        [shape((2, whole, width), jnp.float32)], [],
        cost(8 * whole * 5 * BLK * width, 7 * 1024 * 1024, whole * 5 * BLK * heads),
        "attention_back_next", 24,
    )[0]


def combine(dq, own, far, meta, group, rows):
    whole, width = own.shape[1:]
    heads = width // HD

    def body(meta_ref, dq_ref, own_ref, *refs):
        (far_refs, outs, (acc,)), refs = split_refs(refs, (len(far), group, 1))
        me, offset = meta_ref[0], meta_ref[2]
        acc[...] = own_ref[...]
        at = pl.multiple_of(offset * BLK, BLK)
        for ref in far_refs:
            acc[:, pl.ds(at, BLK), :] += ref[...].astype(jnp.float32)
        for k in range(group):
            here = pl.ds(pl.multiple_of((me ^ k) * rows, rows), rows)
            outs[k][0] = dq_ref[here, :]
            for which in range(2):
                for h in range(heads):
                    lanes = slice(h * HD, (h + 1) * HD)
                    outs[k][1 + which * heads + h] = acc[which, here, lanes].astype(jnp.bfloat16)

    return call(
        body, (meta,), (dq, own, *far), [shape((1 + 2 * heads, rows, HD))] * group,
        [pltpu.VMEM((2, whole, width), jnp.float32)],
        cost(0, 4 * 1024 * 1024), "combine",
    )


def project(head, mine, theirs, attn, before, meta, group, parts):
    height, whole = mine.shape
    each = 2 * height // parts
    full = group * HD
    more = parts // 2 - 1

    def body(meta_ref, mine_ref, theirs_ref, *refs):
        (attn_refs, before_refs, outs), refs = split_refs(refs, (group, len(before), 6))
        keep, first, odds, evens, pool, total = outs
        for ref in before_refs:
            first[:head] = ref[...]
        me, at_group, core = meta_ref[0], meta_ref[1], meta_ref[3]
        for k in range(group):
            at = pl.multiple_of((me ^ k) * HD, HD)
            pool[:, pl.ds(at, HD)] = attn_refs[k][:whole, :]
        upper = pl.ds(pl.multiple_of(core * height, height), height)
        lower = pl.ds(pl.multiple_of((1 - core) * height, height), height)
        total[upper, :] = dot(mine_ref[...], pool[...], NN)
        total[lower, :] = dot(theirs_ref[...], pool[...], NN)
        for m in range(parts):
            part = total[pl.ds(pl.multiple_of((at_group ^ m) * each, each), each), :]
            if m == 0:
                keep[...] = part
            elif m == 1:
                first[head] = part.astype(jnp.bfloat16)
            elif m % 2 == 1:
                odds[m // 2 - 1] = part.astype(jnp.bfloat16)
            else:
                evens[m // 2 - 1] = part

    return call(
        body, (meta,), (mine, theirs, *attn, *before),
        [
            shape((each, full), jnp.float32),
            shape((head + 1, each, full)),
            shape((more, each, full)),
            shape((more, each, full), jnp.float32),
        ],
        [pltpu.VMEM((whole, full), jnp.bfloat16), pltpu.VMEM((2 * height, full), jnp.float32)],
        cost(4 * height * whole * full, 6 * 1024 * 1024), f"project_{head}",
    )


def halve(head, evens, arrived):
    count, each, full = evens.shape
    more = (count - 1) // 2

    def body(evens_ref, arrived_ref, first, *rest):
        for m in range(1, count + 1):
            summed = evens_ref[m - 1] + arrived_ref[m - 1].astype(jnp.float32)
            if m == 1:
                first[...] = summed.astype(jnp.bfloat16)
            elif m % 2 == 1:
                rest[0][m // 2 - 1] = summed.astype(jnp.bfloat16)
            else:
                rest[1][m // 2 - 1] = summed

    others = [shape((more, each, full)), shape((more, each, full), jnp.float32)]
    return call(
        body, (), (evens, arrived), [shape((each, full))] + (others if more else []), [],
        cost(0, 3 * 1024 * 1024), f"halve_{head}",
    )


def finish(keep, neighbour, arrived, group):
    heads = len(keep)
    count = len(arrived[0])
    each = keep[0].shape[0]

    def body(*refs):
        (keep_refs, arrived_refs, (first, out)), refs = split_refs(refs, (heads, heads * count, 2))
        for h in range(heads):
            total = keep_refs[h][...] + first[h].astype(jnp.float32)
            for ref in arrived_refs[h * count : (h + 1) * count]:
                total = total + ref[...].astype(jnp.float32)
            for j in range(group):
                at = (j * heads + h) * HD
                out[:, at : at + HD] = total[:, j * HD : (j + 1) * HD]

    flat = [piece for pieces in arrived for piece in pieces]
    return call(
        body, (), (*keep, *flat, neighbour),
        [shape((each, group * heads * HD), jnp.float32)], [],
        cost(0, 3 * 1024 * 1024), "finish",
    )[0]


def unpack(early, pieces, meta, group):
    count, rows, _ = pieces[0].shape
    heads = (count - 1) // 2
    whole = early[0].shape[0] - rows

    def body(meta_ref, *refs):
        (early_refs, piece_refs, outs, (sems,)), refs = split_refs(refs, (group, group, 3, 1))
        me = meta_ref[0]
        copies = []
        for k in range(group):
            sources = [early_refs[k].at[pl.ds(whole, rows), :]]
            sources += [piece_refs[k].at[which] for which in range(count)]
            for which, source in enumerate(sources):
                at = (me ^ k) * heads * HD + (which % heads) * HD
                target = outs[which // heads].at[:, pl.ds(pl.multiple_of(at, HD), HD)]
                copies.append(pltpu.make_async_copy(source, target, sems.at[k, which]))
        copied(*copies)

    return pl.pallas_call(
        body,
        out_shape=[shape((rows, group * heads * HD))] * 3,
        in_specs=[SMEM] + [ANY] * (2 * group),
        out_specs=[ANY] * 3,
        scratch_shapes=[pltpu.SemaphoreType.DMA((group, count + 1))],
        compiler_params=params(16),
        cost_estimate=cost(0, 3 * MIB),
        name="unpack",
    )(meta, *early, *pieces)


def after(value, *others):
    return lax.optimization_barrier((value, *others))[0]


def local(devices, queries, keys, values, out_grad, proj_weight, layout):
    rows, columns = queries.shape
    group = LOCAL * BLK // rows
    parts = devices // group
    width = columns // group
    heads = width // HD
    blocks = layout.shape[0]
    slots = blocks // STRIDE
    position = lax.axis_index("seq")
    me, at_group = position % group, position // group
    core = lax.axis_index("head")
    offset = layout[blocks - 1, 0] % STRIDE
    place = jnp.stack([me, at_group, core]).astype(jnp.int32)
    meta = jnp.stack([me, at_group, offset, core]).astype(jnp.int32)

    def swap(piece, k):
        route = [(i, (i // group) * group + ((i % group) ^ k)) for i in range(devices)]
        return lax.ppermute(piece, "seq", route)

    def shifted(piece, distance):
        route = [
            (i, i + distance * group)
            for i in range(devices)
            if 0 <= i + distance * group < devices
        ]
        return lax.ppermute(piece, "seq", route)

    def swap_groups(piece, bit):
        route = [(i, ((i // group) ^ bit) * group + i % group) for i in range(devices)]
        return lax.ppermute(piece, "seq", route)

    def summary_route(distance, back):
        route = [
            (i, i + distance * group)
            for i in range(devices - distance * group)
            if (i // group) % 2 == 0
        ]
        return [(b, a) for a, b in route] if back else route

    def exchange(pieces):
        return [pieces[0]] + [swap(pieces[k], k) for k in range(1, group)]

    def add_up(head, odds, evens, before, token):
        arrivals, bit = [], 2
        odds = after(odds, *jax.tree.leaves(before))
        while True:
            first, *more = halve(head, evens, odds)
            token = after(token, first)
            done = first
            arrivals.append(swap_groups(first, bit))
            if not more:
                return arrivals, token, done
            odds, evens = swap_groups(more[0], bit), more[1]
            bit *= 2

    kv = pack_kv(keys, values, place, group, width)
    own_kv = exchange(kv)
    early = after(place, own_kv[1])
    qd_cut = grads_packed(queries, out_grad, proj_weight, early, group, parts)
    pool, strided = assemble_kv(own_kv, after(meta, qd_cut[0]), group)
    prev = shifted(pool, 1)
    qd_pieces = exchange(qd_cut)
    later = after(strided, qd_pieces[1])
    far = [
        lax.ppermute(
            strided if distance == 2 else later, "seq", summary_route(distance, False)
        )
        for distance in range(2, parts)
    ]
    bias, bias_next = masks_of(layout, after(meta, strided), parts, slots)
    qd, mine = assemble(qd_pieces, after(meta, bias, prev, *far), group)
    theirs = lax.ppermute(mine, "head", [(0, 1), (1, 0)])
    next_qd = shifted(qd, -1)

    stats = jnp.zeros((LOCAL // 2, 2 * heads, PAIR), jnp.float32)
    order = meta
    attn = []
    for h in range(heads):
        got, stats = forward(h, qd, pool, prev, far, bias, stats, order, group, slots)
        attn.append(got)
        if h == 0:
            attn[0] = [got] + [swap(got, k) for k in range(1, group)]
        order = after(meta, got, theirs)

    assert heads == 2
    grads, keep, finals = [], [], []
    far_grads = [jnp.zeros((2, BLK, width), jnp.bfloat16) for _ in far]
    order, first = after(meta, stats, theirs), []
    for h in range(heads):
        carry = attn[1:] if h == 0 else []
        got = backward(
            h, qd, pool, prev, far, far_grads, carry, bias, stats, order, group, slots
        )
        grads.append(got[0])
        far_grads = got[1]
        if h == 0:
            attn[1] = early_dq = exchange(got[2])
        else:
            dq = got[2][0]
        order = after(meta, got[0])
        kept, first, odds, evens = project(h, mine, theirs, attn[h], first, order, group, parts)
        keep.append(kept)
        first, odds = [first], swap_groups(odds, 1)
        order = after(meta, *first)
        if h == 0:
            next_stats = shifted(after(stats, next_qd, *first), -1)
        if h < heads - 1:
            sums, order, _ = add_up(h, odds, evens, (first, next_stats), order)
            finals.append(sums)
    far_back = [
        lax.ppermute(piece, "seq", summary_route(index + 2, True))
        for index, piece in enumerate(far_grads)
    ]
    own_grad = backward_next(grads, next_qd, pool, bias_next, next_stats, order)
    final_cut = combine(dq, own_grad, far_back, after(meta, finals[0]), group, rows)
    final = exchange(final_cut)
    sums, _, _ = add_up(heads - 1, odds, evens, final_cut, meta)
    finals.append(sums)
    neighbour = swap_groups(after(first[0], final_cut[0]), 1)
    proj_grad = finish(keep, neighbour, finals, group)
    query_grad, key_grad, value_grad = unpack(early_dq, final, meta, group)
    return (query_grad, key_grad, value_grad, proj_grad)


def solution(mesh):
    split = P(("dp", "seq"), "head")
    return jax.shard_map(
        functools.partial(local, mesh.shape["seq"]),
        mesh=mesh,
        in_specs=(split, split, split, P(("dp", "seq"), None), P(None, "head"), P()),
        out_specs=(split, split, split, split),
        check_vma=False,
    )
```
